32 devices in a mesh: section: 4 (over y, x), row: 4 (over z), col: 2 (over core).
Axes of the slice: x: 2, y: 2, z: 4, core: 2. Of those that a mesh axis runs over, the one named last changes fastest.
Arguments:
- inputs: bfloat16 [4, 3, 128, 2048], P('section', None, 'row', 'col'), may hold values from -6 to 6
- sample_ids: int32 [6], replicated, may hold values from 0 to 15
- send_base: bfloat16 [4, 16, 128, 2048], P('section', None, 'row', 'col'), may hold values from -1.796875 to 1.796875
- recv_base: bfloat16 [4, 16, 128, 2048], P('section', None, 'row', 'col'), may hold values from -1.796875 to 1.796875
- w_up: bfloat16 [4, 2048, 8192], P('section', 'col', 'row'), may hold values from -0.125 to 0.125
- w_down: bfloat16 [4, 8192, 2048], P('section', 'row', 'col'), may hold values from -0.0625 to 0.0625
- cotangent: bfloat16 [4, 3, 128, 2048], P('section', None, 'row', 'col'), may hold values from -6 to 6
Outputs:
- section_input: bfloat16 [4, 3, 128, 2048], P('section', None, 'row', 'col')
- section_output: bfloat16 [4, 3, 128, 2048], P('section', None, 'row', 'col')
- input_grad: bfloat16 [4, 3, 128, 2048], P('section', None, 'row', 'col')
- grad_up: bfloat16 [4, 2048, 8192], P('section', 'col', 'row')
- grad_down: bfloat16 [4, 8192, 2048], P('section', 'row', 'col')
The draws below stay inside these ranges and needn't reach their ends.
All inputs are finite; a program needn't handle non-finite values.
Results may differ from the reference program's by a relative error of at most 0.04.
Values may be sent and summed in bfloat16 or wider, within the bound.
No kernel may reach another device: no remote copies, remote signals or barrier semaphores. Data moves between devices by JAX's collectives and lax.ppermute only.
A program may use at most 64 MiB of HBM per device.

```python
import jax
import jax.numpy as jnp
from jax import lax

D = 2048
FF = 8192
MTOK = 128
TICKS = 3
SAMPLES = 16
N_SECTION = 4
N_ROW = 4
N_COL = 2


def set_ends(entries, rng, smallest, high):
    place = [jax.random.randint(jax.random.fold_in(rng, axis), (), 0, length) for axis, length in enumerate(entries.shape)]
    main_axis = entries.shape.index(max(entries.shape))
    beside = place[:main_axis] + [(place[main_axis] + 1) % entries.shape[main_axis]] + place[main_axis + 1:]
    return entries.at[tuple(place)].set(smallest).at[tuple(beside)].set(high)


def steps_of(own_key, shape, cuts, low, high):
    level = 1.0
    for dim, shards_of in cuts:
        draws = jax.random.uniform(jax.random.fold_in(jax.random.fold_in(own_key, 6), dim), (shards_of,), jnp.float32, low / len(cuts), high / len(cuts))
        level = level * jnp.repeat(jnp.exp(draws), shape[dim] // shards_of).reshape((-1,) + (1,) * (len(shape) - 1 - dim))
    return level


def noise(stream_key, dims, scale, limit, pieces=(), kind=jnp.bfloat16):
    array = scale * jax.random.normal(stream_key, dims, jnp.float32)
    if pieces:
        array = array * steps_of(stream_key, dims, pieces, -0.22, 0.18)
    return jnp.clip(array, -limit, limit).astype(kind)


def setup_inputs(seed: int = 0) -> dict:
    splits = jax.random.split(jax.random.key(seed), 8)
    return {
        "inputs": noise(splits[0], (N_SECTION, TICKS, MTOK, D), 1.0, 6.0, ((0, 4), (2, 4), (3, 2))),
        "sample_ids": set_ends(jax.random.randint(splits[1], (N_SECTION + TICKS - 1,), 0, SAMPLES), jax.random.fold_in(splits[1], 1), 0, SAMPLES - 1).astype(jnp.int32),
        "send_base": noise(splits[2], (N_SECTION, SAMPLES, MTOK, D), 0.3, 1.796875, ((0, 4), (2, 4), (3, 2))),
        "recv_base": noise(splits[3], (N_SECTION, SAMPLES, MTOK, D), 0.3, 1.796875, ((0, 4), (2, 4), (3, 2))),
        "w_up": noise(splits[4], (N_SECTION, D, FF), D ** -0.5, 0.125, ((0, 4), (1, 2), (2, 4))),
        "w_down": noise(splits[5], (N_SECTION, FF, D), FF ** -0.5, 0.0625, ((0, 4), (1, 4), (2, 2))),
        "cotangent": noise(splits[6], (N_SECTION, TICKS, MTOK, D), 1.0, 6.0, ((0, 4), (2, 4), (3, 2))),
    }


def split_sum(left, right, parts):
    size = left.shape[1] // parts
    total = jnp.zeros((left.shape[0], right.shape[1]), jnp.float32)
    for index in range(parts):
        block = jnp.dot(left[:, index * size:(index + 1) * size], right[index * size:(index + 1) * size], preferred_element_type=jnp.float32)
        total = total + lax.optimization_barrier(block.astype(jnp.bfloat16)).astype(jnp.float32)
    return total


def silu_slope(value):
    sig = jax.nn.sigmoid(value)
    return sig * (1.0 + value * (1.0 - sig))


def reference(inputs, sample_ids, send_base, recv_base, w_up, w_down, cotangent):
    entering = [[None] * TICKS for index in range(N_SECTION)]
    leaving = [[None] * TICKS for index in range(N_SECTION)]
    deltas = [[None] * TICKS for index in range(N_SECTION)]
    hidden_pre = [[None] * TICKS for index in range(N_SECTION)]
    hidden_act = [[None] * TICKS for index in range(N_SECTION)]
    for tick in range(TICKS):
        for section in range(N_SECTION):
            sample = sample_ids[tick - section + N_SECTION - 1]
            if tick == 0 or section == 0:
                current = inputs[section, tick]
            else:
                stored = lax.dynamic_index_in_dim(recv_base[section], sample, 0, keepdims=False)
                current = (stored.astype(jnp.float32) + deltas[section - 1][tick - 1].astype(jnp.float32)).astype(jnp.bfloat16)
            entering[section][tick] = current
            pre = split_sum(current, w_up[section], N_COL)
            act = jax.nn.silu(pre).astype(jnp.bfloat16)
            output = (current.astype(jnp.float32) + split_sum(act, w_down[section], N_ROW)).astype(jnp.bfloat16)
            hidden_pre[section][tick] = pre
            hidden_act[section][tick] = act
            leaving[section][tick] = output
            sent = lax.dynamic_index_in_dim(send_base[section], sample, 0, keepdims=False)
            deltas[section][tick] = (output.astype(jnp.float32) - sent.astype(jnp.float32)).astype(jnp.bfloat16)
    back = [[None] * TICKS for index in range(N_SECTION)]
    total_up = [jnp.zeros((D, FF), jnp.float32) for index in range(N_SECTION)]
    total_down = [jnp.zeros((FF, D), jnp.float32) for index in range(N_SECTION)]
    for turn in range(TICKS):
        tick = TICKS - 1 - turn
        for section in range(N_SECTION - 1, -1, -1):
            if turn == 0 or section == N_SECTION - 1:
                grad_out = cotangent[section, tick]
            else:
                grad_out = back[section + 1][tick + 1]
            grad_act = split_sum(grad_out, w_down[section].T, N_COL)
            grad_pre = (grad_act * silu_slope(hidden_pre[section][tick])).astype(jnp.bfloat16)
            grad_in = (grad_out.astype(jnp.float32) + split_sum(grad_pre, w_up[section].T, N_ROW)).astype(jnp.bfloat16)
            back[section][tick] = grad_in
            total_up[section] = total_up[section] + jnp.dot(entering[section][tick].T, grad_pre, preferred_element_type=jnp.float32)
            total_down[section] = total_down[section] + jnp.dot(hidden_act[section][tick].T, grad_out, preferred_element_type=jnp.float32)
    section_input = jnp.stack([jnp.stack(entering[index]) for index in range(N_SECTION)])
    section_output = jnp.stack([jnp.stack(leaving[index]) for index in range(N_SECTION)])
    input_grad = jnp.stack([jnp.stack(back[index]) for index in range(N_SECTION)])
    grads_up = jnp.stack([value.astype(jnp.bfloat16) for value in total_up])
    grads_down = jnp.stack([value.astype(jnp.bfloat16) for value in total_down])
    return (section_input, section_output, input_grad, grads_up, grads_down)
```

```python
import jax
import jax.numpy as jnp
from jax import lax
from jax.sharding import PartitionSpec as P

BF = jnp.bfloat16
F32 = jnp.float32
LAST = (((1,), (1,)), ((), ()))
FIRST = (((0,), (0,)), ((), ()))


def from_behind(block, axis, distance):
    devices = range(lax.axis_size(axis))
    route = [(i - distance, i) for i in devices if i - distance in devices]
    return lax.ppermute(block, axis, route)


def turn(block, axis, distance):
    size = lax.axis_size(axis)
    return lax.ppermute(block, axis, [(i, (i + distance) % size) for i in range(size)])


def gather_rows(block):
    size = lax.axis_size("row")
    return jnp.concatenate([block] + [turn(block, "row", -j) for j in range(1, size)], axis=0)


def scatter_rows(partial):
    size = lax.axis_size("row")
    pieces = jnp.split(partial, size, axis=0)
    total = pieces[0].astype(F32)
    for j in range(1, size):
        total = total + turn(pieces[j], "row", j).astype(F32)
    return total


def sum_cols(partial):
    size = lax.axis_size("col")
    if size > 2:
        return lax.psum(partial, "col").astype(F32)
    total = partial.astype(F32)
    for j in range(1, size):
        total = total + turn(partial, "col", j).astype(F32)
    return total


def silu_slope(value):
    sig = jax.nn.sigmoid(value)
    return sig * (1.0 + value * (1.0 - sig))


def pick(table, index):
    return lax.dynamic_index_in_dim(table, index, 0, keepdims=False)


def matmul(a, b, dims=(((1,), (0,)), ((), ()))):
    return lax.dot_general(a, b, dims, preferred_element_type=F32)


def per_device(inputs, sample_ids, send_base, recv_base, w_up, w_down, cotangent):
    section = lax.axis_index("section")
    sections = lax.axis_size("section")
    ticks = inputs.shape[1]
    up_block = w_up[0]
    down_block = w_down[0]
    full_ins, pres, acts, seen_in, seen_out = [], [], [], [], []
    sending = None
    for tick in range(ticks):
        sample = pick(sample_ids, tick - section + sections - 1)
        if tick == 0:
            act_in = inputs[0, tick]
        else:
            arrived = from_behind(sending, "section", 1)
            rebuilt = (pick(recv_base[0], sample).astype(F32) + arrived.astype(F32)).astype(BF)
            act_in = jnp.where(section == 0, inputs[0, tick], rebuilt)
        full_in = gather_rows(act_in)
        pre = sum_cols(matmul(full_in, up_block).astype(BF))
        act = jax.nn.silu(pre).astype(BF)
        mixed = scatter_rows(matmul(act, down_block).astype(BF))
        act_out = (act_in.astype(F32) + mixed).astype(BF)
        stored = pick(send_base[0], sample)
        sending = (act_out.astype(F32) - stored.astype(F32)).astype(BF)
        full_ins.append(full_in)
        pres.append(pre)
        acts.append(act)
        seen_in.append(act_in)
        seen_out.append(act_out)
    full_grads = [None] * ticks
    pre_grads = [None] * ticks
    seen_grad = [None] * ticks
    for step in range(ticks):
        tick = ticks - 1 - step
        if step == 0:
            grad_out = cotangent[0, tick]
        else:
            arrived = from_behind(sending, "section", -1)
            grad_out = jnp.where(section == sections - 1, cotangent[0, tick], arrived)
        full_grad = gather_rows(grad_out)
        grad_act = sum_cols(matmul(full_grad, down_block, LAST).astype(BF))
        grad_pre = (grad_act * silu_slope(pres[tick])).astype(BF)
        returned = scatter_rows(matmul(grad_pre, up_block, LAST).astype(BF))
        sending = (grad_out.astype(F32) + returned).astype(BF)
        full_grads[tick] = full_grad
        pre_grads[tick] = grad_pre
        seen_grad[tick] = sending
    grad_up = matmul(jnp.concatenate(full_ins, axis=0), jnp.concatenate(pre_grads, axis=0), FIRST)
    grad_down = matmul(jnp.concatenate(acts, axis=0), jnp.concatenate(full_grads, axis=0), FIRST)
    return (
        jnp.stack(seen_in)[None],
        jnp.stack(seen_out)[None],
        jnp.stack(seen_grad)[None],
        grad_up.astype(BF)[None],
        grad_down.astype(BF)[None],
    )


def solution(mesh):
    placed = (
        P("section", None, "row", "col"),
        P(),
        P("section", None, "row", "col"),
        P("section", None, "row", "col"),
        P("section", "col", "row"),
        P("section", "row", "col"),
        P("section", None, "row", "col"),
    )
    return jax.shard_map(
        per_device,
        mesh=mesh,
        in_specs=placed,
        out_specs=(
            P("section", None, "row", "col"),
            P("section", None, "row", "col"),
            P("section", None, "row", "col"),
            P("section", "col", "row"),
            P("section", "row", "col"),
        ),
        check_vma=False,
    )
```

```python
import jax
import jax.numpy as jnp
from jax import lax
from jax.sharding import PartitionSpec as P

BF = jnp.bfloat16
F32 = jnp.float32
LAST = (((1,), (1,)), ((), ()))
FIRST = (((0,), (0,)), ((), ()))


def from_behind(block, axis, distance):
    devices = range(lax.axis_size(axis))
    route = [(i - distance, i) for i in devices if i - distance in devices]
    return lax.ppermute(block, axis, route)


def turn(block, axis, distance):
    size = lax.axis_size(axis)
    return lax.ppermute(block, axis, [(i, (i + distance) % size) for i in range(size)])


def gather_rows(block):
    size = lax.axis_size("row")
    copies = jnp.broadcast_to(block[None], (size,) + block.shape)
    full = lax.all_to_all(copies, "row", 0, 0)
    return full.reshape((size * block.shape[0],) + block.shape[1:])


def scatter_rows(partial):
    size = lax.axis_size("row")
    pieces = partial.reshape((size, partial.shape[0] // size) + partial.shape[1:])
    return lax.all_to_all(pieces, "row", 0, 0).astype(F32).sum(axis=0)


def sum_cols(partial):
    size = lax.axis_size("col")
    if size > 2:
        return lax.psum(partial, "col").astype(F32)
    total = partial.astype(F32)
    for j in range(1, size):
        total = total + turn(partial, "col", j).astype(F32)
    return total


def silu_slope(value):
    sig = jax.nn.sigmoid(value)
    return sig * (1.0 + value * (1.0 - sig))


def pick(table, index):
    return lax.dynamic_index_in_dim(table, index, 0, keepdims=False)


def matmul(a, b, dims=(((1,), (0,)), ((), ()))):
    return lax.dot_general(a, b, dims, preferred_element_type=F32)


def per_device(inputs, sample_ids, send_base, recv_base, w_up, w_down, cotangent):
    section = lax.axis_index("section")
    sections = lax.axis_size("section")
    ticks = inputs.shape[1]
    up_block = w_up[0]
    down_block = w_down[0]
    full_ins, pres, acts, seen_in, seen_out = [], [], [], [], []
    sending = None
    for tick in range(ticks):
        sample = pick(sample_ids, tick - section + sections - 1)
        if tick == 0:
            act_in = inputs[0, tick]
        else:
            arrived = from_behind(sending, "section", 1)
            rebuilt = (pick(recv_base[0], sample).astype(F32) + arrived.astype(F32)).astype(BF)
            act_in = jnp.where(section == 0, inputs[0, tick], rebuilt)
        full_in = gather_rows(act_in)
        pre = sum_cols(matmul(full_in, up_block).astype(BF))
        act = jax.nn.silu(pre).astype(BF)
        mixed = scatter_rows(matmul(act, down_block).astype(BF))
        act_out = (act_in.astype(F32) + mixed).astype(BF)
        stored = pick(send_base[0], sample)
        sending = (act_out.astype(F32) - stored.astype(F32)).astype(BF)
        full_ins.append(full_in)
        pres.append(pre)
        acts.append(act)
        seen_in.append(act_in)
        seen_out.append(act_out)
    full_grads = [None] * ticks
    pre_grads = [None] * ticks
    seen_grad = [None] * ticks
    for step in range(ticks):
        tick = ticks - 1 - step
        if step == 0:
            grad_out = cotangent[0, tick]
        else:
            arrived = from_behind(sending, "section", -1)
            grad_out = jnp.where(section == sections - 1, cotangent[0, tick], arrived)
        full_grad = gather_rows(grad_out)
        grad_act = sum_cols(matmul(full_grad, down_block, LAST).astype(BF))
        grad_pre = (grad_act * silu_slope(pres[tick])).astype(BF)
        returned = scatter_rows(matmul(grad_pre, up_block, LAST).astype(BF))
        sending = (grad_out.astype(F32) + returned).astype(BF)
        full_grads[tick] = full_grad
        pre_grads[tick] = grad_pre
        seen_grad[tick] = sending
    grad_up = matmul(jnp.concatenate(full_ins, axis=0), jnp.concatenate(pre_grads, axis=0), FIRST)
    grad_down = matmul(jnp.concatenate(acts, axis=0), jnp.concatenate(full_grads, axis=0), FIRST)
    return (
        jnp.stack(seen_in)[None],
        jnp.stack(seen_out)[None],
        jnp.stack(seen_grad)[None],
        grad_up.astype(BF)[None],
        grad_down.astype(BF)[None],
    )


def solution(mesh):
    placed = (
        P("section", None, "row", "col"),
        P(),
        P("section", None, "row", "col"),
        P("section", None, "row", "col"),
        P("section", "col", "row"),
        P("section", "row", "col"),
        P("section", None, "row", "col"),
    )
    return jax.shard_map(
        per_device,
        mesh=mesh,
        in_specs=placed,
        out_specs=(
            P("section", None, "row", "col"),
            P("section", None, "row", "col"),
            P("section", None, "row", "col"),
            P("section", "col", "row"),
            P("section", "row", "col"),
        ),
        check_vma=False,
    )
```

```python
import jax
import jax.numpy as jnp
from jax import lax
from jax.sharding import PartitionSpec as P

BF = jnp.bfloat16
F32 = jnp.float32
LAST = (((1,), (1,)), ((), ()))
FIRST = (((0,), (0,)), ((), ()))


def partner(row, j, size):
    return row ^ j if size & (size - 1) == 0 else (j - row) % size


def turn(block, axis, distance):
    size = lax.axis_size(axis)
    return lax.ppermute(block, axis, [(i, (i + distance) % size) for i in range(size)])


def swap_rows(block, j):
    size = lax.axis_size("row")
    return lax.ppermute(block, "row", [(i, partner(i, j, size)) for i in range(size)])


def gather_rows(block):
    return [swap_rows(block, j) if j else block for j in range(lax.axis_size("row"))]


def spread(block, step):
    sections, size = lax.axis_size("section"), lax.axis_size("row")
    there = [s for s in range(sections) if 0 <= s + step < sections]
    return [
        lax.ppermute(
            block,
            ("section", "row"),
            [(s * size + i, (s + step) * size + partner(i, j, size)) for s in there for i in range(size)],
        )
        for j in range(size)
    ]


def gather_last(block):
    last, size = lax.axis_size("section") - 1, lax.axis_size("row")
    return [block] + [
        lax.ppermute(
            block,
            ("section", "row"),
            [(last * size + i, last * size + partner(i, j, size)) for i in range(size)],
        )
        for j in range(1, size)
    ]


def after(block, other):
    return lax.optimization_barrier((block, other))[0]


def scatter_rows(partial):
    size = lax.axis_size("row")
    pieces = jnp.split(partial, size, axis=0)
    total = pieces[0].astype(F32)
    for j in range(1, size):
        total = total + swap_rows(pieces[j], j).astype(F32)
    return total


def sum_cols(partial):
    size = lax.axis_size("col")
    if size > 2:
        return lax.psum(partial, "col").astype(F32)
    total = partial.astype(F32)
    for j in range(1, size):
        total = total + turn(partial, "col", j).astype(F32)
    return total


def silu_slope(value):
    sig = jax.nn.sigmoid(value)
    return sig * (1.0 + value * (1.0 - sig))


def pick(table, index):
    return lax.dynamic_index_in_dim(table, index, 0, keepdims=False)


def matmul(a, b, dims=(((1,), (0,)), ((), ()))):
    return lax.dot_general(a, b, dims, preferred_element_type=F32)


def per_device(inputs, sample_ids, send_base, recv_base, w_up, w_down, cotangent):
    section = lax.axis_index("section")
    sections = lax.axis_size("section")
    ticks = inputs.shape[1]
    up_block = w_up[0]
    down_block = w_down[0]
    full_ins, pres, acts, seen_out = [], [], [], []
    samples = [pick(sample_ids, tick - section + sections - 1) for tick in range(ticks)]
    bases = [
        jnp.where(section == 0, inputs[0, tick], pick(recv_base[0], samples[tick])) for tick in range(1, ticks)
    ]
    sending = None
    for tick in range(ticks):
        if tick == 0:
            pieces = gather_rows(inputs[0, tick])
        else:
            pieces = [
                (base[tick - 1].astype(F32) + arrived.astype(F32)).astype(BF)
                for base, arrived in zip(full_bases, spread(sending, 1))
            ]
        full_in = jnp.concatenate(pieces, axis=0)
        partial = matmul(full_in, up_block).astype(BF)
        if tick == 0:
            full_bases = gather_rows(after(jnp.stack(bases), partial))
        elif tick == 1:
            first_cots = gather_rows(after(cotangent[0, ticks - 1], partial))
        else:
            last_cots = gather_last(after(cotangent[0, : ticks - 1], partial))
        pre = sum_cols(partial)
        act = jax.nn.silu(pre).astype(BF)
        mixed = scatter_rows(matmul(act, down_block).astype(BF))
        act_out = (pieces[0].astype(F32) + mixed).astype(BF)
        stored = pick(send_base[0], samples[tick])
        sending = (act_out.astype(F32) - stored.astype(F32)).astype(BF)
        if tick == 0:
            sending = after(sending, full_bases)
        elif tick == 1:
            first_grads = matmul(jnp.concatenate(first_cots, axis=0), down_block, LAST).astype(BF)
            sending = after(sending, first_grads)
        full_ins.append(full_in)
        pres.append(pre)
        acts.append(act)
        seen_out.append(act_out)
    full_grads = [None] * ticks
    pre_grads = [None] * ticks
    seen_grad = [None] * ticks
    for step in range(ticks):
        tick = ticks - 1 - step
        if step == 0:
            pieces = first_cots
        else:
            pieces = [
                jnp.where(section == sections - 1, own[tick], arrived)
                for own, arrived in zip(last_cots, spread(sending, -1))
            ]
        full_grad = jnp.concatenate(pieces, axis=0)
        partial = matmul(full_grad, down_block, LAST).astype(BF) if step else first_grads
        grad_act = sum_cols(partial)
        grad_pre = (grad_act * silu_slope(pres[tick])).astype(BF)
        returned = scatter_rows(matmul(grad_pre, up_block, LAST).astype(BF))
        sending = (pieces[0].astype(F32) + returned).astype(BF)
        if step == 0:
            sending = after(sending, last_cots)
        full_grads[tick] = full_grad
        pre_grads[tick] = grad_pre
        seen_grad[tick] = sending
    piece_rows = inputs.shape[2]
    seen_in = [full[:piece_rows] for full in full_ins]
    grad_up = matmul(jnp.concatenate(full_ins, axis=0), jnp.concatenate(pre_grads, axis=0), FIRST)
    grad_down = matmul(jnp.concatenate(acts, axis=0), jnp.concatenate(full_grads, axis=0), FIRST)
    return (
        jnp.stack(seen_in)[None],
        jnp.stack(seen_out)[None],
        jnp.stack(seen_grad)[None],
        grad_up.astype(BF)[None],
        grad_down.astype(BF)[None],
    )


def solution(mesh):
    placed = (
        P("section", None, "row", "col"),
        P(),
        P("section", None, "row", "col"),
        P("section", None, "row", "col"),
        P("section", "col", "row"),
        P("section", "row", "col"),
        P("section", None, "row", "col"),
    )
    return jax.shard_map(
        per_device,
        mesh=mesh,
        in_specs=placed,
        out_specs=(
            P("section", None, "row", "col"),
            P("section", None, "row", "col"),
            P("section", None, "row", "col"),
            P("section", "col", "row"),
            P("section", "row", "col"),
        ),
        check_vma=False,
    )
```

```python
import jax
import jax.numpy as jnp
from jax import lax
from jax.sharding import PartitionSpec as P

BF = jnp.bfloat16
F32 = jnp.float32
LAST = (((1,), (1,)), ((), ()))
FIRST = (((0,), (0,)), ((), ()))


def turn(block, axis, distance):
    size = lax.axis_size(axis)
    return lax.ppermute(block, axis, [(i, (i + distance) % size) for i in range(size)])


def near(block):
    size = lax.axis_size("row")
    return lax.ppermute(block, "row", [(i, i ^ 1) for i in range(size)])


def far(block, j):
    size = lax.axis_size("row")
    return lax.ppermute(block, "row", [(i, i ^ (2 * j)) for i in range(size)])


def far_count():
    return lax.axis_size("row") // 2


def half_of(block):
    return jnp.stack([far(block, j) if j else block for j in range(far_count())])


def hand_over(half, step):
    sections, size, count = lax.axis_size("section"), lax.axis_size("row"), far_count()
    there = [s for s in range(sections) if 0 <= s + step < sections]
    arrived = []
    for j in range(count):
        route = [(s * size + i, (s + step) * size + (i ^ (2 * j))) for s in there for i in range(size)]
        block = lax.ppermute(half, ("section", "row"), route)
        arrived.append(block if j == 0 else jnp.stack([block[k ^ j] for k in range(count)]))
    return arrived


def whole(half):
    rows = half.shape[0] * half.shape[1]
    half = half.reshape(rows, half.shape[2])
    return jnp.concatenate([half, near(half)], axis=0)


def near_sum(partial):
    rows = partial.shape[0] // 2
    total = partial[:rows].astype(F32) + near(partial[rows:]).astype(F32)
    return total.reshape(far_count(), rows // far_count(), partial.shape[1])


def after(block, other):
    return lax.optimization_barrier((block, other))[0]


def sum_cols(partial):
    size = lax.axis_size("col")
    if size > 2:
        return lax.psum(partial, "col").astype(F32)
    total = partial.astype(F32)
    for j in range(1, size):
        total = total + turn(partial, "col", j).astype(F32)
    return total


def silu_slope(value):
    sig = jax.nn.sigmoid(value)
    return sig * (1.0 + value * (1.0 - sig))


def pick(table, index):
    return lax.dynamic_index_in_dim(table, index, 0, keepdims=False)


def matmul(a, b, dims=(((1,), (0,)), ((), ()))):
    return lax.dot_general(a, b, dims, preferred_element_type=F32)


def per_device(inputs, sample_ids, send_base, recv_base, w_up, w_down, cotangent):
    section = lax.axis_index("section")
    sections = lax.axis_size("section")
    ticks = inputs.shape[1]
    up_block = w_up[0]
    down_block = w_down[0]
    samples = [pick(sample_ids, tick - section + sections - 1) for tick in range(ticks)]
    stored = [pick(send_base[0], samples[tick]).astype(F32) for tick in range(ticks - 1)]
    bases = [jnp.where(section == 0, inputs[0, t], pick(recv_base[0], samples[t])) for t in range(1, ticks)]
    cots = [cotangent[0, tick] for tick in range(ticks)]
    half = half_of(inputs[0, 0])
    known = half_of(after(jnp.stack(bases + cots), half))
    base_halves = [None] + [known[:, tick] for tick in range(ticks - 1)]
    cot_halves = [known[:, ticks - 1 + tick] for tick in range(ticks)]
    full_ins, pres, acts, seen_in, outs, out_rest = [], [], [], [], [], []
    for tick in range(ticks):
        if tick:
            half = base_halves[tick].astype(F32)
            for block in hand_over(sending, 1):
                half = half + block.astype(F32)
            half = half.astype(BF)
        full_in = whole(half)
        partial = matmul(full_in, up_block).astype(BF)
        if tick == 1:
            full_cot = whole(after(cot_halves[-1], partial))
        pre = sum_cols(partial)
        act = jax.nn.silu(pre).astype(BF)
        mixed = near_sum(matmul(act, down_block).astype(BF))
        out = half[0].astype(F32) + mixed[0]
        if tick < ticks - 1:
            sending = jnp.concatenate([(out - stored[tick])[None], mixed[1:]]).astype(BF)
        if tick == 1:
            first_grads = matmul(full_cot, down_block, LAST).astype(BF)
            sending = after(sending, first_grads)
        full_ins.append(full_in)
        pres.append(pre)
        acts.append(act)
        seen_in.append(half[0])
        outs.append(out)
        out_rest.append(mixed[1:].astype(BF))
    full_grads = [None] * ticks
    pre_grads = [None] * ticks
    grads = [None] * ticks
    grad_rest = [None] * ticks
    for step in range(ticks):
        tick = ticks - 1 - step
        if step == 0:
            half, full_grad, partial = cot_halves[tick], full_cot, first_grads
        else:
            half = sum(block.astype(F32) for block in hand_over(sending, -1)).astype(BF)
            half = jnp.where(section == sections - 1, cot_halves[tick], half)
            full_grad = whole(half)
            partial = matmul(full_grad, down_block, LAST).astype(BF)
        grad_act = sum_cols(partial)
        grad_pre = (grad_act * silu_slope(pres[tick])).astype(BF)
        back = matmul(grad_pre, up_block, LAST).astype(BF)
        returned = near_sum(back)
        grad = half[0].astype(F32) + returned[0]
        sending = jnp.concatenate([grad[None], returned[1:]]).astype(BF)
        full_grads[tick] = full_grad
        pre_grads[tick] = grad_pre
        grads[tick] = grad
        grad_rest[tick] = sending[1:]
        if step == 1:
            early = far_sum(outs, after(jnp.stack(out_rest), partial))
        if step == 2:
            late = far_sum(grads[1:], after(jnp.stack(grad_rest[1:]), partial))
    last = far_sum(grads[:1], jnp.stack(grad_rest[:1]))
    flat = [jnp.concatenate(parts, axis=0) for parts in (full_ins, pre_grads, acts, full_grads)]
    flat_in, flat_pre, flat_act, flat_grad = lax.optimization_barrier((*flat, back))[:4]
    grad_up = matmul(flat_in, flat_pre, FIRST)
    grad_down = matmul(flat_act, flat_grad, FIRST)
    return (
        jnp.stack(seen_in)[None],
        early[None],
        jnp.concatenate([last, late])[None],
        grad_up.astype(BF)[None],
        grad_down.astype(BF)[None],
    )


def far_sum(owns, rests):
    total = jnp.stack(owns)
    for j in range(1, far_count()):
        total = total + far(rests[:, j - 1], j).astype(F32)
    return total.astype(BF)


def solution(mesh):
    placed = (
        P("section", None, "row", "col"),
        P(),
        P("section", None, "row", "col"),
        P("section", None, "row", "col"),
        P("section", "col", "row"),
        P("section", "row", "col"),
        P("section", None, "row", "col"),
    )
    return jax.shard_map(
        per_device,
        mesh=mesh,
        in_specs=placed,
        out_specs=(
            P("section", None, "row", "col"),
            P("section", None, "row", "col"),
            P("section", None, "row", "col"),
            P("section", "col", "row"),
            P("section", "row", "col"),
        ),
        check_vma=False,
    )
```

```python
import jax
import jax.numpy as jnp
from jax import lax
from jax.experimental import pallas as pl
from jax.experimental.pallas import tpu as pltpu
from jax.sharding import PartitionSpec as P

BF = jnp.bfloat16
F32 = jnp.float32
LAST = (((1,), (1,)), ((), ()))
FIRST = (((0,), (0,)), ((), ()))


def from_behind(block, axis, distance):
    devices = range(lax.axis_size(axis))
    route = [(i - distance, i) for i in devices if i - distance in devices]
    return lax.ppermute(block, axis, route)


def turn(block, axis, distance):
    size = lax.axis_size(axis)
    return lax.ppermute(block, axis, [(i, (i + distance) % size) for i in range(size)])


def partner(row, j, size):
    return row ^ j if size & (size - 1) == 0 else (j - row) % size


def swap_rows(block, j):
    size = lax.axis_size("row")
    return lax.ppermute(block, "row", [(i, partner(i, j, size)) for i in range(size)])


def gather_rows(block):
    return [swap_rows(block, j) if j else block for j in range(lax.axis_size("row"))]


def scatter_rows(partial):
    size = lax.axis_size("row")
    pieces = jnp.split(partial, size, axis=0)
    return [swap_rows(pieces[j], j) if j else pieces[0] for j in range(size)]


def add_up(first, terms):
    total = first.astype(F32)
    for term in terms:
        total = total + term.astype(F32)
    return total


def after(block, other):
    return lax.optimization_barrier((block, other))[0]


def hold_kernel(up_hbm, down_hbm, up, down, sems):
    copies = [
        pltpu.make_async_copy(up_hbm, up, sems.at[0]),
        pltpu.make_async_copy(down_hbm, down, sems.at[1]),
    ]
    for copy in copies:
        copy.start()
    for copy in copies:
        copy.wait()


def hold(up_block, down_block):
    size = up_block.size * 2
    return pl.pallas_call(
        hold_kernel,
        in_specs=[pl.BlockSpec(memory_space=pl.ANY)] * 2,
        out_specs=[pl.BlockSpec(memory_space=pltpu.VMEM)] * 2,
        out_shape=[pltpu.VMEM(up_block.shape, BF), pltpu.VMEM(down_block.shape, BF)],
        scratch_shapes=[pltpu.SemaphoreType.DMA((2,))],
        compiler_params=pltpu.CompilerParams(vmem_limit_bytes=4 * size),
        cost_estimate=pl.CostEstimate(flops=0, bytes_accessed=4 * size, transcendentals=0),
        name="hold",
    )(up_block, down_block)


def sum_cols(partial):
    size = lax.axis_size("col")
    if size > 2:
        return lax.psum(partial, "col").astype(F32)
    total = partial.astype(F32)
    for j in range(1, size):
        total = total + turn(partial, "col", j).astype(F32)
    return total


def silu_slope(value):
    sig = jax.nn.sigmoid(value)
    return sig * (1.0 + value * (1.0 - sig))


def pick(table, index):
    return lax.dynamic_index_in_dim(table, index, 0, keepdims=False)


def matmul(a, b, dims=(((1,), (0,)), ((), ()))):
    return lax.dot_general(a, b, dims, preferred_element_type=F32)


def per_device(inputs, sample_ids, send_base, recv_base, w_up, w_down, cotangent):
    section = lax.axis_index("section")
    sections = lax.axis_size("section")
    ticks = inputs.shape[1]
    up_block, down_block = hold(w_up[0], w_down[0])
    samples = [pick(sample_ids, tick - section + sections - 1) for tick in range(ticks)]
    stored = [pick(send_base[0], samples[tick]) for tick in range(ticks - 1)]
    bases = [jnp.where(section == 0, inputs[0, t], pick(recv_base[0], samples[t])) for t in range(1, ticks)]
    stored, bases = lax.optimization_barrier((stored, [None] + bases))
    full_ins, pres, acts, seen_in, seen_out = [], [], [], [], []
    cot_pieces = [cotangent[0, ticks - 1]] + [None] * (lax.axis_size("row") - 1)
    sending = inputs[0, 0]
    for tick in range(ticks):
        if tick == 0:
            act_in = sending
        else:
            arrived = from_behind(sending, "section", 1)
            chosen = [j for j in range(1, len(cot_pieces)) if (j % 2 == 0) == (tick == 1)] if tick < 3 else []
            for j in chosen:
                cot_pieces[j] = swap_rows(after(cot_pieces[0], sending), j)
            act_in = (bases[tick].astype(F32) + arrived.astype(F32)).astype(BF)
            act_in = after(act_in, [cot_pieces[j] for j in chosen])
        full_in = jnp.concatenate(gather_rows(act_in), axis=0)
        partial = matmul(full_in, up_block).astype(BF)
        if tick == ticks - 1:
            full_cot = jnp.concatenate(cot_pieces, axis=0)
            first_grads = matmul(full_cot, down_block, LAST).astype(BF)
        pre = sum_cols(partial)
        act = jax.nn.silu(pre).astype(BF)
        if tick < ticks - 1:
            terms = scatter_rows(matmul(act, down_block).astype(BF))
            act_out = add_up(act_in, terms).astype(BF)
            sending = (act_out.astype(F32) - stored[tick].astype(F32)).astype(BF)
            seen_out.append(act_out)
        full_ins.append(full_in)
        pres.append(pre)
        acts.append(act)
        seen_in.append(act_in)
    full_grads = [None] * ticks
    pre_grads = [None] * ticks
    seen_grad = [None] * ticks
    for step in range(ticks):
        tick = ticks - 1 - step
        if step == 0:
            grad_out, full_grad, partial = cot_pieces[0], full_cot, first_grads
        else:
            arrived = from_behind(sending, "section", -1)
            if step == 1:
                out_terms = jnp.split(matmul(after(acts[-1], sending), down_block).astype(BF), len(cot_pieces), axis=0)
            chosen = [j for j in range(1, len(cot_pieces)) if (j % 2 == 0) == (step == 1)]
            for j in chosen:
                out_terms[j] = swap_rows(after(out_terms[j], sending), j)
            grad_out = jnp.where(section == sections - 1, cotangent[0, tick], arrived)
            grad_out = after(grad_out, [out_terms[j] for j in chosen])
            full_grad = jnp.concatenate(gather_rows(grad_out), axis=0)
            partial = matmul(full_grad, down_block, LAST).astype(BF)
        grad_act = sum_cols(partial)
        grad_pre = (grad_act * silu_slope(pres[tick])).astype(BF)
        back = matmul(grad_pre, up_block, LAST).astype(BF)
        sending = add_up(grad_out, scatter_rows(back)).astype(BF)
        full_grads[tick] = full_grad
        pre_grads[tick] = grad_pre
        seen_grad[tick] = sending
    seen_out.append(add_up(act_in, out_terms).astype(BF))
    full_ins, pre_grads, acts, full_grads = lax.optimization_barrier(((full_ins, pre_grads, acts, full_grads), back))[0]
    grad_up = matmul(jnp.concatenate(full_ins, axis=0), jnp.concatenate(pre_grads, axis=0), FIRST)
    grad_down = matmul(jnp.concatenate(acts, axis=0), jnp.concatenate(full_grads, axis=0), FIRST)
    return (
        jnp.stack(seen_in)[None],
        jnp.stack(seen_out)[None],
        jnp.stack(seen_grad)[None],
        grad_up.astype(BF)[None],
        grad_down.astype(BF)[None],
    )


def solution(mesh):
    placed = (
        P("section", None, "row", "col"),
        P(),
        P("section", None, "row", "col"),
        P("section", None, "row", "col"),
        P("section", "col", "row"),
        P("section", "row", "col"),
        P("section", None, "row", "col"),
    )
    return jax.shard_map(
        per_device,
        mesh=mesh,
        in_specs=placed,
        out_specs=(
            P("section", None, "row", "col"),
            P("section", None, "row", "col"),
            P("section", None, "row", "col"),
            P("section", "col", "row"),
            P("section", "row", "col"),
        ),
        check_vma=False,
    )
```

```python
import jax
import jax.numpy as jnp
from jax import lax
from jax.experimental import pallas as pl
from jax.experimental.pallas import tpu as pltpu
from jax.sharding import PartitionSpec as P

BF = jnp.bfloat16
F32 = jnp.float32
LAST = (((1,), (1,)), ((), ()))
FIRST = (((0,), (0,)), ((), ()))


def from_behind(block, axis, distance):
    devices = range(lax.axis_size(axis))
    route = [(i - distance, i) for i in devices if i - distance in devices]
    return lax.ppermute(block, axis, route)


def turn(block, axis, distance):
    size = lax.axis_size(axis)
    return lax.ppermute(block, axis, [(i, (i + distance) % size) for i in range(size)])


def partner(row, j, size):
    return row ^ j if size & (size - 1) == 0 else (j - row) % size


def swap_rows(block, j):
    size = lax.axis_size("row")
    return lax.ppermute(block, "row", [(i, partner(i, j, size)) for i in range(size)])


def gather_rows(block):
    return [swap_rows(block, j) if j else block for j in range(lax.axis_size("row"))]


def scatter_rows(pieces):
    return [swap_rows(piece, j) if j else piece for j, piece in enumerate(pieces)]


def beside(turn):
    size = lax.axis_size("row")
    return [[1], [2], range(3, size)][turn] if size > 2 else [[], [], [1]][turn]


def add_up(first, terms):
    total = first.astype(F32)
    for term in terms:
        total = total + term.astype(F32)
    return total


def after(block, other):
    return lax.optimization_barrier((block, other))[0]


def run(kernel, outs, *ins, flops):
    ins = [pltpu.with_memory_space_constraint(block, pltpu.VMEM) for block in ins]
    size = sum(x.size * x.dtype.itemsize for x in [*ins, *outs])
    return pl.pallas_call(
        kernel,
        in_specs=[pl.BlockSpec(memory_space=pltpu.VMEM)] * len(ins),
        out_specs=[pl.BlockSpec(memory_space=pltpu.VMEM)] * len(outs),
        out_shape=[pltpu.VMEM(x.shape, x.dtype) for x in outs],
        compiler_params=pltpu.CompilerParams(vmem_limit_bytes=32 << 20),
        cost_estimate=pl.CostEstimate(flops=flops, bytes_accessed=size, transcendentals=0),
        name=kernel.__name__,
    )(*ins)


def hold_kernel(source, kept, sem):
    copy = pltpu.make_async_copy(source, kept, sem)
    copy.start()
    copy.wait()


def hold(weight, other):
    return pl.pallas_call(
        hold_kernel,
        in_specs=[pl.BlockSpec(memory_space=pltpu.HBM)],
        out_specs=pl.BlockSpec(memory_space=pltpu.VMEM),
        out_shape=pltpu.VMEM(weight.shape, weight.dtype),
        scratch_shapes=[pltpu.SemaphoreType.DMA],
        compiler_params=pltpu.CompilerParams(vmem_limit_bytes=32 << 20),
        cost_estimate=pl.CostEstimate(flops=0, bytes_accessed=4 * weight.size, transcendentals=0),
        name="hold",
    )(after(weight, other))


def columns(width, step=256):
    step = min(width, step)
    return [slice(n, n + step) for n in range(0, width, step)]


def up_product(*refs):
    *pieces, weight, whole, product = refs
    whole[...] = jnp.concatenate([piece[...] for piece in pieces], axis=0)
    for n in columns(product.shape[1]):
        product[:, n] = matmul(whole[...], weight[:, n]).astype(BF)


def back_product(*refs):
    *pieces, weight, whole, product = refs
    whole[...] = jnp.concatenate([piece[...] for piece in pieces], axis=0)
    for n in columns(product.shape[1]):
        product[:, n] = matmul(whole[...], weight[n, :], LAST).astype(BF)


def put_rows(pieces, n, product):
    rows = pieces[0].shape[0]
    for j, piece in enumerate(pieces):
        piece[:, n] = product[j * rows : (j + 1) * rows].astype(BF)


def down_product(mine, other, weight, act, *pieces):
    for n in columns(act.shape[1]):
        pre = mine[:, n].astype(F32) + other[:, n].astype(F32)
        act[:, n] = jax.nn.silu(pre).astype(BF)
    for n in columns(weight.shape[1]):
        put_rows(pieces, n, matmul(act[...], weight[:, n]))


def down_again(act, weight, *pieces):
    for n in columns(weight.shape[1]):
        put_rows(pieces, n, matmul(act[...], weight[:, n]))


def in_product(mine, other, pre_mine, pre_other, weight, grad_pre, *pieces):
    for n in columns(grad_pre.shape[1]):
        pre = pre_mine[:, n].astype(F32) + pre_other[:, n].astype(F32)
        grad = mine[:, n].astype(F32) + other[:, n].astype(F32)
        grad_pre[:, n] = (grad * silu_slope(pre)).astype(BF)
    for n in columns(weight.shape[0]):
        put_rows(pieces, n, matmul(grad_pre[...], weight[n, :], LAST))


def act_only(mine, other, act):
    for n in columns(act.shape[1]):
        pre = mine[:, n].astype(F32) + other[:, n].astype(F32)
        act[:, n] = jax.nn.silu(pre).astype(BF)


def weight_grad(*refs):
    count = len(refs) // 2
    left = jnp.concatenate([ref[...] for ref in refs[:count]], axis=0)
    right = jnp.concatenate([ref[...] for ref in refs[count:-1]], axis=0)
    refs[-1][...] = matmul(left, right, FIRST).astype(BF)


def weight_product(lefts, rights, step=256):
    rows, width, depth = lefts[0].shape[1], rights[0].shape[1], lefts[0].shape[0]
    step = min(rows, step)
    return pl.pallas_call(
        weight_grad,
        grid=(rows // step,),
        in_specs=[pl.BlockSpec((depth, step), lambda i: (0, i))] * len(lefts)
        + [pl.BlockSpec((depth, width), lambda i: (0, 0))] * len(rights),
        out_specs=pl.BlockSpec((step, width), lambda i: (i, 0)),
        out_shape=jax.ShapeDtypeStruct((rows, width), BF),
        compiler_params=pltpu.CompilerParams(vmem_limit_bytes=32 << 20),
        cost_estimate=pl.CostEstimate(
            flops=2 * rows * width * depth * len(lefts), bytes_accessed=2 * rows * width, transcendentals=0
        ),
        name="weight_grad",
    )(*lefts, *rights)


def other_cols(partial):
    size = lax.axis_size("col")
    if size == 2:
        return turn(partial, "col", 1)
    return (lax.psum(partial.astype(F32), "col") - partial.astype(F32)).astype(BF)


def silu_slope(value):
    sig = jax.nn.sigmoid(value)
    return sig * (1.0 + value * (1.0 - sig))


def pick(table, index):
    return lax.dynamic_index_in_dim(table, index, 0, keepdims=False)


def matmul(a, b, dims=(((1,), (0,)), ((), ()))):
    return lax.dot_general(a, b, dims, preferred_element_type=F32)


def per_device(inputs, sample_ids, send_base, recv_base, w_up, w_down, cotangent):
    section = lax.axis_index("section")
    sections = lax.axis_size("section")
    ticks = inputs.shape[1]
    up_block, down_block = w_up[0], w_down[0]
    rows = lax.axis_size("row")
    piece_rows, width = inputs.shape[2:]
    tokens, hidden = rows * piece_rows, up_block.shape[1]
    flops = 2 * tokens * width * hidden
    pieces_like = [jax.ShapeDtypeStruct((piece_rows, width), BF)] * rows
    whole_like = jax.ShapeDtypeStruct((tokens, width), BF)
    hidden_like = jax.ShapeDtypeStruct((tokens, hidden), BF)

    cot_pieces = [cotangent[0, ticks - 1]] + [None] * (rows - 1)
    full_ins, pres, acts, seen_in, seen_out = [], [], [], [], []
    sending = inputs[0, 0]
    for tick in range(ticks):
        if tick == 0:
            act_in = sending
        else:
            arrived = from_behind(sending, "section", 1)
            act_in = (bases[tick].astype(F32) + arrived.astype(F32)).astype(BF)
        pieces = gather_rows(act_in)
        if tick == 0:
            for j in beside(0):
                cot_pieces[j] = swap_rows(after(cot_pieces[0], act_in), j)
            pieces = after(pieces, [cot_pieces[j] for j in beside(0)])
        if tick == ticks - 1:
            full_cot, first_grads = run(
                back_product, [whole_like, hidden_like], *cot_pieces, hold(down_block, act_in), flops=flops
            )
            pieces = after(pieces, first_grads)
        full_in, partial = run(up_product, [whole_like, hidden_like], *pieces, hold(up_block, act_in), flops=flops)
        other = other_cols(partial)
        if tick == 0:
            samples = [pick(after(sample_ids, partial), t - section + sections - 1) for t in range(ticks)]
            stored = [pick(send_base[0], samples[t]) for t in range(ticks - 1)]
            bases = [jnp.where(section == 0, inputs[0, t], pick(recv_base[0], samples[t])) for t in range(1, ticks)]
            stored, bases, other = lax.optimization_barrier((stored, [None] + bases, other))
        if tick < ticks - 1:
            for j in beside(tick + 1):
                cot_pieces[j] = swap_rows(after(cot_pieces[0], partial), j)
            act, *terms = run(
                down_product, [hidden_like, *pieces_like], partial, other, hold(down_block, partial), flops=flops
            )
            terms = after(terms, [cot_pieces[j] for j in beside(tick + 1)])
            act_out = add_up(act_in, scatter_rows(terms)).astype(BF)
            sending = (act_out.astype(F32) - stored[tick].astype(F32)).astype(BF)
            seen_out.append(act_out)
            acts.append(act)
        full_ins.append(full_in)
        pres.append((partial, other))
        seen_in.append(act_in)
    full_grads = [None] * ticks
    pre_grads = [None] * ticks
    seen_grad = [None] * ticks
    for step in range(ticks):
        tick = ticks - 1 - step
        if step == 0:
            grad_out, full_grad, partial = cot_pieces[0], full_cot, first_grads
        else:
            arrived = from_behind(sending, "section", -1)
            grad_out = jnp.where(section == sections - 1, cotangent[0, tick], arrived)
            if step == 1:
                (act,) = run(act_only, [hidden_like], *after(pres[-1], sending), flops=0)
                acts.append(act)
                out_pieces = list(run(down_again, pieces_like, act, hold(down_block, sending), flops=flops))
                grad_out = after(grad_out, out_pieces)
            pieces = gather_rows(grad_out)
            full_grad, partial = run(
                back_product, [whole_like, hidden_like], *pieces, hold(down_block, grad_out), flops=flops
            )
        other = other_cols(partial)
        for j in beside(step) if step else []:
            out_pieces[j] = swap_rows(after(out_pieces[j], partial), j)
        up_kept = hold(up_block, pres[-1][0] if step == 0 else partial)
        grad_pre, *terms = run(
            in_product, [hidden_like, *pieces_like], partial, other, *pres[tick], up_kept, flops=flops
        )
        if step:
            terms = after(terms, [out_pieces[j] for j in beside(step)])
        sending = add_up(grad_out, scatter_rows(terms)).astype(BF)
        full_grads[tick] = full_grad
        pre_grads[tick] = grad_pre
        seen_grad[tick] = sending
    for j in beside(0):
        out_pieces[j] = swap_rows(after(out_pieces[j], terms), j)
    seen_out.append(add_up(act_in, out_pieces).astype(BF))
    acts, full_grads = after((acts, full_grads), terms)
    grad_up = weight_product(full_ins, pre_grads)
    grad_down = weight_product(acts, full_grads)
    return (
        jnp.stack(seen_in)[None],
        jnp.stack(seen_out)[None],
        jnp.stack(seen_grad)[None],
        grad_up[None],
        grad_down[None],
    )


def solution(mesh):
    placed = (
        P("section", None, "row", "col"),
        P(),
        P("section", None, "row", "col"),
        P("section", None, "row", "col"),
        P("section", "col", "row"),
        P("section", "row", "col"),
        P("section", None, "row", "col"),
    )
    return jax.shard_map(
        per_device,
        mesh=mesh,
        in_specs=placed,
        out_specs=(
            P("section", None, "row", "col"),
            P("section", None, "row", "col"),
            P("section", None, "row", "col"),
            P("section", "col", "row"),
            P("section", "row", "col"),
        ),
        check_vma=False,
    )
```

```python
import jax
import jax.numpy as jnp
from jax import lax
from jax.experimental import pallas as pl
from jax.experimental.pallas import tpu as pltpu
from jax.sharding import PartitionSpec as P

BF = jnp.bfloat16
F32 = jnp.float32
LAST = (((1,), (1,)), ((), ()))
FIRST = (((0,), (0,)), ((), ()))


def from_behind(block, axis, distance):
    devices = range(lax.axis_size(axis))
    route = [(i - distance, i) for i in devices if i - distance in devices]
    return lax.ppermute(block, axis, route)


def turn(block, axis, distance):
    size = lax.axis_size(axis)
    return lax.ppermute(block, axis, [(i, (i + distance) % size) for i in range(size)])


def partner(row, j, size):
    return row ^ j if size & (size - 1) == 0 else (j - row) % size


def swap_rows(block, j):
    size = lax.axis_size("row")
    return lax.ppermute(block, "row", [(i, partner(i, j, size)) for i in range(size)])


def gather_rows(block):
    return [swap_rows(block, j) if j else block for j in range(lax.axis_size("row"))]


def scatter_rows(pieces):
    return [swap_rows(piece, j) if j else piece for j, piece in enumerate(pieces)]


def beside(turn):
    size = lax.axis_size("row")
    return [[1], [2], range(3, size)][turn] if size > 2 else [[], [], [1]][turn]


def after(block, other):
    return lax.optimization_barrier((block, other))[0]


def vmem(count):
    return [pl.BlockSpec(memory_space=pltpu.VMEM)] * count


def run(kernel, outs, *ins, flops=0, scratch=()):
    ins = [pltpu.with_memory_space_constraint(block, pltpu.VMEM) for block in ins]
    size = sum(x.size * x.dtype.itemsize for x in [*ins, *outs])
    return pl.pallas_call(
        kernel,
        in_specs=vmem(len(ins)),
        out_specs=vmem(len(outs)),
        out_shape=[pltpu.VMEM(x.shape, x.dtype) for x in outs],
        scratch_shapes=scratch,
        compiler_params=pltpu.CompilerParams(vmem_limit_bytes=6 << 20),
        cost_estimate=pl.CostEstimate(flops=flops, bytes_accessed=size, transcendentals=0),
        name=kernel.__name__,
    )(*ins)


def first_kernel(inputs, cotangent, first, last, sems):
    copies = [
        pltpu.make_async_copy(inputs.at[0, 0], first, sems.at[0]),
        pltpu.make_async_copy(cotangent.at[0, cotangent.shape[1] - 1], last, sems.at[1]),
    ]
    for copy in copies:
        copy.start()
    for copy in copies:
        copy.wait()


def fetch_kernel(sample_ids, inputs, send_base, recv_base, cotangent, *refs):
    ticks = inputs.shape[1]
    count = ticks - 1
    stored, bases, cots = refs[:count], refs[count : 2 * count], refs[2 * count : 3 * count]
    fresh, sems = refs[3 * count :]
    section, sections = lax.axis_index("section"), lax.axis_size("section")
    samples = [sample_ids[tick - section + sections - 1] for tick in range(ticks)]
    copies = []
    for t in range(count):
        copies += [
            pltpu.make_async_copy(send_base.at[0, samples[t]], stored[t], sems.at[4 * t]),
            pltpu.make_async_copy(recv_base.at[0, samples[t + 1]], bases[t], sems.at[4 * t + 1]),
            pltpu.make_async_copy(inputs.at[0, t + 1], fresh.at[t], sems.at[4 * t + 2]),
            pltpu.make_async_copy(cotangent.at[0, t], cots[t], sems.at[4 * t + 3]),
        ]
    for copy in copies:
        copy.start()
    for copy in copies:
        copy.wait()
    for t in range(count):
        bases[t][...] = jnp.where(section == 0, fresh[t], bases[t][...])
        cots[t][...] = jnp.where(section == sections - 1, cots[t][...], jnp.zeros_like(cots[t]))


def fetch(sample_ids, inputs, send_base, recv_base, cotangent):
    count = inputs.shape[1] - 1
    piece = inputs.shape[2:]
    outs = pl.pallas_call(
        fetch_kernel,
        in_specs=[pl.BlockSpec(memory_space=pltpu.SMEM)] + [pl.BlockSpec(memory_space=pltpu.HBM)] * 4,
        out_specs=vmem(3 * count),
        out_shape=[pltpu.VMEM(piece, BF)] * (3 * count),
        scratch_shapes=[pltpu.VMEM((count, *piece), BF), pltpu.SemaphoreType.DMA((4 * count,))],
        compiler_params=pltpu.CompilerParams(vmem_limit_bytes=4 << 20),
        cost_estimate=pl.CostEstimate(flops=0, bytes_accessed=2 << 20, transcendentals=0),
        name="fetch",
    )(sample_ids, *[pltpu.with_memory_space_constraint(x, pltpu.HBM) for x in (inputs, send_base, recv_base, cotangent)])
    return outs[:count], outs[count : 2 * count], outs[2 * count :]


def first_pieces(inputs, cotangent):
    piece = inputs.shape[2:]
    return pl.pallas_call(
        first_kernel,
        in_specs=[pl.BlockSpec(memory_space=pltpu.HBM)] * 2,
        out_specs=vmem(2),
        out_shape=[pltpu.VMEM(piece, BF)] * 2,
        scratch_shapes=[pltpu.SemaphoreType.DMA((2,))],
        compiler_params=pltpu.CompilerParams(vmem_limit_bytes=2 << 20),
        cost_estimate=pl.CostEstimate(flops=0, bytes_accessed=1 << 18, transcendentals=0),
        name="first",
    )(*[pltpu.with_memory_space_constraint(x, pltpu.HBM) for x in (inputs, cotangent)])


def added(first, terms):
    total = first[...].astype(F32)
    for term in terms:
        total = total + term[...].astype(F32)
    return total.astype(BF)


def arrive(base, arrived, out):
    out[...] = added(base, [arrived])


def leave(first, *refs):
    *terms, stored, out, delta = refs
    out[...] = added(first, terms)
    delta[...] = (out[...].astype(F32) - stored[...].astype(F32)).astype(BF)


def leave_back(first, *refs):
    *terms, out = refs
    out[...] = added(first, terms)


def finish(first_out, first_grad, *refs):
    *rest, outs, grads = refs
    count = outs.shape[1] - 1
    terms, known_outs, known_grads = rest[: -2 * count], rest[-2 * count : -count], rest[-count:]
    outs[0, count] = added(first_out, [term.at[1] for term in terms])
    grads[0, 0] = added(first_grad, [term.at[0] for term in terms])
    for t in range(count):
        outs[0, t] = known_outs[t][...]
        grads[0, t + 1] = known_grads[t][...]


def turned(*refs):
    *pieces, out = refs
    out[...] = jnp.concatenate([piece[...] for piece in pieces], axis=0).T


def hold_kernel(source, kept, sem):
    copy = pltpu.make_async_copy(source, kept, sem)
    copy.start()
    copy.wait()


def hold(weight, other):
    return pl.pallas_call(
        hold_kernel,
        in_specs=[pl.BlockSpec(memory_space=pltpu.HBM)],
        out_specs=pl.BlockSpec(memory_space=pltpu.VMEM),
        out_shape=pltpu.VMEM(weight.shape, weight.dtype),
        scratch_shapes=[pltpu.SemaphoreType.DMA],
        compiler_params=pltpu.CompilerParams(vmem_limit_bytes=2 << 20),
        cost_estimate=pl.CostEstimate(flops=0, bytes_accessed=4 * weight.size, transcendentals=0),
        name="hold",
    )(pltpu.with_memory_space_constraint(after(weight, other), pltpu.HBM))


def columns(width, step=256):
    step = min(width, step)
    return [slice(n, n + step) for n in range(0, width, step)]


def up_product(*refs):
    *pieces, weight, product, whole = refs
    whole[...] = jnp.concatenate([piece[...] for piece in pieces], axis=0)
    for n in columns(product.shape[1]):
        product[:, n] = matmul(whole[...], weight[:, n]).astype(BF)


def back_product(*refs):
    *pieces, weight, whole, product = refs
    whole[...] = jnp.concatenate([piece[...] for piece in pieces], axis=0)
    for n in columns(product.shape[1]):
        product[:, n] = matmul(whole[...], weight[n, :], LAST).astype(BF)


def put_rows(pieces, n, product):
    rows = pieces[0].shape[0]
    for j, piece in enumerate(pieces):
        piece[:, n] = product[j * rows : (j + 1) * rows].astype(BF)


def down_product(mine, other, weight, act, *pieces):
    for n in columns(act.shape[1]):
        pre = mine[:, n].astype(F32) + other[:, n].astype(F32)
        act[:, n] = jax.nn.silu(pre).astype(BF)
    for n in columns(weight.shape[1]):
        put_rows(pieces, n, matmul(act[...], weight[:, n]))


def down_again(act, weight, *pieces):
    for n in columns(weight.shape[1]):
        put_rows(pieces, n, matmul(act[...], weight[:, n]))


def in_product(mine, other, pre_mine, pre_other, weight, grad_pre, *pieces):
    for n in columns(grad_pre.shape[1]):
        pre = pre_mine[:, n].astype(F32) + pre_other[:, n].astype(F32)
        grad = mine[:, n].astype(F32) + other[:, n].astype(F32)
        grad_pre[:, n] = (grad * silu_slope(pre)).astype(BF)
    for n in columns(weight.shape[0]):
        put_rows(pieces, n, matmul(grad_pre[...], weight[n, :], LAST))


def in_product_last(*refs):
    *ins, grad_pre = refs[: 6 + (len(refs) - 6) // 2]
    pairs = refs[len(ins) + 1 :]
    for piece, pair in zip(ins[5:], pairs):
        pair[1] = piece[...]
    in_product(*ins[:5], grad_pre, *[pair.at[0] for pair in pairs])


def act_only(mine, other, act):
    for n in columns(act.shape[1]):
        pre = mine[:, n].astype(F32) + other[:, n].astype(F32)
        act[:, n] = jax.nn.silu(pre).astype(BF)


def weight_grad(*refs):
    count = len(refs) // 2
    left = jnp.concatenate([ref[...] for ref in refs[:count]], axis=1)
    for n in columns(refs[-1].shape[1], 512):
        right = jnp.concatenate([ref[:, n] for ref in refs[count:-1]], axis=0)
        refs[-1][:, n] = matmul(left, right).astype(BF)


def weight_product(lefts, rights, step=256):
    rows, width, depth = lefts[0].shape[0], rights[0].shape[1], rights[0].shape[0]
    step = min(rows, step)
    return pl.pallas_call(
        weight_grad,
        grid=(rows // step,),
        in_specs=[pl.BlockSpec((step, depth), lambda i: (i, 0))] * len(lefts)
        + [pl.BlockSpec((depth, width), lambda i: (0, 0))] * len(rights),
        out_specs=pl.BlockSpec((step, width), lambda i: (i, 0)),
        out_shape=jax.ShapeDtypeStruct((rows, width), BF),
        compiler_params=pltpu.CompilerParams(vmem_limit_bytes=16 << 20),
        cost_estimate=pl.CostEstimate(
            flops=2 * rows * width * depth * len(lefts), bytes_accessed=2 * rows * width, transcendentals=0
        ),
        name="weight_grad",
    )(*lefts, *rights)


def other_cols(partial):
    size = lax.axis_size("col")
    if size == 2:
        return turn(partial, "col", 1)
    return (lax.psum(partial.astype(F32), "col") - partial.astype(F32)).astype(BF)


def silu_slope(value):
    sig = jax.nn.sigmoid(value)
    return sig * (1.0 + value * (1.0 - sig))


def matmul(a, b, dims=(((1,), (0,)), ((), ()))):
    return lax.dot_general(a, b, dims, preferred_element_type=F32)


def per_device(inputs, sample_ids, send_base, recv_base, w_up, w_down, cotangent):
    ticks = inputs.shape[1]
    up_block, down_block = w_up[0], w_down[0]
    rows = lax.axis_size("row")
    piece_rows, width = inputs.shape[2:]
    tokens, hidden = rows * piece_rows, up_block.shape[1]
    flops = 2 * tokens * width * hidden
    piece_like = jax.ShapeDtypeStruct((piece_rows, width), BF)
    pair_like = jax.ShapeDtypeStruct((2, piece_rows, width), BF)
    whole_like = jax.ShapeDtypeStruct((tokens, width), BF)
    hidden_like = jax.ShapeDtypeStruct((tokens, hidden), BF)
    turned_like = jax.ShapeDtypeStruct((width, tokens), BF)
    turned_hidden = jax.ShapeDtypeStruct((hidden, tokens), BF)
    room = [pltpu.VMEM((tokens, width), BF)]

    act_in, last_cot = first_pieces(inputs, cotangent)
    cot_pieces = [last_cot] + [None] * (rows - 1)
    in_pieces, acts, pres, seen_in, seen_out = [], [], [], [], []
    turned_ins, turned_acts = [], []
    for tick in range(ticks):
        if tick:
            (act_in,) = run(arrive, [piece_like], bases[tick - 1], from_behind(sending, "section", 1))
        pieces = gather_rows(act_in)
        if tick == 0:
            for j in beside(0):
                cot_pieces[j] = swap_rows(after(cot_pieces[0], act_in), j)
            stored, bases, cots = fetch(after(sample_ids, act_in), inputs, send_base, recv_base, cotangent)
            pieces = after(pieces, ([cot_pieces[j] for j in beside(0)], stored))
        if tick == ticks - 1:
            full_cot, first_grads = run(
                back_product, [whole_like, hidden_like], *cot_pieces, hold(down_block, act_in), flops=flops
            )
            pieces = after(pieces, first_grads)
        (partial,) = run(up_product, [hidden_like], *pieces, hold(up_block, act_in), flops=flops, scratch=room)
        other = other_cols(partial)
        if tick < ticks - 1:
            for j in beside(tick + 1):
                cot_pieces[j] = swap_rows(after(cot_pieces[0], partial), j)
            act, *terms = run(
                down_product, [hidden_like] + [piece_like] * rows, partial, other, hold(down_block, partial), flops=flops
            )
            terms = after(terms, [cot_pieces[j] for j in beside(tick + 1)])
            acts.append(act)
            terms_in = scatter_rows(terms)
            if tick == 1:
                turned_ins += run(turned, [turned_like], *after(in_pieces[0], terms))
                turned_acts += run(turned, [turned_hidden], after(acts[0], terms))
                terms_in[0] = after(terms_in[0], (turned_ins, turned_acts))
            act_out, sending = run(leave, [piece_like] * 2, act_in, *terms_in, stored[tick])
            seen_out.append(act_out)
        in_pieces.append(pieces)
        pres.append((partial, other))
        seen_in.append(act_in)
    full_grads = [None] * ticks
    pre_grads = [None] * ticks
    seen_grad = [None] * ticks
    for step in range(ticks):
        tick = ticks - 1 - step
        if step == 0:
            grad_out, full_grad, partial = last_cot, full_cot, first_grads
        else:
            arrived = from_behind(sending, "section", -1)
            if step == 1:
                (act,) = run(act_only, [hidden_like], *after(pres[-1], sending))
                acts.append(act)
                out_pieces = run(down_again, [piece_like] * rows, act, hold(down_block, sending), flops=flops)
                arrived = after(arrived, out_pieces)
            (grad_out,) = run(arrive, [piece_like], cots[tick], arrived)
            pieces = gather_rows(grad_out)
            full_grad, partial = run(
                back_product, [whole_like, hidden_like], *pieces, hold(down_block, grad_out), flops=flops
            )
        other = other_cols(partial)
        up_kept = hold(up_block, pres[-1][0] if step == 0 else partial)
        if step < ticks - 1:
            grad_pre, *terms = run(
                in_product,
                [hidden_like] + [piece_like] * rows,
                partial, other, *pres[tick], up_kept,
                flops=flops,
            )
            terms_in = scatter_rows(terms)
            while len(turned_ins) < min(step + 2, ticks):
                turned_ins += run(turned, [turned_like], *after(in_pieces[len(turned_ins)], terms))
                turned_acts += run(turned, [turned_hidden], after(acts[len(turned_acts)], terms))
            terms_in[0] = after(terms_in[0], (turned_ins, turned_acts))
            (sending,) = run(leave_back, [piece_like], grad_out, *terms_in)
            seen_grad[tick] = sending
        else:
            grad_pre, *terms = run(
                in_product_last,
                [hidden_like] + [pair_like] * rows,
                partial, other, *pres[tick], up_kept, *out_pieces,
                flops=flops,
            )
            terms_in = scatter_rows(terms)
        full_grads[tick] = full_grad
        pre_grads[tick] = grad_pre
    lefts = after((turned_ins, turned_acts), terms)
    grad_up = weight_product(lefts[0], pre_grads)
    grad_down = weight_product(lefts[1], full_grads)
    stack_like = jax.ShapeDtypeStruct((1, ticks, piece_rows, width), BF)
    terms_in[0] = after(terms_in[0], (grad_up, grad_down))
    section_output, input_grad = pl.pallas_call(
        finish,
        in_specs=vmem(2 + rows + 2 * (ticks - 1)),
        out_specs=vmem(2),
        out_shape=[stack_like] * 2,
        compiler_params=pltpu.CompilerParams(vmem_limit_bytes=6 << 20),
        name="finish",
    )(act_in, grad_out, *terms_in, *seen_out, *seen_grad[1:])
    return (
        jnp.stack(seen_in)[None],
        section_output,
        input_grad,
        grad_up[None],
        grad_down[None],
    )


def solution(mesh):
    placed = (
        P("section", None, "row", "col"),
        P(),
        P("section", None, "row", "col"),
        P("section", None, "row", "col"),
        P("section", "col", "row"),
        P("section", "row", "col"),
        P("section", None, "row", "col"),
    )
    return jax.shard_map(
        per_device,
        mesh=mesh,
        in_specs=placed,
        out_specs=(
            P("section", None, "row", "col"),
            P("section", None, "row", "col"),
            P("section", None, "row", "col"),
            P("section", "col", "row"),
            P("section", "row", "col"),
        ),
        check_vma=False,
    )
```

```python
import jax
import jax.numpy as jnp
from jax import lax
from jax.experimental import pallas as pl
from jax.experimental.pallas import tpu as pltpu
from jax.sharding import PartitionSpec as P

BF = jnp.bfloat16
F32 = jnp.float32
WEIGHT_CUTS = 8


def from_behind(block, axis, distance):
    devices = range(lax.axis_size(axis))
    route = [(i - distance, i) for i in devices if i - distance in devices]
    return lax.ppermute(block, axis, route)


def turn(block, axis, distance):
    size = lax.axis_size(axis)
    return lax.ppermute(block, axis, [(i, (i + distance) % size) for i in range(size)])


def partner(row, j, size):
    return row ^ ((size - j) % size) if size & (size - 1) == 0 else (j - row) % size


def swap_rows(block, j):
    size = lax.axis_size("row")
    return lax.ppermute(block, "row", [(i, partner(i, j, size)) for i in range(size)])


def gather_rows(block):
    return [swap_rows(block, j) if j else block for j in range(lax.axis_size("row"))]


def scatter_rows(pieces):
    return [swap_rows(piece, j) if j else piece for j, piece in enumerate(pieces)]


def beside(turn):
    size = lax.axis_size("row")
    return [[size - 1], [size - 2], range(1, size - 2)][turn] if size > 2 else [[], [], [1]][turn]


def after(block, other):
    return lax.optimization_barrier((block, other))[0]


def vmem(count):
    return [pl.BlockSpec(memory_space=pltpu.VMEM)] * count


def run(kernel, outs, *ins, flops=0, scratch=()):
    ins = [pltpu.with_memory_space_constraint(block, pltpu.VMEM) for block in ins]
    size = sum(x.size * x.dtype.itemsize for x in [*ins, *outs])
    return pl.pallas_call(
        kernel,
        in_specs=vmem(len(ins)),
        out_specs=vmem(len(outs)),
        out_shape=[pltpu.VMEM(x.shape, x.dtype) for x in outs],
        scratch_shapes=scratch,
        compiler_params=pltpu.CompilerParams(vmem_limit_bytes=6 << 20),
        cost_estimate=pl.CostEstimate(flops=flops, bytes_accessed=size, transcendentals=0),
        name=kernel.__name__,
    )(*ins)


def first_kernel(inputs, cotangent, first, last, sems):
    copies = [
        pltpu.make_async_copy(inputs.at[0, 0], first, sems.at[0]),
        pltpu.make_async_copy(cotangent.at[0, cotangent.shape[1] - 1], last, sems.at[1]),
    ]
    for copy in copies:
        copy.start()
    for copy in copies:
        copy.wait()


def fetch_kernel(sample_ids, inputs, send_base, recv_base, cotangent, *refs):
    ticks = inputs.shape[1]
    count = ticks - 1
    weights, refs = refs[:2], refs[2:]
    stored, bases, cots = refs[:count], refs[count : 2 * count], refs[2 * count : 3 * count]
    *kept, fresh, sems, weight_sems = refs[3 * count :]
    section, sections = lax.axis_index("section"), lax.axis_size("section")
    samples = [sample_ids[tick - section + sections - 1] for tick in range(ticks)]
    copies = []
    for t in range(count):
        copies += [
            pltpu.make_async_copy(send_base.at[0, samples[t]], stored[t], sems.at[4 * t]),
            pltpu.make_async_copy(recv_base.at[0, samples[t + 1]], bases[t], sems.at[4 * t + 1]),
            pltpu.make_async_copy(inputs.at[0, t + 1], fresh.at[t], sems.at[4 * t + 2]),
            pltpu.make_async_copy(cotangent.at[0, t], cots[t], sems.at[4 * t + 3]),
        ]
    for k, (weight, room) in enumerate(zip(weights, kept)):
        step = weight.shape[0] // WEIGHT_CUTS
        for i in range(WEIGHT_CUTS):
            part = pl.ds(i * step, step)
            copies.append(pltpu.make_async_copy(weight.at[part], room.at[part], weight_sems.at[k, i]))
    for copy in copies:
        copy.start()
    for copy in copies:
        copy.wait()
    for t in range(count):
        bases[t][...] = jnp.where(section == 0, fresh[t], bases[t][...])
        cots[t][...] = jnp.where(section == sections - 1, cots[t][...], jnp.zeros_like(cots[t]))


def fetch(sample_ids, inputs, send_base, recv_base, cotangent, *weights):
    count = inputs.shape[1] - 1
    piece = inputs.shape[2:]
    large = [pltpu.with_memory_space_constraint(x, pltpu.HBM) for x in (inputs, send_base, recv_base, cotangent, *weights)]
    *outs, up_kept, down_kept = pl.pallas_call(
        fetch_kernel,
        in_specs=[pl.BlockSpec(memory_space=pltpu.SMEM)] + [pl.BlockSpec(memory_space=pltpu.HBM)] * len(large),
        out_specs=vmem(3 * count + 2),
        out_shape=[pltpu.VMEM(piece, BF)] * (3 * count) + [pltpu.VMEM(x.shape, BF) for x in weights],
        scratch_shapes=[
            pltpu.VMEM((count, *piece), BF),
            pltpu.SemaphoreType.DMA((4 * count,)),
            pltpu.SemaphoreType.DMA((2, WEIGHT_CUTS)),
        ],
        compiler_params=pltpu.CompilerParams(vmem_limit_bytes=4 << 20),
        cost_estimate=pl.CostEstimate(flops=0, bytes_accessed=10 << 20, transcendentals=0),
        name="fetch",
    )(sample_ids, *large)
    return outs[:count], outs[count : 2 * count], outs[2 * count :], up_kept, down_kept


def first_pieces(inputs, cotangent):
    piece = inputs.shape[2:]
    return pl.pallas_call(
        first_kernel,
        in_specs=[pl.BlockSpec(memory_space=pltpu.HBM)] * 2,
        out_specs=vmem(2),
        out_shape=[pltpu.VMEM(piece, BF)] * 2,
        scratch_shapes=[pltpu.SemaphoreType.DMA((2,))],
        compiler_params=pltpu.CompilerParams(vmem_limit_bytes=2 << 20),
        cost_estimate=pl.CostEstimate(flops=0, bytes_accessed=1 << 18, transcendentals=0),
        name="first",
    )(*[pltpu.with_memory_space_constraint(x, pltpu.HBM) for x in (inputs, cotangent)])


def added(first, terms):
    total = first[...].astype(F32)
    for term in terms:
        total = total + term[...].astype(F32)
    return total.astype(BF)


def arrive(base, arrived, out):
    out[...] = added(base, [arrived])


def leave(first, *refs):
    *terms, stored, out, delta = refs
    out[...] = added(first, terms)
    delta[...] = (out[...].astype(F32) - stored[...].astype(F32)).astype(BF)


def leave_back(first, *refs):
    *terms, out = refs
    out[...] = added(first, terms)


def finish(first_out, first_grad, *refs):
    *rest, outs, grads = refs
    count = outs.shape[1] - 1
    terms, known = rest[: -2 * count], rest[-2 * count :]
    half = len(terms) // 2
    outs[0, count] = added(first_out, terms[:half])
    grads[0, 0] = added(first_grad, terms[half:])
    for t in range(count):
        outs[0, t] = known[t][...]
        grads[0, t + 1] = known[count + t][...]


def turned(*refs):
    *pieces, out = refs
    out[...] = jnp.concatenate([piece[...] for piece in pieces], axis=0).T


def turned_weight(weight, out):
    for n in columns(out.shape[0]):
        out[n, :] = weight[:, n].T


def columns(width, step=256):
    step = min(width, step)
    return [slice(n, n + step) for n in range(0, width, step)]


def up_product(*refs):
    *pieces, weight, product, whole = refs
    whole[...] = jnp.concatenate([piece[...] for piece in pieces], axis=0)
    for n in columns(product.shape[1]):
        product[:, n] = matmul(whole[...], weight[:, n]).astype(BF)


def back_product(*refs):
    *ins, whole, product = refs
    up_product(*ins, product, whole)


def put_rows(pieces, n, product):
    rows = pieces[0].shape[0]
    for j, piece in enumerate(pieces):
        piece[:, n] = product[j * rows : (j + 1) * rows].astype(BF)


def down_product(mine, other, weight, act, *pieces):
    for n in columns(act.shape[1]):
        pre = mine[:, n].astype(F32) + other[:, n].astype(F32)
        act[:, n] = jax.nn.silu(pre).astype(BF)
    for n in columns(weight.shape[1]):
        put_rows(pieces, n, matmul(act[...], weight[:, n]))


def down_again(act, weight, *pieces):
    for n in columns(weight.shape[1]):
        put_rows(pieces, n, matmul(act[...], weight[:, n]))


def in_product(mine, other, pre_mine, pre_other, weight, grad_pre, *pieces):
    for n in columns(grad_pre.shape[1]):
        pre = pre_mine[:, n].astype(F32) + pre_other[:, n].astype(F32)
        grad = mine[:, n].astype(F32) + other[:, n].astype(F32)
        grad_pre[:, n] = (grad * silu_slope(pre)).astype(BF)
    for n in columns(weight.shape[1]):
        put_rows(pieces, n, matmul(grad_pre[...], weight[:, n]))


def act_only(mine, other, act):
    for n in columns(act.shape[1]):
        pre = mine[:, n].astype(F32) + other[:, n].astype(F32)
        act[:, n] = jax.nn.silu(pre).astype(BF)


def weight_grad(*refs):
    *blocks, out, left, right, room, sems = refs
    count = len(blocks) // 2
    depth = blocks[-1].shape[0]
    for t in range(count):
        left[:, t * depth : (t + 1) * depth] = blocks[t][...]
        right[t * depth : (t + 1) * depth, :] = blocks[count + t][...]
    copies = []
    for i, m in enumerate(columns(out.shape[0])):
        for n in columns(out.shape[1]):
            room[m, n] = matmul(left[m, :], right[:, n]).astype(BF)
        part = pl.ds(m.start, m.stop - m.start)
        copies.append(pltpu.make_async_copy(room.at[part], out.at[part], sems.at[i]))
        copies[-1].start()
    for copy in copies:
        copy.wait()


def weight_product(lefts, rights):
    rows, width, depth = lefts[0].shape[0], rights[0].shape[1], rights[0].shape[0] * len(rights)
    return pl.pallas_call(
        weight_grad,
        in_specs=vmem(len(lefts) + len(rights)),
        out_specs=pl.BlockSpec(memory_space=pl.ANY),
        out_shape=jax.ShapeDtypeStruct((rows, width), BF),
        scratch_shapes=[
            pltpu.VMEM((rows, depth), BF),
            pltpu.VMEM((depth, width), BF),
            pltpu.VMEM((rows, width), BF),
            pltpu.SemaphoreType.DMA((len(columns(rows)),)),
        ],
        compiler_params=pltpu.CompilerParams(vmem_limit_bytes=12 << 20),
        cost_estimate=pl.CostEstimate(
            flops=2 * rows * width * depth, bytes_accessed=2 * rows * width, transcendentals=0
        ),
        name="weight_grad",
    )(*[pltpu.with_memory_space_constraint(x, pltpu.VMEM) for x in (*lefts, *rights)])


def other_cols(partial):
    size = lax.axis_size("col")
    if size == 2:
        return turn(partial, "col", 1)
    return (lax.psum(partial.astype(F32), "col") - partial.astype(F32)).astype(BF)


def silu_slope(value):
    sig = jax.nn.sigmoid(value)
    return sig * (1.0 + value * (1.0 - sig))


def matmul(a, b, dims=(((1,), (0,)), ((), ()))):
    return lax.dot_general(a, b, dims, preferred_element_type=F32)


def per_device(inputs, sample_ids, send_base, recv_base, w_up, w_down, cotangent):
    ticks = inputs.shape[1]
    rows = lax.axis_size("row")
    piece_rows, width = inputs.shape[2:]
    tokens, hidden = rows * piece_rows, w_up.shape[2]
    flops = 2 * tokens * width * hidden
    piece_like = jax.ShapeDtypeStruct((piece_rows, width), BF)
    whole_like = jax.ShapeDtypeStruct((tokens, width), BF)
    hidden_like = jax.ShapeDtypeStruct((tokens, hidden), BF)
    turned_like = jax.ShapeDtypeStruct((width, tokens), BF)
    turned_hidden = jax.ShapeDtypeStruct((hidden, tokens), BF)
    split_like = [hidden_like] + [piece_like] * rows
    room = [pltpu.VMEM((tokens, width), BF)]

    act_in, last_cot = first_pieces(inputs, cotangent)
    cot_pieces = [last_cot] + [None] * (rows - 1)
    in_pieces, acts, pres, seen_in, seen_out = [], [], [], [], []
    turned_ins, turned_acts = [], []
    for tick in range(ticks):
        if tick:
            (act_in,) = run(arrive, [piece_like], bases[tick - 1], from_behind(sending, "section", 1))
        pieces = gather_rows(act_in)
        if tick == 0:
            for j in beside(0):
                cot_pieces[j] = swap_rows(after(cot_pieces[0], act_in), j)
            stored, bases, cots, up_kept, down_kept = fetch(
                after(sample_ids, act_in), inputs, send_base, recv_base, cotangent, w_up[0], w_down[0]
            )
            pieces = after(pieces, ([cot_pieces[j] for j in beside(0)], stored))
        if tick == ticks - 1:
            full_cot, first_grads = run(
                back_product, [whole_like, hidden_like], *cot_pieces, after(down_turned, act_in), flops=flops
            )
            pieces = after(pieces, first_grads)
        (partial,) = run(up_product, [hidden_like], *pieces, up_kept, flops=flops, scratch=room)
        other = other_cols(partial)
        if tick < ticks - 1:
            for j in beside(tick + 1):
                cot_pieces[j] = swap_rows(after(cot_pieces[0], partial), j)
            act, *terms = run(down_product, split_like, partial, other, down_kept, flops=flops)
            terms = after(terms, [cot_pieces[j] for j in beside(tick + 1)])
            acts.append(act)
            terms_in = scatter_rows(terms)
            if tick == 0:
                (down_turned,) = run(
                    turned_weight, [jax.ShapeDtypeStruct((width, hidden), BF)], after(down_kept, terms)
                )
                terms_in[0] = after(terms_in[0], down_turned)
            if tick == 1:
                (up_turned,) = run(turned_weight, [jax.ShapeDtypeStruct((hidden, width), BF)], after(up_kept, terms))
                turned_ins += run(turned, [turned_like], *after(in_pieces[0], terms))
                turned_acts += run(turned, [turned_hidden], after(acts[0], terms))
                terms_in[0] = after(terms_in[0], (up_turned, turned_ins, turned_acts))
            act_out, sending = run(leave, [piece_like] * 2, act_in, *terms_in, stored[tick])
            seen_out.append(act_out)
        in_pieces.append(pieces)
        pres.append((partial, other))
        seen_in.append(act_in)
    full_grads = [None] * ticks
    pre_grads = [None] * ticks
    seen_grad = [None] * ticks
    for step in range(ticks):
        tick = ticks - 1 - step
        if step == 0:
            grad_out, full_grad, partial = last_cot, full_cot, first_grads
        else:
            arrived = from_behind(sending, "section", -1)
            if step == 1:
                (act,) = run(act_only, [hidden_like], *after(pres[-1], sending))
                acts.append(act)
                out_pieces = run(down_again, [piece_like] * rows, act, down_kept, flops=flops)
                arrived = after(arrived, out_pieces)
                out_terms = list(out_pieces)
            (grad_out,) = run(arrive, [piece_like], cots[tick], arrived)
            pieces = gather_rows(grad_out)
            full_grad, partial = run(back_product, [whole_like, hidden_like], *pieces, down_turned, flops=flops)
        other = other_cols(partial)
        for j in beside(step) if step else []:
            out_terms[j] = swap_rows(after(out_pieces[j], partial), j)
        grad_pre, *terms = run(in_product, split_like, partial, other, *pres[tick], up_turned, flops=flops)
        if step:
            terms = after(terms, [out_terms[j] for j in beside(step)])
        terms_in = scatter_rows(terms)
        if step < ticks - 1:
            while len(turned_ins) < min(step + 2, ticks):
                turned_ins += run(turned, [turned_like], *after(in_pieces[len(turned_ins)], terms))
                turned_acts += run(turned, [turned_hidden], after(acts[len(turned_acts)], terms))
            terms_in[0] = after(terms_in[0], (turned_ins, turned_acts))
            (sending,) = run(leave_back, [piece_like], grad_out, *terms_in)
            seen_grad[tick] = sending
        full_grads[tick] = full_grad
        pre_grads[tick] = grad_pre
    for j in beside(0):
        out_terms[j] = swap_rows(after(out_pieces[j], terms), j)
    lefts = after((turned_ins, turned_acts), terms)
    grad_up = weight_product(lefts[0], pre_grads)
    grad_down = weight_product(lefts[1], full_grads)
    stack_like = jax.ShapeDtypeStruct((1, ticks, piece_rows, width), BF)
    terms_in[0] = after(terms_in[0], (grad_up, grad_down))
    section_output, input_grad = pl.pallas_call(
        finish,
        in_specs=vmem(2 + 2 * rows + 2 * (ticks - 1)),
        out_specs=vmem(2),
        out_shape=[stack_like] * 2,
        compiler_params=pltpu.CompilerParams(vmem_limit_bytes=6 << 20),
        name="finish",
    )(act_in, grad_out, *out_terms, *terms_in, *seen_out, *seen_grad[1:])
    return (
        jnp.stack(seen_in)[None],
        section_output,
        input_grad,
        grad_up[None],
        grad_down[None],
    )


def solution(mesh):
    placed = (
        P("section", None, "row", "col"),
        P(),
        P("section", None, "row", "col"),
        P("section", None, "row", "col"),
        P("section", "col", "row"),
        P("section", "row", "col"),
        P("section", None, "row", "col"),
    )
    return jax.shard_map(
        per_device,
        mesh=mesh,
        in_specs=placed,
        out_specs=(
            P("section", None, "row", "col"),
            P("section", None, "row", "col"),
            P("section", None, "row", "col"),
            P("section", "col", "row"),
            P("section", "row", "col"),
        ),
        check_vma=False,
    )
```

```python
import functools

import jax
import jax.numpy as jnp
from jax import lax
from jax.experimental import pallas as pl
from jax.experimental.pallas import tpu as pltpu
from jax.sharding import PartitionSpec as P

BF = jnp.bfloat16
F32 = jnp.float32
WEIGHT_CUTS = 8


def hand_over(block):
    count = lax.axis_size("section")
    within = [(s, s ^ 1) for s in range(count)]
    across = [(s, s + 1 if s % 2 else s - 1) for s in range(count)]
    return [
        lax.ppermute(block, "section", [(s, t) for s, t in pairs if 0 <= t < count]) for pairs in (within, across)
    ]


def turn(block, axis, distance):
    size = lax.axis_size(axis)
    return lax.ppermute(block, axis, [(i, (i + distance) % size) for i in range(size)])


def partner(row, j, size):
    return row ^ ((size - j) % size) if size & (size - 1) == 0 else (j - row) % size


def swap_rows(block, j):
    size = lax.axis_size("row")
    return lax.ppermute(block, "row", [(i, partner(i, j, size)) for i in range(size)])


def gather_rows(block):
    return [swap_rows(block, j) if j else block for j in range(lax.axis_size("row"))]


def scatter_rows(pieces):
    return [swap_rows(piece, j) if j else piece for j, piece in enumerate(pieces)]


def beside(turn):
    size = lax.axis_size("row")
    return [[size - 1], [size - 2], range(1, size - 2)][turn] if size > 2 else [[], [], [1]][turn]


def after(block, other):
    return lax.optimization_barrier((block, other))[0]


def vmem(count):
    return [pl.BlockSpec(memory_space=pltpu.VMEM)] * count


def run(kernel, outs, *ins, flops=0, scratch=()):
    ins = [pltpu.with_memory_space_constraint(block, pltpu.VMEM) for block in ins]
    size = sum(x.size * x.dtype.itemsize for x in [*ins, *outs])
    return pl.pallas_call(
        kernel,
        in_specs=vmem(len(ins)),
        out_specs=vmem(len(outs)),
        out_shape=[pltpu.VMEM(x.shape, x.dtype) for x in outs],
        scratch_shapes=scratch,
        compiler_params=pltpu.CompilerParams(vmem_limit_bytes=6 << 20),
        cost_estimate=pl.CostEstimate(flops=flops, bytes_accessed=size, transcendentals=0),
        name=kernel.__name__,
    )(*ins)


def first_kernel(inputs, cotangent, first, last, sems):
    copies = [
        pltpu.make_async_copy(inputs.at[0, 0], first, sems.at[0]),
        pltpu.make_async_copy(cotangent.at[0, cotangent.shape[1] - 1], last, sems.at[1]),
    ]
    for copy in copies:
        copy.start()
    for copy in copies:
        copy.wait()


def fetch_kernel(sample_ids, inputs, send_base, recv_base, cotangent, *refs):
    ticks = inputs.shape[1]
    count = ticks - 1
    weights, refs = refs[:1], refs[1:]
    stored, bases, cots = refs[:count], refs[count : 2 * count], refs[2 * count : 3 * count]
    *kept, fresh, sems, weight_sems = refs[3 * count :]
    section, sections = lax.axis_index("section"), lax.axis_size("section")
    samples = [sample_ids[tick - section + sections - 1] for tick in range(ticks)]
    copies = []
    for t in range(count):
        copies += [
            pltpu.make_async_copy(send_base.at[0, samples[t]], stored[t], sems.at[4 * t]),
            pltpu.make_async_copy(recv_base.at[0, samples[t + 1]], bases[t], sems.at[4 * t + 1]),
            pltpu.make_async_copy(inputs.at[0, t + 1], fresh.at[t], sems.at[4 * t + 2]),
            pltpu.make_async_copy(cotangent.at[0, t], cots[t], sems.at[4 * t + 3]),
        ]
    for k, (weight, room) in enumerate(zip(weights, kept)):
        step = weight.shape[0] // WEIGHT_CUTS
        for i in range(WEIGHT_CUTS):
            part = pl.ds(i * step, step)
            copies.append(pltpu.make_async_copy(weight.at[part], room.at[part], weight_sems.at[k, i]))
    for copy in copies:
        copy.start()
    for copy in copies:
        copy.wait()
    for t in range(count):
        bases[t][...] = jnp.where(section == 0, fresh[t], bases[t][...])
        cots[t][...] = jnp.where(section == sections - 1, cots[t][...], jnp.zeros_like(cots[t]))


def fetch(sample_ids, inputs, send_base, recv_base, cotangent, weight):
    count = inputs.shape[1] - 1
    piece = inputs.shape[2:]
    large = [pltpu.with_memory_space_constraint(x, pltpu.HBM) for x in (inputs, send_base, recv_base, cotangent, weight)]
    *outs, kept = pl.pallas_call(
        fetch_kernel,
        in_specs=[pl.BlockSpec(memory_space=pltpu.SMEM)] + [pl.BlockSpec(memory_space=pltpu.HBM)] * len(large),
        out_specs=vmem(3 * count + 1),
        out_shape=[pltpu.VMEM(piece, BF)] * (3 * count) + [pltpu.VMEM(weight.shape, BF)],
        scratch_shapes=[
            pltpu.VMEM((count, *piece), BF),
            pltpu.SemaphoreType.DMA((4 * count,)),
            pltpu.SemaphoreType.DMA((1, WEIGHT_CUTS)),
        ],
        compiler_params=pltpu.CompilerParams(vmem_limit_bytes=4 << 20),
        cost_estimate=pl.CostEstimate(flops=0, bytes_accessed=6 << 20, transcendentals=0),
        name="fetch",
    )(sample_ids, *large)
    return outs[:count], outs[count : 2 * count], outs[2 * count :], kept


def first_pieces(inputs, cotangent):
    piece = inputs.shape[2:]
    return pl.pallas_call(
        first_kernel,
        in_specs=[pl.BlockSpec(memory_space=pltpu.HBM)] * 2,
        out_specs=vmem(2),
        out_shape=[pltpu.VMEM(piece, BF)] * 2,
        scratch_shapes=[pltpu.SemaphoreType.DMA((2,))],
        compiler_params=pltpu.CompilerParams(vmem_limit_bytes=2 << 20),
        cost_estimate=pl.CostEstimate(flops=0, bytes_accessed=1 << 18, transcendentals=0),
        name="first",
    )(*[pltpu.with_memory_space_constraint(x, pltpu.HBM) for x in (inputs, cotangent)])


def added(first, terms):
    total = first[...].astype(F32)
    for term in terms:
        total = total + term[...].astype(F32)
    return total.astype(BF)


def arrive(base, within, across, out):
    odd = lax.axis_index("section") % 2 == 1
    out[...] = added(base, [jnp.where(odd, within[...], across[...])])


def arrive_back(base, within, across, out):
    odd = lax.axis_index("section") % 2 == 1
    out[...] = added(base, [jnp.where(odd, across[...], within[...])])


def leave(first, *refs):
    *terms, stored, out, delta = refs
    out[...] = added(first, terms)
    delta[...] = (out[...].astype(F32) - stored[...].astype(F32)).astype(BF)


def leave_back(first, *refs):
    *terms, out = refs
    out[...] = added(first, terms)


def finish(first_out, first_grad, *refs):
    *rest, ins, outs, grads = refs
    count = outs.shape[1] - 1
    terms, known = rest[: -3 * count - 1], rest[-3 * count - 1 :]
    half = len(terms) // 2
    outs[0, count] = added(first_out, terms[:half])
    grads[0, 0] = added(first_grad, terms[half:])
    for t in range(count):
        outs[0, t] = known[t][...]
        grads[0, t + 1] = known[count + t][...]
    for t in range(count + 1):
        ins[0, t] = known[2 * count + t][...]


def turned(*refs):
    *pieces, out = refs
    out[...] = jnp.concatenate([piece[...] for piece in pieces], axis=0).T


def turned_weight(weight, out):
    for n in columns(out.shape[0]):
        out[n, :] = weight[:, n].T


def hold_kernel(weight, kept, sems):
    step = weight.shape[0] // WEIGHT_CUTS
    copies = []
    for i in range(WEIGHT_CUTS):
        part = pl.ds(i * step, step)
        copies.append(pltpu.make_async_copy(weight.at[part], kept.at[part], sems.at[i]))
    for copy in copies:
        copy.start()
    for copy in copies:
        copy.wait()


def hold(weight):
    return pl.pallas_call(
        hold_kernel,
        in_specs=[pl.BlockSpec(memory_space=pltpu.HBM)],
        out_specs=pl.BlockSpec(memory_space=pltpu.VMEM),
        out_shape=pltpu.VMEM(weight.shape, BF),
        scratch_shapes=[pltpu.SemaphoreType.DMA((WEIGHT_CUTS,))],
        compiler_params=pltpu.CompilerParams(vmem_limit_bytes=2 << 20),
        cost_estimate=pl.CostEstimate(flops=0, bytes_accessed=4 * weight.size, transcendentals=0),
        name="hold",
    )(pltpu.with_memory_space_constraint(weight, pltpu.HBM))


def columns(width, step=256):
    step = min(width, step)
    return [slice(n, n + step) for n in range(0, width, step)]


def up_product_after(_, *refs):
    up_product(*refs)


def back_product_after(_, *refs):
    back_product(*refs)


def up_product(*refs):
    *pieces, weight, product, whole = refs
    whole[...] = jnp.concatenate([piece[...] for piece in pieces], axis=0)
    for n in columns(product.shape[1]):
        product[:, n] = matmul(whole[...], weight[:, n]).astype(BF)


def back_product(*refs):
    *ins, whole, product = refs
    up_product(*ins, product, whole)


def put_rows(pieces, n, product):
    rows = pieces[0].shape[0]
    for j, piece in enumerate(pieces):
        piece[:, n] = product[j * rows : (j + 1) * rows].astype(BF)


def down_product(mine, other, weight, act, *pieces):
    for n in columns(act.shape[1]):
        pre = mine[:, n].astype(F32) + other[:, n].astype(F32)
        act[:, n] = jax.nn.silu(pre).astype(BF)
    for n in columns(weight.shape[1]):
        put_rows(pieces, n, matmul(act[...], weight[:, n]))


def down_again(act, weight, *pieces):
    for n in columns(weight.shape[1]):
        put_rows(pieces, n, matmul(act[...], weight[:, n]))


def in_product(mine, other, pre_mine, pre_other, weight, grad_pre, *pieces):
    for n in columns(grad_pre.shape[1]):
        pre = pre_mine[:, n].astype(F32) + pre_other[:, n].astype(F32)
        grad = mine[:, n].astype(F32) + other[:, n].astype(F32)
        grad_pre[:, n] = (grad * silu_slope(pre)).astype(BF)
    for n in columns(weight.shape[1]):
        put_rows(pieces, n, matmul(grad_pre[...], weight[:, n]))


def act_only(mine, other, act):
    for n in columns(act.shape[1]):
        pre = mine[:, n].astype(F32) + other[:, n].astype(F32)
        act[:, n] = jax.nn.silu(pre).astype(BF)


def weight_grad(first, last, *refs):
    *blocks, out, left, right, room, sems = refs
    if first:
        blocks = blocks[:-1]
    count = len(blocks) // 2
    depth = blocks[-1].shape[0]
    for t in range(count):
        left[:, t * depth : (t + 1) * depth] = blocks[t][first:last, :]
        right[t * depth : (t + 1) * depth, :] = blocks[count + t][...]
    copies = []
    for i, m in enumerate(columns(last - first)):
        for n in columns(out.shape[1]):
            room[m, n] = matmul(left[m, :], right[:, n]).astype(BF)
        size = m.stop - m.start
        copies.append(
            pltpu.make_async_copy(room.at[pl.ds(m.start, size)], out.at[pl.ds(first + m.start, size)], sems.at[i])
        )
        copies[-1].start()
    for copy in copies:
        copy.wait()


def weight_product(lefts, rights, first, last, begun=None):
    rows, width, depth = lefts[0].shape[0], rights[0].shape[1], rights[0].shape[0] * len(rights)
    count = last - first
    return pl.pallas_call(
        functools.partial(weight_grad, first, last),
        in_specs=vmem(len(lefts) + len(rights)) + [pl.BlockSpec(memory_space=pl.ANY)] * (begun is not None),
        out_specs=pl.BlockSpec(memory_space=pl.ANY),
        out_shape=jax.ShapeDtypeStruct((rows, width), BF),
        scratch_shapes=[
            pltpu.VMEM((count, depth), BF),
            pltpu.VMEM((depth, width), BF),
            pltpu.VMEM((count, width), BF),
            pltpu.SemaphoreType.DMA((len(columns(count)),)),
        ],
        input_output_aliases={} if begun is None else {len(lefts) + len(rights): 0},
        compiler_params=pltpu.CompilerParams(vmem_limit_bytes=12 << 20),
        cost_estimate=pl.CostEstimate(
            flops=2 * count * width * depth, bytes_accessed=2 * count * width, transcendentals=0
        ),
        name="weight_grad",
    )(
        *[pltpu.with_memory_space_constraint(x, pltpu.VMEM) for x in (*lefts, *rights)],
        *([] if begun is None else [begun]),
    )


def other_cols(partial):
    size = lax.axis_size("col")
    if size == 2:
        return turn(partial, "col", 1)
    return (lax.psum(partial.astype(F32), "col") - partial.astype(F32)).astype(BF)


def silu_slope(value):
    sig = jax.nn.sigmoid(value)
    return sig * (1.0 + value * (1.0 - sig))


def matmul(a, b, dims=(((1,), (0,)), ((), ()))):
    return lax.dot_general(a, b, dims, preferred_element_type=F32)


def per_device(inputs, sample_ids, send_base, recv_base, w_up, w_down, cotangent):
    ticks = inputs.shape[1]
    rows = lax.axis_size("row")
    piece_rows, width = inputs.shape[2:]
    tokens, hidden = rows * piece_rows, w_up.shape[2]
    flops = 2 * tokens * width * hidden
    piece_like = jax.ShapeDtypeStruct((piece_rows, width), BF)
    whole_like = jax.ShapeDtypeStruct((tokens, width), BF)
    hidden_like = jax.ShapeDtypeStruct((tokens, hidden), BF)
    turned_like = jax.ShapeDtypeStruct((width, tokens), BF)
    turned_hidden = jax.ShapeDtypeStruct((hidden, tokens), BF)
    split_like = [hidden_like] + [piece_like] * rows
    room = [pltpu.VMEM((tokens, width), BF)]

    act_in, last_cot = first_pieces(inputs, cotangent)
    cot_pieces = [last_cot] + [None] * (rows - 1)
    in_pieces, acts, pres, seen_in, seen_out = [], [], [], [], []
    turned_ins, turned_acts = [], []
    for tick in range(ticks):
        if tick:
            (act_in,) = run(arrive, [piece_like], bases[tick - 1], *hand_over(sending))
            (j,) = beside(tick)
            cot_pieces[j] = swap_rows(after(cot_pieces[0], sending), j)
        pieces = gather_rows(act_in)
        if tick == 0:
            for j in beside(0):
                cot_pieces[j] = swap_rows(after(cot_pieces[0], act_in), j)
            stored, bases, cots, up_kept = fetch(
                after(sample_ids, act_in), inputs, send_base, recv_base, cotangent, w_up[0]
            )
            pieces = after(pieces, ([cot_pieces[j] for j in beside(0)], stored))
        if tick:
            (partial,) = run(
                up_product_after, [hidden_like], cot_pieces[j], *pieces, up_kept, flops=flops, scratch=room
            )
        else:
            (partial,) = run(up_product, [hidden_like], *pieces, up_kept, flops=flops, scratch=room)
            down_kept = hold(after(w_down[0], partial))
        other = other_cols(partial)
        if tick == ticks - 1:
            full_cot, first_grads = run(
                back_product, [whole_like, hidden_like], *after(cot_pieces, partial), down_turned, flops=flops
            )
        if tick < ticks - 1:
            act, *terms = run(down_product, split_like, partial, other, down_kept, flops=flops)
            acts.append(act)
            terms_in = scatter_rows(terms)
            if tick == 0:
                (down_turned,) = run(
                    turned_weight, [jax.ShapeDtypeStruct((width, hidden), BF)], after(down_kept, terms)
                )
                terms_in[0] = after(terms_in[0], down_turned)
            if tick == 1:
                (up_turned,) = run(turned_weight, [jax.ShapeDtypeStruct((hidden, width), BF)], after(up_kept, terms))
                turned_ins += run(turned, [turned_like], *after(in_pieces[0], terms))
                turned_acts += run(turned, [turned_hidden], after(acts[0], terms))
                terms_in[0] = after(terms_in[0], (up_turned, turned_ins, turned_acts))
            act_out, sending = run(leave, [piece_like] * 2, act_in, *terms_in, stored[tick])
            seen_out.append(act_out)
        in_pieces.append(pieces)
        pres.append((partial, other))
        seen_in.append(act_in)
    full_grads = [None] * ticks
    pre_grads = [None] * ticks
    seen_grad = [None] * ticks
    for step in range(ticks):
        tick = ticks - 1 - step
        if step == 0:
            grad_out, full_grad, partial = last_cot, full_cot, first_grads
        else:
            arrived = hand_over(sending)
            if step == 1:
                (act,) = run(act_only, [hidden_like], *after(pres[-1], sending))
                acts.append(act)
                out_pieces = run(down_again, [piece_like] * rows, act, down_kept, flops=flops)
                arrived = after(arrived, out_pieces)
                out_terms = list(out_pieces)
            (grad_out,) = run(arrive_back, [piece_like], cots[tick], *arrived)
            (j,) = beside(step)
            out_terms[j] = swap_rows(after(out_pieces[j], sending), j)
            pieces = gather_rows(grad_out)
            full_grad, partial = run(
                back_product_after, [whole_like, hidden_like], out_terms[j], *pieces, down_turned, flops=flops
            )
        other = other_cols(partial)
        if step == ticks - 1:
            full_grads[tick] = full_grad
            half_down = weight_product(turned_acts, full_grads, 0, hidden // 2)
            other = after(other, half_down)
        grad_pre, *terms = run(in_product, split_like, partial, other, *pres[tick], up_turned, flops=flops)
        terms_in = scatter_rows(terms)
        if step < ticks - 1:
            while len(turned_ins) < min(step + 2, ticks):
                turned_ins += run(turned, [turned_like], *after(in_pieces[len(turned_ins)], terms))
                turned_acts += run(turned, [turned_hidden], after(acts[len(turned_acts)], terms))
            terms_in[0] = after(terms_in[0], (turned_ins, turned_acts))
            (sending,) = run(leave_back, [piece_like], grad_out, *terms_in)
            seen_grad[tick] = sending
        full_grads[tick] = full_grad
        pre_grads[tick] = grad_pre
    for j in beside(0):
        out_terms[j] = swap_rows(after(out_pieces[j], terms), j)
    lefts = after((turned_ins, turned_acts), terms)
    grad_up = weight_product(lefts[0], pre_grads, 0, width)
    grad_down = weight_product(lefts[1], full_grads, hidden // 2, hidden, half_down)
    stack_like = jax.ShapeDtypeStruct((1, ticks, piece_rows, width), BF)
    terms_in[0] = after(terms_in[0], (grad_up, grad_down))
    section_input, section_output, input_grad = pl.pallas_call(
        finish,
        in_specs=vmem(2 + 2 * rows + 3 * ticks - 2),
        out_specs=vmem(3),
        out_shape=[stack_like] * 3,
        compiler_params=pltpu.CompilerParams(vmem_limit_bytes=6 << 20),
        name="finish",
    )(act_in, grad_out, *out_terms, *terms_in, *seen_out, *seen_grad[1:], *seen_in)
    return (
        section_input,
        section_output,
        input_grad,
        grad_up[None],
        grad_down[None],
    )


def solution(mesh):
    placed = (
        P("section", None, "row", "col"),
        P(),
        P("section", None, "row", "col"),
        P("section", None, "row", "col"),
        P("section", "col", "row"),
        P("section", "row", "col"),
        P("section", None, "row", "col"),
    )
    return jax.shard_map(
        per_device,
        mesh=mesh,
        in_specs=placed,
        out_specs=(
            P("section", None, "row", "col"),
            P("section", None, "row", "col"),
            P("section", None, "row", "col"),
            P("section", "col", "row"),
            P("section", "row", "col"),
        ),
        check_vma=False,
    )
```

```python
import functools

import jax
import jax.numpy as jnp
from jax import lax
from jax.experimental import pallas as pl
from jax.experimental.pallas import tpu as pltpu
from jax.sharding import PartitionSpec as P

BF = jnp.bfloat16
F32 = jnp.float32
WEIGHT_CUTS = 8


def hand_over(block, distance):
    sections = range(lax.axis_size("section"))
    return lax.ppermute(block, "section", [(i - distance, i) for i in sections if i - distance in sections])


def turn(block, axis, distance):
    size = lax.axis_size(axis)
    return lax.ppermute(block, axis, [(i, (i + distance) % size) for i in range(size)])


def partner(row, j, size):
    return row ^ ((size - j) % size) if size & (size - 1) == 0 else (j - row) % size


def swap_rows(block, j):
    size = lax.axis_size("row")
    return lax.ppermute(block, "row", [(i, partner(i, j, size)) for i in range(size)])


def gather_rows(block):
    return [swap_rows(block, j) if j else block for j in range(lax.axis_size("row"))]


def scatter_rows(pieces):
    return [swap_rows(piece, j) if j else piece for j, piece in enumerate(pieces)]


def beside(turn):
    size = lax.axis_size("row")
    return [[size - 1, size - 2], list(range(1, size - 2))][turn] if size > 2 else [[], [1]][turn]


def after(block, other):
    return lax.optimization_barrier((block, other))[0]


def vmem(count):
    return [pl.BlockSpec(memory_space=pltpu.VMEM)] * count


def run(kernel, outs, *ins, flops=0, scratch=(), name=None):
    ins = [pltpu.with_memory_space_constraint(block, pltpu.VMEM) for block in ins]
    size = sum(x.size * x.dtype.itemsize for x in [*ins, *outs])
    return pl.pallas_call(
        kernel,
        in_specs=vmem(len(ins)),
        out_specs=vmem(len(outs)),
        out_shape=[pltpu.VMEM(x.shape, x.dtype) for x in outs],
        scratch_shapes=scratch,
        compiler_params=pltpu.CompilerParams(vmem_limit_bytes=6 << 20),
        cost_estimate=pl.CostEstimate(flops=flops, bytes_accessed=size, transcendentals=0),
        name=name or kernel.__name__,
    )(*ins)


def first_kernel(inputs, cotangent, first, last, sems):
    copies = [
        pltpu.make_async_copy(inputs.at[0, 0], first, sems.at[0]),
        pltpu.make_async_copy(cotangent.at[0, cotangent.shape[1] - 1], last, sems.at[1]),
    ]
    for copy in copies:
        copy.start()
    for copy in copies:
        copy.wait()


def fetch_kernel(sample_ids, inputs, send_base, recv_base, cotangent, *refs):
    ticks = inputs.shape[1]
    count = ticks - 1
    weights, refs = refs[:1], refs[1:]
    stored, bases, cots = refs[:count], refs[count : 2 * count], refs[2 * count : 3 * count]
    *kept, fresh, sems, weight_sems = refs[3 * count :]
    section, sections = lax.axis_index("section"), lax.axis_size("section")
    samples = [sample_ids[tick - section + sections - 1] for tick in range(ticks)]
    copies = []
    for t in range(count):
        copies += [
            pltpu.make_async_copy(send_base.at[0, samples[t]], stored[t], sems.at[4 * t]),
            pltpu.make_async_copy(recv_base.at[0, samples[t + 1]], bases[t], sems.at[4 * t + 1]),
            pltpu.make_async_copy(inputs.at[0, t + 1], fresh.at[t], sems.at[4 * t + 2]),
            pltpu.make_async_copy(cotangent.at[0, t], cots[t], sems.at[4 * t + 3]),
        ]
    for k, (weight, room) in enumerate(zip(weights, kept)):
        step = weight.shape[0] // WEIGHT_CUTS
        for i in range(WEIGHT_CUTS):
            part = pl.ds(i * step, step)
            copies.append(pltpu.make_async_copy(weight.at[part], room.at[part], weight_sems.at[k, i]))
    for copy in copies:
        copy.start()
    for copy in copies:
        copy.wait()
    for t in range(count):
        bases[t][...] = jnp.where(section == 0, fresh[t], bases[t][...])
        cots[t][...] = jnp.where(section == sections - 1, cots[t][...], jnp.zeros_like(cots[t]))


def fetch(sample_ids, inputs, send_base, recv_base, cotangent, weight):
    count = inputs.shape[1] - 1
    piece = inputs.shape[2:]
    large = [pltpu.with_memory_space_constraint(x, pltpu.HBM) for x in (inputs, send_base, recv_base, cotangent, weight)]
    *outs, kept = pl.pallas_call(
        fetch_kernel,
        in_specs=[pl.BlockSpec(memory_space=pltpu.SMEM)] + [pl.BlockSpec(memory_space=pltpu.HBM)] * len(large),
        out_specs=vmem(3 * count + 1),
        out_shape=[pltpu.VMEM(piece, BF)] * (3 * count) + [pltpu.VMEM(weight.shape, BF)],
        scratch_shapes=[
            pltpu.VMEM((count, *piece), BF),
            pltpu.SemaphoreType.DMA((4 * count,)),
            pltpu.SemaphoreType.DMA((1, WEIGHT_CUTS)),
        ],
        compiler_params=pltpu.CompilerParams(vmem_limit_bytes=4 << 20),
        cost_estimate=pl.CostEstimate(flops=0, bytes_accessed=6 << 20, transcendentals=0),
        name="fetch",
    )(sample_ids, *large)
    return outs[:count], outs[count : 2 * count], outs[2 * count :], kept


def first_pieces(inputs, cotangent):
    piece = inputs.shape[2:]
    return pl.pallas_call(
        first_kernel,
        in_specs=[pl.BlockSpec(memory_space=pltpu.HBM)] * 2,
        out_specs=vmem(2),
        out_shape=[pltpu.VMEM(piece, BF)] * 2,
        scratch_shapes=[pltpu.SemaphoreType.DMA((2,))],
        compiler_params=pltpu.CompilerParams(vmem_limit_bytes=2 << 20),
        cost_estimate=pl.CostEstimate(flops=0, bytes_accessed=1 << 18, transcendentals=0),
        name="first",
    )(*[pltpu.with_memory_space_constraint(x, pltpu.HBM) for x in (inputs, cotangent)])


def added(first, terms):
    total = first[...].astype(F32)
    for term in terms:
        total = total + term[...].astype(F32)
    return total.astype(BF)


def arrive(base, arrived, out):
    out[...] = added(base, [arrived])


def leave(first, *refs):
    *terms, stored, out, delta = refs
    out[...] = added(first, terms)
    delta[...] = (out[...].astype(F32) - stored[...].astype(F32)).astype(BF)


def leave_back(first, *refs):
    *terms, out = refs
    out[...] = added(first, terms)


def finish(first_out, first_grad, *refs):
    *rest, ins, outs, grads = refs
    count = outs.shape[1] - 1
    terms, known = rest[: -3 * count - 1], rest[-3 * count - 1 :]
    half = len(terms) // 2
    outs[0, count] = added(first_out, terms[:half])
    grads[0, 0] = added(first_grad, terms[half:])
    for t in range(count):
        outs[0, t] = known[t][...]
        grads[0, t + 1] = known[count + t][...]
    for t in range(count + 1):
        ins[0, t] = known[2 * count + t][...]


def turned(*refs):
    *pieces, out = refs
    out[...] = jnp.concatenate([piece[...] for piece in pieces], axis=0).T


def turned_weight(weight, out):
    for n in columns(out.shape[0]):
        out[n, :] = weight[:, n].T


def hold_kernel(weight, kept, sems):
    step = weight.shape[0] // WEIGHT_CUTS
    copies = []
    for i in range(WEIGHT_CUTS):
        part = pl.ds(i * step, step)
        copies.append(pltpu.make_async_copy(weight.at[part], kept.at[part], sems.at[i]))
    for copy in copies:
        copy.start()
    for copy in copies:
        copy.wait()


def hold(weight):
    return pl.pallas_call(
        hold_kernel,
        in_specs=[pl.BlockSpec(memory_space=pltpu.HBM)],
        out_specs=pl.BlockSpec(memory_space=pltpu.VMEM),
        out_shape=pltpu.VMEM(weight.shape, BF),
        scratch_shapes=[pltpu.SemaphoreType.DMA((WEIGHT_CUTS,))],
        compiler_params=pltpu.CompilerParams(vmem_limit_bytes=2 << 20),
        cost_estimate=pl.CostEstimate(flops=0, bytes_accessed=4 * weight.size, transcendentals=0),
        name="hold",
    )(pltpu.with_memory_space_constraint(weight, pltpu.HBM))


def columns(width, step=256):
    step = min(width, step)
    return [slice(n, n + step) for n in range(0, width, step)]


def product_part(part, whole, weight, product):
    for n in columns(product.shape[1]):
        product[:, n] = matmul(whole[...], weight[:, n.start + part.start : n.stop + part.start]).astype(BF)


def stack_product(part, skip, *refs):
    *pieces, weight, whole, product = refs[skip:]
    whole[...] = jnp.concatenate([piece[...] for piece in pieces], axis=0)
    product_part(part, whole, weight, product)


def products(parts, pieces, weight, waited=()):
    tokens, width = len(pieces) * pieces[0].shape[0], weight.shape[0]
    whole_like = jax.ShapeDtypeStruct((tokens, width), BF)
    likes = [jax.ShapeDtypeStruct((tokens, part.stop - part.start), BF) for part in parts]
    flops = 2 * tokens * width * likes[0].shape[1]
    whole, first = run(
        functools.partial(stack_product, parts[0], len(waited)), [whole_like, likes[0]],
        *waited, *pieces, weight, flops=flops, name="stack_product",
    )
    rest = [
        run(functools.partial(product_part, part), [like], whole, weight, flops=flops, name="product_part")[0]
        for part, like in zip(parts[1:], likes[1:])
    ]
    return whole, [first, *rest]


def put_rows(pieces, n, product):
    rows = pieces[0].shape[0]
    for j, piece in enumerate(pieces):
        piece[:, n] = product[j * rows : (j + 1) * rows].astype(BF)


def silu_part(mine, other, act):
    for n in columns(act.shape[1]):
        pre = mine[:, n].astype(F32) + other[:, n].astype(F32)
        act[:, n] = jax.nn.silu(pre).astype(BF)


def slope_part(mine, other, pre_mine, pre_other, grad_pre):
    for n in columns(grad_pre.shape[1]):
        pre = pre_mine[:, n].astype(F32) + pre_other[:, n].astype(F32)
        grad = mine[:, n].astype(F32) + other[:, n].astype(F32)
        grad_pre[:, n] = (grad * silu_slope(pre)).astype(BF)


def first_part(pointwise, part, *refs):
    *ins, weight, hidden, total = refs
    pointwise(*ins, hidden)
    for n in columns(weight.shape[1]):
        total[:, n] = matmul(hidden[...], weight[part, n])


def last_part(pointwise, part, count, *refs):
    *ins, weight, total, hidden = refs[:-count]
    pointwise(*ins, hidden)
    for n in columns(weight.shape[1]):
        put_rows(refs[-count:], n, total[:, n] + matmul(hidden[...], weight[part, n]))


def through(pointwise, name, parts, ins, weight, piece_like, rows):
    tokens, width = rows * piece_like.shape[0], piece_like.shape[1]
    (first, last), done = parts, []
    flops = 2 * tokens * width * (first.stop - first.start)
    like = [jax.ShapeDtypeStruct((tokens, part.stop - part.start), BF) for part in parts]
    hidden, total = run(
        functools.partial(first_part, pointwise, first),
        [like[0], jax.ShapeDtypeStruct((tokens, width), F32)],
        *ins[0], weight, flops=flops, name=name,
    )
    rest, *pieces = run(
        functools.partial(last_part, pointwise, last, rows),
        [like[1]] + [piece_like] * rows,
        *ins[1], weight, total, flops=flops, name=name,
    )
    return [hidden, rest], pieces


def both_silu(*refs):
    *ins, first, last = refs
    silu_part(*ins[:2], first)
    silu_part(*ins[2:], last)


def down_again(parts, first, last, weight, *pieces):
    for n in columns(weight.shape[1]):
        total = matmul(first[...], weight[parts[0], n]) + matmul(last[...], weight[parts[1], n])
        put_rows(pieces, n, total)


def weight_grad(start, count, *refs):
    *blocks, out, left, right, room, sems = refs
    lefts, rights = blocks[:count], blocks[count:]
    if start:
        rights = rights[:-1]
    depth = rights[0].shape[0]
    for t in range(count):
        left[:, t * depth : (t + 1) * depth] = lefts[t][...]
        place = 0
        for block in rights[t * len(rights) // count : (t + 1) * len(rights) // count]:
            right[t * depth : (t + 1) * depth, place : place + block.shape[1]] = block[...]
            place += block.shape[1]
    copies = []
    for i, m in enumerate(columns(left.shape[0])):
        for n in columns(out.shape[1]):
            room[m, n] = matmul(left[m, :], right[:, n]).astype(BF)
        size = m.stop - m.start
        copies.append(
            pltpu.make_async_copy(room.at[pl.ds(m.start, size)], out.at[pl.ds(start + m.start, size)], sems.at[i])
        )
        copies[-1].start()
    for copy in copies:
        copy.wait()


def weight_product(lefts, rights, shape, start=0, begun=None):
    count, depth = lefts[0].shape[0], rights[0].shape[0] * len(lefts)
    ins = [*lefts, *rights]
    return pl.pallas_call(
        functools.partial(weight_grad, start, len(lefts)),
        in_specs=vmem(len(ins)) + [pl.BlockSpec(memory_space=pl.ANY)] * (begun is not None),
        out_specs=pl.BlockSpec(memory_space=pl.ANY),
        out_shape=jax.ShapeDtypeStruct(shape, BF),
        scratch_shapes=[
            pltpu.VMEM((count, depth), BF),
            pltpu.VMEM((depth, shape[1]), BF),
            pltpu.VMEM((count, shape[1]), BF),
            pltpu.SemaphoreType.DMA((len(columns(count)),)),
        ],
        input_output_aliases={} if begun is None else {len(ins): 0},
        compiler_params=pltpu.CompilerParams(vmem_limit_bytes=12 << 20),
        cost_estimate=pl.CostEstimate(
            flops=2 * count * shape[1] * depth, bytes_accessed=2 * count * shape[1], transcendentals=0
        ),
        name="weight_grad",
    )(
        *[pltpu.with_memory_space_constraint(x, pltpu.VMEM) for x in ins],
        *([] if begun is None else [begun]),
    )


def other_cols(partial):
    size = lax.axis_size("col")
    if size == 2:
        return turn(partial, "col", 1)
    return (lax.psum(partial.astype(F32), "col") - partial.astype(F32)).astype(BF)


def silu_slope(value):
    sig = jax.nn.sigmoid(value)
    return sig * (1.0 + value * (1.0 - sig))


def matmul(a, b, dims=(((1,), (0,)), ((), ()))):
    return lax.dot_general(a, b, dims, preferred_element_type=F32)


def per_device(inputs, sample_ids, send_base, recv_base, w_up, w_down, cotangent):
    ticks = inputs.shape[1]
    rows = lax.axis_size("row")
    piece_rows, width = inputs.shape[2:]
    tokens, hidden = rows * piece_rows, w_up.shape[2]
    parts = [slice(0, hidden // 2), slice(hidden // 2, hidden)]
    piece_like = jax.ShapeDtypeStruct((piece_rows, width), BF)
    part_like = jax.ShapeDtypeStruct((tokens, hidden // 2), BF)
    turned_like = jax.ShapeDtypeStruct((width, tokens), BF)
    turned_part = jax.ShapeDtypeStruct((hidden // 2, tokens), BF)

    def turn_blocks(tick, other):
        turned_ins.extend(run(turned, [turned_like], after(full_ins[tick], other)))
        for k in range(2):
            turned_acts[k].extend(run(turned, [turned_part], after(acts[tick][k], other)))

    act_in, last_cot = first_pieces(inputs, cotangent)
    cot_pieces = [last_cot] + [None] * (rows - 1)
    full_ins, acts, pres, seen_in, seen_out = [], [], [], [], []
    turned_ins, turned_acts = [], [[], []]
    for tick in range(ticks):
        waited = []
        if tick:
            act_in = run(arrive, [piece_like], bases[tick - 1], hand_over(sending, 1))[0]
            for j in beside(tick - 1):
                cot_pieces[j] = swap_rows(after(last_cot, sending), j)
                waited.append(cot_pieces[j])
        pieces = gather_rows(act_in)
        if tick == 0:
            stored, bases, cots, up_kept = fetch(
                after(sample_ids, act_in), inputs, send_base, recv_base, cotangent, w_up[0]
            )
            pieces = after(pieces, stored)
        full_in, partial = products(parts, pieces, up_kept, waited)
        if tick == 0:
            down_kept = hold(after(w_down[0], partial[-1]))
        pre = [(mine, other_cols(mine)) for mine in partial]
        if tick == ticks - 1:
            full_cot, first_grads = products(parts, after(cot_pieces, partial[-1]), down_turned)
        else:
            act, terms = through(silu_part, "down_part", parts, pre, down_kept, piece_like, rows)
            acts.append(act)
            terms_in = scatter_rows(terms)
            if tick == 0:
                (down_turned,) = run(
                    turned_weight, [jax.ShapeDtypeStruct((width, hidden), BF)], after(down_kept, terms)
                )
                terms_in[0] = after(terms_in[0], down_turned)
            if tick == 1:
                (up_turned,) = run(turned_weight, [jax.ShapeDtypeStruct((hidden, width), BF)], after(up_kept, terms))
                turn_blocks(0, terms)
                terms_in[0] = after(terms_in[0], (up_turned, turned_ins, turned_acts))
            act_out, sending = run(leave, [piece_like] * 2, act_in, *terms_in, stored[tick])
            seen_out.append(act_out)
        full_ins.append(full_in)
        pres.append(pre)
        seen_in.append(act_in)
    full_grads, pre_grads, seen_grad = [None] * ticks, [None] * ticks, [None] * ticks
    for step in range(ticks):
        tick = ticks - 1 - step
        if step == 0:
            grad_out, full_grad, partial = last_cot, full_cot, first_grads
        else:
            arrived = hand_over(sending, -1)
            if step == 1:
                acts.append(run(both_silu, [part_like] * 2, *after([*pres[-1][0], *pres[-1][1]], sending)))
                out_pieces = run(
                    functools.partial(down_again, parts), [piece_like] * rows, *acts[-1], down_kept,
                    flops=2 * tokens * width * hidden, name="down_again",
                )
                arrived = after(arrived, out_pieces)
                out_terms = list(out_pieces)
            (grad_out,) = run(arrive, [piece_like], cots[tick], arrived)
            waited = []
            for j in beside(step - 1):
                out_terms[j] = swap_rows(after(out_pieces[j], sending), j)
                waited.append(out_terms[j])
            full_grad, partial = products(parts, gather_rows(grad_out), down_turned, waited)
        full_grads[tick] = full_grad
        ins = [(mine, other_cols(mine), *known) for mine, known in zip(partial, pres[tick])]
        if step == ticks - 1:
            half_down = weight_product(turned_acts[0], full_grads, (hidden, width))
            ins[0] = after(ins[0], half_down)
        grad_pre, terms = through(slope_part, "in_part", parts, ins, up_turned, piece_like, rows)
        terms_in = scatter_rows(terms)
        if step < ticks - 1:
            turn_blocks(step + 1, terms)
            terms_in[0] = after(terms_in[0], (turned_ins, turned_acts))
            (sending,) = run(leave_back, [piece_like], grad_out, *terms_in)
            seen_grad[tick] = sending
        pre_grads[tick] = grad_pre
    turned_ins, last_acts = after((turned_ins, turned_acts[1]), terms)
    grad_up = weight_product(turned_ins, [part for grad_pre in pre_grads for part in grad_pre], (width, hidden))
    grad_down = weight_product(last_acts, full_grads, (hidden, width), hidden // 2, half_down)
    stack_like = jax.ShapeDtypeStruct((1, ticks, piece_rows, width), BF)
    terms_in[0] = after(terms_in[0], (grad_up, grad_down))
    section_input, section_output, input_grad = pl.pallas_call(
        finish,
        in_specs=vmem(2 + 2 * rows + 3 * ticks - 2),
        out_specs=vmem(3),
        out_shape=[stack_like] * 3,
        compiler_params=pltpu.CompilerParams(vmem_limit_bytes=6 << 20),
        name="finish",
    )(act_in, grad_out, *out_terms, *terms_in, *seen_out, *seen_grad[1:], *seen_in)
    return (
        section_input,
        section_output,
        input_grad,
        grad_up[None],
        grad_down[None],
    )


def solution(mesh):
    placed = (
        P("section", None, "row", "col"),
        P(),
        P("section", None, "row", "col"),
        P("section", None, "row", "col"),
        P("section", "col", "row"),
        P("section", "row", "col"),
        P("section", None, "row", "col"),
    )
    return jax.shard_map(
        per_device,
        mesh=mesh,
        in_specs=placed,
        out_specs=(
            P("section", None, "row", "col"),
            P("section", None, "row", "col"),
            P("section", None, "row", "col"),
            P("section", "col", "row"),
            P("section", "row", "col"),
        ),
        check_vma=False,
    )
```

```python
import functools

import jax
import jax.numpy as jnp
from jax import lax
from jax.experimental import pallas as pl
from jax.experimental.pallas import tpu as pltpu
from jax.sharding import PartitionSpec as P

BF = jnp.bfloat16
F32 = jnp.float32
WEIGHT_CUTS = 8


def hand_over(block, distance):
    sections = range(lax.axis_size("section"))
    return lax.ppermute(block, "section", [(i - distance, i) for i in sections if i - distance in sections])


def turn(block, axis, distance):
    size = lax.axis_size(axis)
    return lax.ppermute(block, axis, [(i, (i + distance) % size) for i in range(size)])


def partner(row, j, size):
    return row ^ ((size - j) % size) if size & (size - 1) == 0 else (j - row) % size


def swap_rows(block, j):
    size = lax.axis_size("row")
    return lax.ppermute(block, "row", [(i, partner(i, j, size)) for i in range(size)])


def gather_rows(block):
    return [swap_rows(block, j) if j else block for j in range(lax.axis_size("row"))]


def scatter_rows(pieces):
    return [swap_rows(piece, j) if j else piece for j, piece in enumerate(pieces)]


def beside(turn):
    size = lax.axis_size("row")
    return [[size - 1, size - 2], list(range(1, size - 2))][turn] if size > 2 else [[], [1]][turn]


def after(block, other):
    return lax.optimization_barrier((block, other))[0]


def vmem(count):
    return [pl.BlockSpec(memory_space=pltpu.VMEM)] * count


def run(kernel, outs, *ins, flops=0, scratch=(), name=None):
    ins = [pltpu.with_memory_space_constraint(block, pltpu.VMEM) for block in ins]
    size = sum(x.size * x.dtype.itemsize for x in [*ins, *outs])
    return pl.pallas_call(
        kernel,
        in_specs=vmem(len(ins)),
        out_specs=vmem(len(outs)),
        out_shape=[pltpu.VMEM(x.shape, x.dtype) for x in outs],
        scratch_shapes=scratch,
        compiler_params=pltpu.CompilerParams(vmem_limit_bytes=6 << 20),
        cost_estimate=pl.CostEstimate(flops=flops, bytes_accessed=size, transcendentals=0),
        name=name or kernel.__name__,
    )(*ins)


def first_kernel(inputs, cotangent, first, last, sems):
    copies = [
        pltpu.make_async_copy(inputs.at[0, 0], first, sems.at[0]),
        pltpu.make_async_copy(cotangent.at[0, cotangent.shape[1] - 1], last, sems.at[1]),
    ]
    for copy in copies:
        copy.start()
    for copy in copies:
        copy.wait()


def fetch_kernel(sample_ids, inputs, send_base, recv_base, cotangent, *refs):
    ticks = inputs.shape[1]
    count = ticks - 1
    stored, bases, cots = refs[:count], refs[count : 2 * count], refs[2 * count : 3 * count]
    fresh, sems = refs[3 * count :]
    section, sections = lax.axis_index("section"), lax.axis_size("section")
    samples = [sample_ids[tick - section + sections - 1] for tick in range(ticks)]
    copies = []
    for t in range(count):
        copies += [
            pltpu.make_async_copy(send_base.at[0, samples[t]], stored[t], sems.at[4 * t]),
            pltpu.make_async_copy(recv_base.at[0, samples[t + 1]], bases[t], sems.at[4 * t + 1]),
            pltpu.make_async_copy(inputs.at[0, t + 1], fresh.at[t], sems.at[4 * t + 2]),
            pltpu.make_async_copy(cotangent.at[0, t], cots[t], sems.at[4 * t + 3]),
        ]
    for copy in copies:
        copy.start()
    for copy in copies:
        copy.wait()
    for t in range(count):
        bases[t][...] = jnp.where(section == 0, fresh[t], bases[t][...])
        cots[t][...] = jnp.where(section == sections - 1, cots[t][...], jnp.zeros_like(cots[t]))


def fetch(sample_ids, inputs, send_base, recv_base, cotangent):
    count = inputs.shape[1] - 1
    piece = inputs.shape[2:]
    large = [pltpu.with_memory_space_constraint(x, pltpu.HBM) for x in (inputs, send_base, recv_base, cotangent)]
    outs = pl.pallas_call(
        fetch_kernel,
        in_specs=[pl.BlockSpec(memory_space=pltpu.SMEM)] + [pl.BlockSpec(memory_space=pltpu.HBM)] * len(large),
        out_specs=vmem(3 * count),
        out_shape=[pltpu.VMEM(piece, BF)] * (3 * count),
        scratch_shapes=[pltpu.VMEM((count, *piece), BF), pltpu.SemaphoreType.DMA((4 * count,))],
        compiler_params=pltpu.CompilerParams(vmem_limit_bytes=4 << 20),
        cost_estimate=pl.CostEstimate(flops=0, bytes_accessed=2 << 20, transcendentals=0),
        name="fetch",
    )(sample_ids, *large)
    return outs[:count], outs[count : 2 * count], outs[2 * count :]


def first_pieces(inputs, cotangent):
    piece = inputs.shape[2:]
    return pl.pallas_call(
        first_kernel,
        in_specs=[pl.BlockSpec(memory_space=pltpu.HBM)] * 2,
        out_specs=vmem(2),
        out_shape=[pltpu.VMEM(piece, BF)] * 2,
        scratch_shapes=[pltpu.SemaphoreType.DMA((2,))],
        compiler_params=pltpu.CompilerParams(vmem_limit_bytes=2 << 20),
        cost_estimate=pl.CostEstimate(flops=0, bytes_accessed=1 << 18, transcendentals=0),
        name="first",
    )(*[pltpu.with_memory_space_constraint(x, pltpu.HBM) for x in (inputs, cotangent)])


def added(first, terms):
    total = first[...].astype(F32)
    for term in terms:
        total = total + term[...].astype(F32)
    return total.astype(BF)


def arrive(base, arrived, out):
    out[...] = added(base, [arrived])


def leave(first, *refs):
    *terms, stored, out, delta = refs
    out[...] = added(first, terms)
    delta[...] = (out[...].astype(F32) - stored[...].astype(F32)).astype(BF)


def leave_back(first, *refs):
    *terms, out = refs
    out[...] = added(first, terms)


def finish_forward(count, *refs):
    *terms, ins, outs = refs
    entered, left, terms = terms[:count], terms[count : 2 * count - 1], terms[2 * count - 1 :]
    for t in range(count):
        ins[0, t] = entered[t][...]
    for t in range(count - 1):
        outs[0, t] = left[t][...]
    outs[0, count - 1] = added(entered[-1], terms)


def finish(first, *refs):
    *rest, grads = refs
    count = grads.shape[1] - 1
    grads[0, 0] = added(first, rest[:-count])
    for t in range(count):
        grads[0, t + 1] = rest[t - count][...]


def stacked(kernel, count, ins, like, name):
    return pl.pallas_call(
        kernel,
        in_specs=vmem(len(ins)),
        out_specs=vmem(count),
        out_shape=[like] * count,
        compiler_params=pltpu.CompilerParams(vmem_limit_bytes=6 << 20),
        cost_estimate=pl.CostEstimate(flops=0, bytes_accessed=1 << 20, transcendentals=0),
        name=name,
    )(*[pltpu.with_memory_space_constraint(x, pltpu.VMEM) for x in ins])


def turned(*refs):
    *pieces, out = refs
    out[...] = jnp.concatenate([piece[...] for piece in pieces], axis=0).T


def turned_weight(weight, out):
    for n in columns(out.shape[0]):
        out[n, :] = weight[:, n].T


def hold_kernel(*refs):
    *refs, sems = refs
    count = len(refs) // 2
    copies = []
    for k in range(count):
        step = refs[k].shape[0] // WEIGHT_CUTS
        for i in range(WEIGHT_CUTS):
            part = pl.ds(i * step, step)
            copies.append(pltpu.make_async_copy(refs[k].at[part], refs[count + k].at[part], sems.at[k, i]))
    for copy in copies:
        copy.start()
    for copy in copies:
        copy.wait()


def hold(weights):
    return pl.pallas_call(
        hold_kernel,
        in_specs=[pl.BlockSpec(memory_space=pltpu.HBM)] * len(weights),
        out_specs=vmem(len(weights)),
        out_shape=[pltpu.VMEM(weight.shape, BF) for weight in weights],
        scratch_shapes=[pltpu.SemaphoreType.DMA((len(weights), WEIGHT_CUTS))],
        compiler_params=pltpu.CompilerParams(vmem_limit_bytes=2 << 20),
        cost_estimate=pl.CostEstimate(flops=0, bytes_accessed=16 << 20, transcendentals=0),
        name="hold",
    )(*[pltpu.with_memory_space_constraint(weight, pltpu.HBM) for weight in weights])


def columns(width, step=256):
    step = min(width, step)
    return [slice(n, n + step) for n in range(0, width, step)]


def product_part(part, whole, weight, product):
    for n in columns(product.shape[1]):
        product[:, n] = matmul(whole[...], weight[:, n.start + part.start : n.stop + part.start]).astype(BF)


def stack_product(part, skip, *refs):
    *pieces, weight, whole, product = refs[skip:]
    whole[...] = jnp.concatenate([piece[...] for piece in pieces], axis=0)
    product_part(part, whole, weight, product)


def products(parts, pieces, weight, waited=()):
    tokens, width = len(pieces) * pieces[0].shape[0], weight.shape[0]
    whole_like = jax.ShapeDtypeStruct((tokens, width), BF)
    likes = [jax.ShapeDtypeStruct((tokens, part.stop - part.start), BF) for part in parts]
    flops = 2 * tokens * width * likes[0].shape[1]
    whole, first = run(
        functools.partial(stack_product, parts[0], len(waited)), [whole_like, likes[0]],
        *waited, *pieces, weight, flops=flops, name="stack_product",
    )
    rest = [
        run(functools.partial(product_part, part), [like], whole, weight, flops=flops, name="product_part")[0]
        for part, like in zip(parts[1:], likes[1:])
    ]
    return whole, [first, *rest]


def put_rows(pieces, n, product):
    rows = pieces[0].shape[0]
    for j, piece in enumerate(pieces):
        piece[:, n] = product[j * rows : (j + 1) * rows].astype(BF)


def silu_part(mine, other, act):
    for n in columns(act.shape[1]):
        pre = mine[:, n].astype(F32) + other[:, n].astype(F32)
        act[:, n] = jax.nn.silu(pre).astype(BF)


def slope_part(mine, other, pre_mine, pre_other, grad_pre):
    for n in columns(grad_pre.shape[1]):
        pre = pre_mine[:, n].astype(F32) + pre_other[:, n].astype(F32)
        grad = mine[:, n].astype(F32) + other[:, n].astype(F32)
        grad_pre[:, n] = (grad * silu_slope(pre)).astype(BF)


def first_part(pointwise, part, *refs):
    *ins, weight, hidden, total = refs
    pointwise(*ins, hidden)
    for n in columns(weight.shape[1]):
        total[:, n] = matmul(hidden[...], weight[part, n])


def last_part(pointwise, part, count, *refs):
    *ins, weight, total, hidden = refs[:-count]
    pointwise(*ins, hidden)
    for n in columns(weight.shape[1]):
        put_rows(refs[-count:], n, total[:, n] + matmul(hidden[...], weight[part, n]))


def through(pointwise, name, parts, ins, weight, piece_like, rows):
    tokens, width = rows * piece_like.shape[0], piece_like.shape[1]
    (first, last), done = parts, []
    flops = 2 * tokens * width * (first.stop - first.start)
    like = [jax.ShapeDtypeStruct((tokens, part.stop - part.start), BF) for part in parts]
    hidden, total = run(
        functools.partial(first_part, pointwise, first),
        [like[0], jax.ShapeDtypeStruct((tokens, width), F32)],
        *ins[0], weight, flops=flops, name=name,
    )
    rest, *pieces = run(
        functools.partial(last_part, pointwise, last, rows),
        [like[1]] + [piece_like] * rows,
        *ins[1], weight, total, flops=flops, name=name,
    )
    return [hidden, rest], pieces


def both_silu(*refs):
    *ins, first, last = refs
    silu_part(*ins[:2], first)
    silu_part(*ins[2:], last)


def down_again(parts, first, last, weight, *pieces):
    for n in columns(weight.shape[1]):
        total = matmul(first[...], weight[parts[0], n]) + matmul(last[...], weight[parts[1], n])
        put_rows(pieces, n, total)


def weight_grad(start, lefts, rights, out, left, right, room, sems):
    count, depth = len(lefts), rights[0].shape[0]
    for t in range(count):
        left[:, t * depth : (t + 1) * depth] = lefts[t][...]
        place = 0
        for block in rights[t * len(rights) // count : (t + 1) * len(rights) // count]:
            right[t * depth : (t + 1) * depth, place : place + block.shape[1]] = block[...]
            place += block.shape[1]
    copies = []
    for i, m in enumerate(columns(left.shape[0])):
        for n in columns(out.shape[1]):
            room[m, n] = matmul(left[m, :], right[:, n]).astype(BF)
        size = m.stop - m.start
        copies.append(
            pltpu.make_async_copy(room.at[pl.ds(m.start, size)], out.at[pl.ds(start + m.start, size)], sems.at[i])
        )
        copies[-1].start()
    return copies


def weight_grads(cuts, begun, *refs):
    ins, refs = refs[: sum(left + right for _, left, right in cuts)], refs[sum(left + right for _, left, right in cuts) + begun :]
    outs, rooms = refs[: len(cuts)], refs[len(cuts) :]
    copies, place = [], 0
    for k, (start, left, right) in enumerate(cuts):
        lefts, rights = ins[place : place + left], ins[place + left : place + left + right]
        copies += weight_grad(start, lefts, rights, outs[k], *rooms[4 * k : 4 * k + 4])
        place += left + right
    for copy in copies:
        copy.wait()


def weight_products(jobs, begun=None):
    cuts, ins, scratch = [], [], []
    flops = size = 0
    for lefts, rights, shape, start in jobs:
        count, depth = lefts[0].shape[0], rights[0].shape[0] * len(lefts)
        cuts.append((start, len(lefts), len(rights)))
        ins += [*lefts, *rights]
        scratch += [
            pltpu.VMEM((count, depth), BF),
            pltpu.VMEM((depth, shape[1]), BF),
            pltpu.VMEM((count, shape[1]), BF),
            pltpu.SemaphoreType.DMA((len(columns(count)),)),
        ]
        flops += 2 * count * shape[1] * depth
        size += 2 * count * shape[1]
    return pl.pallas_call(
        functools.partial(weight_grads, tuple(cuts), begun is not None),
        in_specs=vmem(len(ins)) + [pl.BlockSpec(memory_space=pl.ANY)] * (begun is not None),
        out_specs=[pl.BlockSpec(memory_space=pl.ANY)] * len(jobs),
        out_shape=[jax.ShapeDtypeStruct(shape, BF) for _, _, shape, _ in jobs],
        scratch_shapes=scratch,
        input_output_aliases={} if begun is None else {len(ins): len(jobs) - 1},
        compiler_params=pltpu.CompilerParams(vmem_limit_bytes=18 << 20),
        cost_estimate=pl.CostEstimate(flops=flops, bytes_accessed=size, transcendentals=0),
        name="weight_grads",
    )(
        *[pltpu.with_memory_space_constraint(x, pltpu.VMEM) for x in ins],
        *([] if begun is None else [begun]),
    )


def other_cols(partial):
    size = lax.axis_size("col")
    if size == 2:
        return turn(partial, "col", 1)
    return (lax.psum(partial.astype(F32), "col") - partial.astype(F32)).astype(BF)


def silu_slope(value):
    sig = jax.nn.sigmoid(value)
    return sig * (1.0 + value * (1.0 - sig))


def matmul(a, b, dims=(((1,), (0,)), ((), ()))):
    return lax.dot_general(a, b, dims, preferred_element_type=F32)


def per_device(inputs, sample_ids, send_base, recv_base, w_up, w_down, cotangent):
    ticks = inputs.shape[1]
    rows = lax.axis_size("row")
    piece_rows, width = inputs.shape[2:]
    tokens, hidden = rows * piece_rows, w_up.shape[2]
    stack_like = jax.ShapeDtypeStruct((1, ticks, piece_rows, width), BF)
    parts = [slice(0, hidden // 2), slice(hidden // 2, hidden)]
    piece_like = jax.ShapeDtypeStruct((piece_rows, width), BF)
    part_like = jax.ShapeDtypeStruct((tokens, hidden // 2), BF)
    turned_like = jax.ShapeDtypeStruct((width, tokens), BF)
    turned_part = jax.ShapeDtypeStruct((hidden // 2, tokens), BF)

    def turn_blocks(tick, other):
        turned_ins.extend(run(turned, [turned_like], after(full_ins[tick], other)))
        for k in range(2):
            turned_acts[k].extend(run(turned, [turned_part], after(acts[tick][k], other)))

    act_in, last_cot = first_pieces(inputs, cotangent)
    cot_pieces = [last_cot] + [None] * (rows - 1)
    full_ins, acts, pres, seen_in, seen_out = [], [], [], [], []
    turned_ins, turned_acts = [], [[], []]
    for tick in range(ticks):
        waited = []
        if tick:
            act_in = run(arrive, [piece_like], bases[tick - 1], hand_over(sending, 1))[0]
            for j in beside(tick - 1):
                cot_pieces[j] = swap_rows(after(last_cot, sending), j)
                waited.append(cot_pieces[j])
        pieces = gather_rows(act_in)
        if tick == 0:
            up_kept, down_kept = hold(after([w_up[0], w_down[0]], act_in))
            pieces = after(pieces, up_kept)
        if tick == ticks - 1:
            full_cot, first_grads = products(parts, cot_pieces, down_turned)
            pieces, waited = after(pieces, first_grads), []
        full_in, partial = products(parts, pieces, up_kept, waited)
        pre = [(mine, other_cols(mine)) for mine in partial]
        if tick < ticks - 1:
            act, terms = through(silu_part, "down_part", parts, pre, down_kept, piece_like, rows)
            acts.append(act)
            terms_in = scatter_rows(terms)
            if tick == 0:
                (down_turned,) = run(
                    turned_weight, [jax.ShapeDtypeStruct((width, hidden), BF)], after(down_kept, terms)
                )
                stored, bases, cots = fetch(after(sample_ids, terms), inputs, send_base, recv_base, cotangent)
                terms_in[0] = after(terms_in[0], (down_turned, stored))
            if tick == 1:
                (up_turned,) = run(turned_weight, [jax.ShapeDtypeStruct((hidden, width), BF)], after(up_kept, terms))
                turn_blocks(0, terms)
                terms_in[0] = after(terms_in[0], (up_turned, turned_ins, turned_acts))
            act_out, sending = run(leave, [piece_like] * 2, act_in, *terms_in, stored[tick])
            seen_out.append(act_out)
        full_ins.append(full_in)
        pres.append(pre)
        seen_in.append(act_in)
    full_grads, pre_grads, seen_grad = [None] * ticks, [None] * ticks, [None] * ticks
    for step in range(ticks):
        tick = ticks - 1 - step
        if step == 0:
            grad_out, full_grad, partial = last_cot, full_cot, first_grads
        else:
            arrived = hand_over(sending, -1)
            if step == 1:
                acts.append(run(both_silu, [part_like] * 2, *after([*pres[-1][0], *pres[-1][1]], sending)))
                out_pieces = run(
                    functools.partial(down_again, parts), [piece_like] * rows, *acts[-1], down_kept,
                    flops=2 * tokens * width * hidden, name="down_again",
                )
                arrived = after(arrived, out_pieces)
                out_terms = list(out_pieces)
            (grad_out,) = run(arrive, [piece_like], cots[tick], arrived)
            waited = []
            for j in beside(step - 1):
                out_terms[j] = swap_rows(after(out_pieces[j], sending), j)
                waited.append(out_terms[j])
            pieces = gather_rows(grad_out)
            if step == ticks - 1:
                section_input, section_output = stacked(
                    functools.partial(finish_forward, ticks), 2, [*seen_in, *seen_out, *out_terms], stack_like,
                    "finish_forward",
                )
                pieces, waited = after(pieces, section_output), []
            full_grad, partial = products(parts, pieces, down_turned, waited)
        full_grads[tick] = full_grad
        ins = [(mine, other_cols(mine), *known) for mine, known in zip(partial, pres[tick])]
        if step == ticks - 1:
            (half_down,) = weight_products([(turned_acts[0], full_grads, (hidden, width), 0)])
            ins[0] = after(ins[0], half_down)
        grad_pre, terms = through(slope_part, "in_part", parts, ins, up_turned, piece_like, rows)
        terms_in = scatter_rows(terms)
        if step < ticks - 1:
            turn_blocks(step + 1, terms)
            terms_in[0] = after(terms_in[0], (turned_ins, turned_acts))
            (sending,) = run(leave_back, [piece_like], grad_out, *terms_in)
            seen_grad[tick] = sending
        pre_grads[tick] = grad_pre
    turned_ins, last_acts = after((turned_ins, turned_acts[1]), terms)
    grad_up, grad_down = weight_products(
        [
            (turned_ins, [part for grad_pre in pre_grads for part in grad_pre], (width, hidden), 0),
            (last_acts, full_grads, (hidden, width), hidden // 2),
        ],
        half_down,
    )
    terms_in[0] = after(terms_in[0], (grad_up, grad_down))
    (input_grad,) = stacked(finish, 1, [grad_out, *terms_in, *seen_grad[1:]], stack_like, "finish")
    return (
        section_input,
        section_output,
        input_grad,
        grad_up[None],
        grad_down[None],
    )


def solution(mesh):
    placed = (
        P("section", None, "row", "col"),
        P(),
        P("section", None, "row", "col"),
        P("section", None, "row", "col"),
        P("section", "col", "row"),
        P("section", "row", "col"),
        P("section", None, "row", "col"),
    )
    return jax.shard_map(
        per_device,
        mesh=mesh,
        in_specs=placed,
        out_specs=(
            P("section", None, "row", "col"),
            P("section", None, "row", "col"),
            P("section", None, "row", "col"),
            P("section", "col", "row"),
            P("section", "row", "col"),
        ),
        check_vma=False,
    )
```

```python
import functools

import jax
import jax.numpy as jnp
from jax import lax
from jax.experimental import pallas as pl
from jax.experimental.pallas import tpu as pltpu
from jax.sharding import PartitionSpec as P

BF = jnp.bfloat16
F32 = jnp.float32
WEIGHT_CUTS = 8


def hand_over(block, distance):
    sections = range(lax.axis_size("section"))
    return lax.ppermute(block, "section", [(i - distance, i) for i in sections if i - distance in sections])


def turn(block, axis, distance):
    size = lax.axis_size(axis)
    return lax.ppermute(block, axis, [(i, (i + distance) % size) for i in range(size)])


def partner(row, j, size):
    return row ^ j if size & (size - 1) == 0 else (j - row) % size


def swap_rows(block, j):
    size = lax.axis_size("row")
    return lax.ppermute(block, "row", [(i, partner(i, j, size)) for i in range(size)])


def gather_rows(block):
    return [swap_rows(block, j) if j else block for j in range(lax.axis_size("row"))]


def scatter_rows(pieces):
    return [swap_rows(piece, j) if j else piece for j, piece in enumerate(pieces)]


def beside(turn):
    size = lax.axis_size("row")
    return [list(range(1, size - 1)), [size - 1]][turn] if size > 2 else [[], [1]][turn]


def halves(pieces):
    return pieces[: len(pieces) // 2], pieces[len(pieces) // 2 :]


def after(block, other):
    return lax.optimization_barrier((block, other))[0]


def vmem(count):
    return [pl.BlockSpec(memory_space=pltpu.VMEM)] * count


def run(kernel, outs, *ins, flops=0, scratch=(), name=None):
    ins = [pltpu.with_memory_space_constraint(block, pltpu.VMEM) for block in ins]
    size = sum(x.size * x.dtype.itemsize for x in [*ins, *outs])
    return pl.pallas_call(
        kernel,
        in_specs=vmem(len(ins)),
        out_specs=vmem(len(outs)),
        out_shape=[pltpu.VMEM(x.shape, x.dtype) for x in outs],
        scratch_shapes=scratch,
        compiler_params=pltpu.CompilerParams(vmem_limit_bytes=6 << 20),
        cost_estimate=pl.CostEstimate(flops=flops, bytes_accessed=size, transcendentals=0),
        name=name or kernel.__name__,
    )(*ins)


def first_kernel(inputs, cotangent, first, last, sems):
    copies = [
        pltpu.make_async_copy(inputs.at[0, 0], first, sems.at[0]),
        pltpu.make_async_copy(cotangent.at[0, cotangent.shape[1] - 1], last, sems.at[1]),
    ]
    for copy in copies:
        copy.start()
    for copy in copies:
        copy.wait()


def fetch_kernel(sample_ids, inputs, send_base, recv_base, cotangent, *refs):
    ticks = inputs.shape[1]
    count = ticks - 1
    stored, bases, cots = refs[:count], refs[count : 2 * count], refs[2 * count : 3 * count]
    fresh, sems = refs[3 * count :]
    section, sections = lax.axis_index("section"), lax.axis_size("section")
    samples = [sample_ids[tick - section + sections - 1] for tick in range(ticks)]
    copies = []
    for t in range(count):
        copies += [
            pltpu.make_async_copy(send_base.at[0, samples[t]], stored[t], sems.at[4 * t]),
            pltpu.make_async_copy(recv_base.at[0, samples[t + 1]], bases[t], sems.at[4 * t + 1]),
            pltpu.make_async_copy(inputs.at[0, t + 1], fresh.at[t], sems.at[4 * t + 2]),
            pltpu.make_async_copy(cotangent.at[0, t], cots[t], sems.at[4 * t + 3]),
        ]
    for copy in copies:
        copy.start()
    for copy in copies:
        copy.wait()
    for t in range(count):
        bases[t][...] = jnp.where(section == 0, fresh[t], bases[t][...])
        cots[t][...] = jnp.where(section == sections - 1, cots[t][...], jnp.zeros_like(cots[t]))


def fetch(sample_ids, inputs, send_base, recv_base, cotangent):
    count = inputs.shape[1] - 1
    piece = inputs.shape[2:]
    large = [pltpu.with_memory_space_constraint(x, pltpu.HBM) for x in (inputs, send_base, recv_base, cotangent)]
    outs = pl.pallas_call(
        fetch_kernel,
        in_specs=[pl.BlockSpec(memory_space=pltpu.SMEM)] + [pl.BlockSpec(memory_space=pltpu.HBM)] * len(large),
        out_specs=vmem(3 * count),
        out_shape=[pltpu.VMEM(piece, BF)] * (3 * count),
        scratch_shapes=[pltpu.VMEM((count, *piece), BF), pltpu.SemaphoreType.DMA((4 * count,))],
        compiler_params=pltpu.CompilerParams(vmem_limit_bytes=4 << 20),
        cost_estimate=pl.CostEstimate(flops=0, bytes_accessed=2 << 20, transcendentals=0),
        name="fetch",
    )(sample_ids, *large)
    return outs[:count], outs[count : 2 * count], outs[2 * count :]


def first_pieces(inputs, cotangent):
    piece = inputs.shape[2:]
    return pl.pallas_call(
        first_kernel,
        in_specs=[pl.BlockSpec(memory_space=pltpu.HBM)] * 2,
        out_specs=vmem(2),
        out_shape=[pltpu.VMEM(piece, BF)] * 2,
        scratch_shapes=[pltpu.SemaphoreType.DMA((2,))],
        compiler_params=pltpu.CompilerParams(vmem_limit_bytes=2 << 20),
        cost_estimate=pl.CostEstimate(flops=0, bytes_accessed=1 << 18, transcendentals=0),
        name="first",
    )(*[pltpu.with_memory_space_constraint(x, pltpu.HBM) for x in (inputs, cotangent)])


def added(first, terms):
    total = first[...].astype(F32)
    for term in terms:
        total = total + term[...].astype(F32)
    return total.astype(BF)


def arrive(base, arrived, out):
    out[...] = added(base, [arrived])


def leave(first, *refs):
    *terms, stored, out, delta = refs
    out[...] = added(first, terms)
    delta[...] = (out[...].astype(F32) - stored[...].astype(F32)).astype(BF)


def leave_back(first, *refs):
    *terms, out = refs
    out[...] = added(first, terms)


def finish_forward(count, *refs):
    *terms, ins, outs = refs
    entered, left, terms = terms[:count], terms[count : 2 * count - 1], terms[2 * count - 1 :]
    for t in range(count):
        ins[0, t] = entered[t][...]
    for t in range(count - 1):
        outs[0, t] = left[t][...]
    outs[0, count - 1] = added(entered[-1], terms)


def finish(first, *refs):
    *rest, grads = refs
    count = grads.shape[1] - 1
    grads[0, 0] = added(first, rest[:-count])
    for t in range(count):
        grads[0, t + 1] = rest[t - count][...]


def stacked(kernel, count, ins, like, name):
    return pl.pallas_call(
        kernel,
        in_specs=vmem(len(ins)),
        out_specs=vmem(count),
        out_shape=[like] * count,
        compiler_params=pltpu.CompilerParams(vmem_limit_bytes=6 << 20),
        cost_estimate=pl.CostEstimate(flops=0, bytes_accessed=1 << 20, transcendentals=0),
        name=name,
    )(*[pltpu.with_memory_space_constraint(x, pltpu.VMEM) for x in ins])


def turned(*refs):
    *pieces, out = refs
    out[...] = jnp.concatenate([piece[...] for piece in pieces], axis=0).T


def turned_weight(weight, out):
    for n in columns(out.shape[0]):
        out[n, :] = weight[:, n].T


def hold_kernel(*refs):
    *refs, sems = refs
    count = len(refs) // 2
    copies = []
    for k in range(count):
        step = refs[k].shape[0] // WEIGHT_CUTS
        for i in range(WEIGHT_CUTS):
            part = pl.ds(i * step, step)
            copies.append(pltpu.make_async_copy(refs[k].at[part], refs[count + k].at[part], sems.at[k, i]))
    for copy in copies:
        copy.start()
    for copy in copies:
        copy.wait()


def hold(weights):
    return pl.pallas_call(
        hold_kernel,
        in_specs=[pl.BlockSpec(memory_space=pltpu.HBM)] * len(weights),
        out_specs=vmem(len(weights)),
        out_shape=[pltpu.VMEM(weight.shape, BF) for weight in weights],
        scratch_shapes=[pltpu.SemaphoreType.DMA((len(weights), WEIGHT_CUTS))],
        compiler_params=pltpu.CompilerParams(vmem_limit_bytes=2 << 20),
        cost_estimate=pl.CostEstimate(flops=0, bytes_accessed=16 << 20, transcendentals=0),
        name="hold",
    )(*[pltpu.with_memory_space_constraint(weight, pltpu.HBM) for weight in weights])


def columns(width, step=256):
    step = min(width, step)
    return [slice(n, n + step) for n in range(0, width, step)]


def stack_product(skip, *refs):
    *pieces, weight, whole, product = refs[skip:]
    whole[...] = jnp.concatenate([piece[...] for piece in pieces], axis=0)
    for n in columns(product.shape[1]):
        product[:, n] = matmul(whole[...], weight[:, n]).astype(BF)


def stack_times(pieces, weight, waited=()):
    tokens = len(pieces) * pieces[0].shape[0]
    return run(
        functools.partial(stack_product, len(waited)),
        [jax.ShapeDtypeStruct((tokens, count), BF) for count in weight.shape],
        *waited, *pieces, weight,
        flops=2 * tokens * weight.size, name="stack_product",
    )


def put_rows(pieces, n, product):
    rows = pieces[0].shape[0]
    for j, piece in enumerate(pieces):
        piece[:, n] = product[j * rows : (j + 1) * rows].astype(BF)


def silu_part(mine, other, act):
    for n in columns(act.shape[1]):
        pre = mine[:, n].astype(F32) + other[:, n].astype(F32)
        act[:, n] = jax.nn.silu(pre).astype(BF)


def slope_part(mine, other, pre_mine, pre_other, grad_pre):
    for n in columns(grad_pre.shape[1]):
        pre = pre_mine[:, n].astype(F32) + pre_other[:, n].astype(F32)
        grad = mine[:, n].astype(F32) + other[:, n].astype(F32)
        grad_pre[:, n] = (grad * silu_slope(pre)).astype(BF)


def hidden_product(pointwise, count, *refs):
    *ins, weight, hidden = refs[:-count]
    pointwise(*ins, hidden)
    for n in columns(weight.shape[1]):
        put_rows(refs[-count:], n, matmul(hidden[...], weight[:, n]))


def through(pointwise, name, ins, weight, piece_like):
    hiddens, pieces = [], []
    for half in ins:
        tokens = half[0].shape[0]
        count = tokens // piece_like.shape[0]
        hidden, *done = run(
            functools.partial(hidden_product, pointwise, count),
            [jax.ShapeDtypeStruct((tokens, weight.shape[0]), BF)] + [piece_like] * count,
            *half, weight, flops=2 * tokens * weight.size, name=name,
        )
        hiddens.append(hidden)
        pieces += done
    return hiddens, pieces


def both_silu(*refs):
    *ins, first, last = refs
    silu_part(*ins[:2], first)
    silu_part(*ins[2:], last)


def down_again(first, last, weight, *pieces):
    for n in columns(weight.shape[1]):
        for hidden, half in zip((first, last), halves(pieces)):
            put_rows(half, n, matmul(hidden[...], weight[:, n]))


def weight_grad(start, lefts, rights, out, left, right, room, sems):
    depth = lefts[0].shape[1]
    for t, block in enumerate(lefts):
        left[:, t * depth : (t + 1) * depth] = block[start : start + left.shape[0], :]
    place = 0
    for block in rights:
        right[place : place + block.shape[0], :] = block[...]
        place += block.shape[0]
    copies = []
    for i, m in enumerate(columns(left.shape[0])):
        for n in columns(out.shape[1]):
            room[m, n] = matmul(left[m, :], right[:, n]).astype(BF)
        size = m.stop - m.start
        copies.append(
            pltpu.make_async_copy(room.at[pl.ds(m.start, size)], out.at[pl.ds(start + m.start, size)], sems.at[i])
        )
        copies[-1].start()
    return copies


def weight_grads(cuts, begun, *refs):
    ins, refs = refs[: sum(left + right for _, left, right in cuts)], refs[sum(left + right for _, left, right in cuts) + begun :]
    outs, rooms = refs[: len(cuts)], refs[len(cuts) :]
    copies, place = [], 0
    for k, (start, left, right) in enumerate(cuts):
        lefts, rights = ins[place : place + left], ins[place + left : place + left + right]
        copies += weight_grad(start, lefts, rights, outs[k], *rooms[4 * k : 4 * k + 4])
        place += left + right
    for copy in copies:
        copy.wait()


def weight_products(jobs, begun=None):
    cuts, ins, scratch = [], [], []
    flops = size = 0
    for lefts, rights, shape, start, end in jobs:
        count, depth = end - start, lefts[0].shape[1] * len(lefts)
        cuts.append((start, len(lefts), len(rights)))
        ins += [*lefts, *rights]
        scratch += [
            pltpu.VMEM((count, depth), BF),
            pltpu.VMEM((depth, shape[1]), BF),
            pltpu.VMEM((count, shape[1]), BF),
            pltpu.SemaphoreType.DMA((len(columns(count)),)),
        ]
        flops += 2 * count * shape[1] * depth
        size += 2 * count * shape[1]
    return pl.pallas_call(
        functools.partial(weight_grads, tuple(cuts), begun is not None),
        in_specs=vmem(len(ins)) + [pl.BlockSpec(memory_space=pl.ANY)] * (begun is not None),
        out_specs=[pl.BlockSpec(memory_space=pl.ANY)] * len(jobs),
        out_shape=[jax.ShapeDtypeStruct(shape, BF) for _, _, shape, _, _ in jobs],
        scratch_shapes=scratch,
        input_output_aliases={} if begun is None else {len(ins): len(jobs) - 1},
        compiler_params=pltpu.CompilerParams(vmem_limit_bytes=18 << 20),
        cost_estimate=pl.CostEstimate(flops=flops, bytes_accessed=size, transcendentals=0),
        name="weight_grads",
    )(
        *[pltpu.with_memory_space_constraint(x, pltpu.VMEM) for x in ins],
        *([] if begun is None else [begun]),
    )


def other_cols(partial):
    size = lax.axis_size("col")
    if size == 2:
        return turn(partial, "col", 1)
    return (lax.psum(partial.astype(F32), "col") - partial.astype(F32)).astype(BF)


def silu_slope(value):
    sig = jax.nn.sigmoid(value)
    return sig * (1.0 + value * (1.0 - sig))


def matmul(a, b, dims=(((1,), (0,)), ((), ()))):
    return lax.dot_general(a, b, dims, preferred_element_type=F32)


def per_device(inputs, sample_ids, send_base, recv_base, w_up, w_down, cotangent):
    ticks = inputs.shape[1]
    rows = lax.axis_size("row")
    piece_rows, width = inputs.shape[2:]
    tokens, hidden = rows * piece_rows, w_up.shape[2]
    stack_like = jax.ShapeDtypeStruct((1, ticks, piece_rows, width), BF)
    piece_like = jax.ShapeDtypeStruct((piece_rows, width), BF)
    half_like = jax.ShapeDtypeStruct((tokens // 2, hidden), BF)

    def products(pieces, weight, waited=()):
        near, far = halves(pieces)
        return zip(stack_times(near, weight, waited), stack_times(far, weight))

    def gathered(block, others=()):
        near, far = halves(gather_rows(block))
        return [*near, *(after(far, others) if others else far)]

    def turn_blocks(tick, other):
        for blocks, done in ((full_ins, turned_ins), (acts, turned_acts)):
            like = jax.ShapeDtypeStruct((blocks[tick][0].shape[1], tokens), BF)
            done.extend(run(turned, [like], *after(blocks[tick], other)))

    act_in, last_cot = first_pieces(inputs, cotangent)
    cot_pieces = [last_cot] + [None] * (rows - 1)
    full_ins, acts, pres, seen_in, seen_out = [], [], [], [], []
    turned_ins, turned_acts = [], []
    for tick in range(ticks):
        if tick == 0:
            up_kept, down_kept = hold(after([w_up[0], w_down[0]], act_in))
            pieces, waited = gathered(act_in), []
        else:
            act_in = run(arrive, [piece_like], bases[tick - 1], hand_over(sending, 1))[0]
            waited = beside(tick - 1)
            for j in waited:
                cot_pieces[j] = swap_rows(after(last_cot, sending), j)
            waited = [cot_pieces[j] for j in waited]
            if tick == ticks - 1:
                full_cot, first_grads = products(cot_pieces, down_turned)
                pieces, waited = gathered(act_in, first_grads), []
            else:
                pieces = gathered(act_in)
        full_in, partial = products(pieces, up_kept, waited)
        pre = [(mine, other_cols(mine)) for mine in partial]
        if tick < ticks - 1:
            act, terms = through(silu_part, "down_part", pre, down_kept, piece_like)
            acts.append(act)
            terms_in = scatter_rows(terms)
            if tick == 0:
                (down_turned,) = run(
                    turned_weight, [jax.ShapeDtypeStruct((width, hidden), BF)], after(down_kept, terms)
                )
                stored, bases, cots = fetch(after(sample_ids, terms), inputs, send_base, recv_base, cotangent)
                terms_in[0] = after(terms_in[0], (down_turned, stored))
            if tick == 1:
                (up_turned,) = run(turned_weight, [jax.ShapeDtypeStruct((hidden, width), BF)], after(up_kept, terms))
                turn_blocks(0, terms)
                terms_in[0] = after(terms_in[0], (up_turned, turned_ins, turned_acts))
            act_out, sending = run(leave, [piece_like] * 2, act_in, *terms_in, stored[tick])
            seen_out.append(act_out)
        full_ins.append(full_in)
        pres.append(pre)
        seen_in.append(act_in)
    full_grads, pre_grads, seen_grad = [None] * ticks, [None] * ticks, [None] * ticks
    for step in range(ticks):
        tick = ticks - 1 - step
        if step == 0:
            grad_out, full_grad, partial = last_cot, full_cot, first_grads
        else:
            arrived = hand_over(sending, -1)
            if step == 1:
                acts.append(run(both_silu, [half_like] * 2, *after([*pres[-1][0], *pres[-1][1]], sending)))
                out_pieces = run(
                    down_again, [piece_like] * rows, *acts[-1], down_kept, flops=2 * tokens * width * hidden
                )
                arrived = after(arrived, out_pieces)
                out_terms = list(out_pieces)
            (grad_out,) = run(arrive, [piece_like], cots[tick], arrived)
            for j in beside(step - 1):
                out_terms[j] = swap_rows(after(out_pieces[j], sending), j)
            waited = [out_terms[j] for j in beside(step - 1)]
            if step == ticks - 1:
                section_input, section_output = stacked(
                    functools.partial(finish_forward, ticks), 2, [*seen_in, *seen_out, *out_terms], stack_like,
                    "finish_forward",
                )
                pieces, waited = gathered(grad_out, [section_output]), []
            else:
                pieces = gathered(grad_out)
            full_grad, partial = products(pieces, down_turned, waited)
        full_grads[tick] = full_grad
        ins = [(mine, other_cols(mine), *known) for mine, known in zip(partial, pres[tick])]
        if step == ticks - 1:
            grad_halves = [half for blocks in full_grads for half in blocks]
            (half_down,) = weight_products([(turned_acts, grad_halves, (hidden, width), 0, hidden // 2)])
            ins[1] = after(ins[1], half_down)
        grad_pre, terms = through(slope_part, "in_part", ins, up_turned, piece_like)
        terms_in = scatter_rows(terms)
        if step < ticks - 1:
            turn_blocks(step + 1, terms)
            terms_in[0] = after(terms_in[0], (turned_ins, turned_acts))
            (sending,) = run(leave_back, [piece_like], grad_out, *terms_in)
            seen_grad[tick] = sending
        pre_grads[tick] = grad_pre
    turned_ins, turned_acts = after((turned_ins, turned_acts), terms)
    grad_up, grad_down = weight_products(
        [
            (turned_ins, [half for blocks in pre_grads for half in blocks], (width, hidden), 0, width),
            (turned_acts, grad_halves, (hidden, width), hidden // 2, hidden),
        ],
        half_down,
    )
    terms_in[0] = after(terms_in[0], (grad_up, grad_down))
    (input_grad,) = stacked(finish, 1, [grad_out, *terms_in, *seen_grad[1:]], stack_like, "finish")
    return (
        section_input,
        section_output,
        input_grad,
        grad_up[None],
        grad_down[None],
    )


def solution(mesh):
    placed = (
        P("section", None, "row", "col"),
        P(),
        P("section", None, "row", "col"),
        P("section", None, "row", "col"),
        P("section", "col", "row"),
        P("section", "row", "col"),
        P("section", None, "row", "col"),
    )
    return jax.shard_map(
        per_device,
        mesh=mesh,
        in_specs=placed,
        out_specs=(
            P("section", None, "row", "col"),
            P("section", None, "row", "col"),
            P("section", None, "row", "col"),
            P("section", "col", "row"),
            P("section", "row", "col"),
        ),
        check_vma=False,
    )
```

```python
import functools

import jax
import jax.numpy as jnp
from jax import lax
from jax.experimental import pallas as pl
from jax.experimental.pallas import tpu as pltpu
from jax.sharding import PartitionSpec as P

BF = jnp.bfloat16
F32 = jnp.float32
WEIGHT_CUTS = 8


def hand_over(block, distance):
    sections = range(lax.axis_size("section"))
    return lax.ppermute(block, "section", [(i - distance, i) for i in sections if i - distance in sections])


def turn(block, axis, distance):
    size = lax.axis_size(axis)
    return lax.ppermute(block, axis, [(i, (i + distance) % size) for i in range(size)])


def partner(row, j, size):
    return row ^ ((size - j) % size) if size & (size - 1) == 0 else (j - row) % size


def swap_rows(block, j):
    size = lax.axis_size("row")
    return lax.ppermute(block, "row", [(i, partner(i, j, size)) for i in range(size)])


def gather_rows(block):
    return [swap_rows(block, j) if j else block for j in range(lax.axis_size("row"))]


def scatter_rows(pieces):
    return [swap_rows(piece, j) if j else piece for j, piece in enumerate(pieces)]


def beside(turn):
    size = lax.axis_size("row")
    return [[size - 1, size - 2], list(range(1, size - 2))][turn] if size > 2 else [[], [1]][turn]


def after(block, other):
    return lax.optimization_barrier((block, other))[0]


def vmem(count):
    return [pl.BlockSpec(memory_space=pltpu.VMEM)] * count


def run(kernel, outs, *ins, flops=0, scratch=(), name=None):
    ins = [pltpu.with_memory_space_constraint(block, pltpu.VMEM) for block in ins]
    size = sum(x.size * x.dtype.itemsize for x in [*ins, *outs])
    return pl.pallas_call(
        kernel,
        in_specs=vmem(len(ins)),
        out_specs=vmem(len(outs)),
        out_shape=[pltpu.VMEM(x.shape, x.dtype) for x in outs],
        scratch_shapes=scratch,
        compiler_params=pltpu.CompilerParams(vmem_limit_bytes=6 << 20),
        cost_estimate=pl.CostEstimate(flops=flops, bytes_accessed=size, transcendentals=0),
        name=name or kernel.__name__,
    )(*ins)


def first_kernel(inputs, cotangent, first, last, sems):
    copies = [
        pltpu.make_async_copy(inputs.at[0, 0], first, sems.at[0]),
        pltpu.make_async_copy(cotangent.at[0, cotangent.shape[1] - 1], last, sems.at[1]),
    ]
    for copy in copies:
        copy.start()
    for copy in copies:
        copy.wait()


def fetch_kernel(sample_ids, inputs, send_base, recv_base, cotangent, *refs):
    ticks = inputs.shape[1]
    count = ticks - 1
    stored, bases, cots = refs[:count], refs[count : 2 * count], refs[2 * count : 3 * count]
    fresh, sems = refs[3 * count :]
    section, sections = lax.axis_index("section"), lax.axis_size("section")
    samples = [sample_ids[tick - section + sections - 1] for tick in range(ticks)]
    copies = []
    for t in range(count):
        copies += [
            pltpu.make_async_copy(send_base.at[0, samples[t]], stored[t], sems.at[4 * t]),
            pltpu.make_async_copy(recv_base.at[0, samples[t + 1]], bases[t], sems.at[4 * t + 1]),
            pltpu.make_async_copy(inputs.at[0, t + 1], fresh.at[t], sems.at[4 * t + 2]),
            pltpu.make_async_copy(cotangent.at[0, t], cots[t], sems.at[4 * t + 3]),
        ]
    for copy in copies:
        copy.start()
    for copy in copies:
        copy.wait()
    for t in range(count):
        bases[t][...] = jnp.where(section == 0, fresh[t], bases[t][...])
        cots[t][...] = jnp.where(section == sections - 1, cots[t][...], jnp.zeros_like(cots[t]))


def fetch(sample_ids, inputs, send_base, recv_base, cotangent):
    count = inputs.shape[1] - 1
    piece = inputs.shape[2:]
    large = [pltpu.with_memory_space_constraint(x, pltpu.HBM) for x in (inputs, send_base, recv_base, cotangent)]
    outs = pl.pallas_call(
        fetch_kernel,
        in_specs=[pl.BlockSpec(memory_space=pltpu.SMEM)] + [pl.BlockSpec(memory_space=pltpu.HBM)] * len(large),
        out_specs=vmem(3 * count),
        out_shape=[pltpu.VMEM(piece, BF)] * (3 * count),
        scratch_shapes=[pltpu.VMEM((count, *piece), BF), pltpu.SemaphoreType.DMA((4 * count,))],
        compiler_params=pltpu.CompilerParams(vmem_limit_bytes=4 << 20),
        cost_estimate=pl.CostEstimate(flops=0, bytes_accessed=2 << 20, transcendentals=0),
        name="fetch",
    )(sample_ids, *large)
    return outs[:count], outs[count : 2 * count], outs[2 * count :]


def first_pieces(inputs, cotangent):
    piece = inputs.shape[2:]
    return pl.pallas_call(
        first_kernel,
        in_specs=[pl.BlockSpec(memory_space=pltpu.HBM)] * 2,
        out_specs=vmem(2),
        out_shape=[pltpu.VMEM(piece, BF)] * 2,
        scratch_shapes=[pltpu.SemaphoreType.DMA((2,))],
        compiler_params=pltpu.CompilerParams(vmem_limit_bytes=2 << 20),
        cost_estimate=pl.CostEstimate(flops=0, bytes_accessed=1 << 18, transcendentals=0),
        name="first",
    )(*[pltpu.with_memory_space_constraint(x, pltpu.HBM) for x in (inputs, cotangent)])


def added(first, terms):
    total = first[...].astype(F32)
    for term in terms:
        total = total + term[...].astype(F32)
    return total.astype(BF)


def arrive(base, arrived, out):
    out[...] = added(base, [arrived])


def leave(first, *refs):
    *terms, stored, out, delta = refs
    out[...] = added(first, terms)
    delta[...] = (out[...].astype(F32) - stored[...].astype(F32)).astype(BF)


def leave_back(first, *refs):
    *terms, out = refs
    out[...] = added(first, terms)


def finish_forward(count, *refs):
    *terms, ins, outs = refs
    entered, left, terms = terms[:count], terms[count : 2 * count - 1], terms[2 * count - 1 :]
    for t in range(count):
        ins[0, t] = entered[t][...]
    for t in range(count - 1):
        outs[0, t] = left[t][...]
    outs[0, count - 1] = added(entered[-1], terms)


def finish(first, *refs):
    *rest, grads = refs
    count = grads.shape[1] - 1
    grads[0, 0] = added(first, rest[:-count])
    for t in range(count):
        grads[0, t + 1] = rest[t - count][...]


def stacked(kernel, count, ins, like, name):
    return pl.pallas_call(
        kernel,
        in_specs=vmem(len(ins)),
        out_specs=vmem(count),
        out_shape=[like] * count,
        compiler_params=pltpu.CompilerParams(vmem_limit_bytes=6 << 20),
        cost_estimate=pl.CostEstimate(flops=0, bytes_accessed=1 << 20, transcendentals=0),
        name=name,
    )(*[pltpu.with_memory_space_constraint(x, pltpu.VMEM) for x in ins])


def turned(*refs):
    *pieces, out = refs
    out[...] = jnp.concatenate([piece[...] for piece in pieces], axis=0).T


def turned_weight(weight, out):
    for n in columns(out.shape[0]):
        out[n, :] = weight[:, n].T


def hold_kernel(*refs):
    *refs, sems = refs
    count = len(refs) // 2
    copies = []
    for k in range(count):
        step = refs[k].shape[0] // WEIGHT_CUTS
        for i in range(WEIGHT_CUTS):
            part = pl.ds(i * step, step)
            copies.append(pltpu.make_async_copy(refs[k].at[part], refs[count + k].at[part], sems.at[k, i]))
    for copy in copies:
        copy.start()
    for copy in copies:
        copy.wait()


def hold(weights):
    return pl.pallas_call(
        hold_kernel,
        in_specs=[pl.BlockSpec(memory_space=pltpu.HBM)] * len(weights),
        out_specs=vmem(len(weights)),
        out_shape=[pltpu.VMEM(weight.shape, BF) for weight in weights],
        scratch_shapes=[pltpu.SemaphoreType.DMA((len(weights), WEIGHT_CUTS))],
        compiler_params=pltpu.CompilerParams(vmem_limit_bytes=2 << 20),
        cost_estimate=pl.CostEstimate(flops=0, bytes_accessed=16 << 20, transcendentals=0),
        name="hold",
    )(*[pltpu.with_memory_space_constraint(weight, pltpu.HBM) for weight in weights])


def columns(width, step=256):
    step = min(width, step)
    return [slice(n, n + step) for n in range(0, width, step)]


def product_part(part, whole, weight, product):
    for n in columns(product.shape[1]):
        product[:, n] = matmul(whole[...], weight[:, n.start + part.start : n.stop + part.start]).astype(BF)


def stack_product(part, skip, *refs):
    *pieces, weight, whole, product = refs[skip:]
    whole[...] = jnp.concatenate([piece[...] for piece in pieces], axis=0)
    product_part(part, whole, weight, product)


def products(parts, pieces, weight, waited=()):
    tokens, width = len(pieces) * pieces[0].shape[0], weight.shape[0]
    whole_like = jax.ShapeDtypeStruct((tokens, width), BF)
    likes = [jax.ShapeDtypeStruct((tokens, part.stop - part.start), BF) for part in parts]
    flops = 2 * tokens * width * likes[0].shape[1]
    whole, first = run(
        functools.partial(stack_product, parts[0], len(waited)), [whole_like, likes[0]],
        *waited, *pieces, weight, flops=flops, name="stack_product",
    )
    rest = [
        run(functools.partial(product_part, part), [like], whole, weight, flops=flops, name="product_part")[0]
        for part, like in zip(parts[1:], likes[1:])
    ]
    return whole, [first, *rest]


def put_rows(pieces, n, product):
    rows = pieces[0].shape[0]
    for j, piece in enumerate(pieces):
        piece[:, n] = product[j * rows : (j + 1) * rows].astype(BF)


def silu_part(mine, other, act):
    for n in columns(act.shape[1]):
        pre = mine[:, n].astype(F32) + other[:, n].astype(F32)
        act[:, n] = jax.nn.silu(pre).astype(BF)


def slope_part(mine, other, pre_mine, pre_other, grad_pre):
    for n in columns(grad_pre.shape[1]):
        pre = pre_mine[:, n].astype(F32) + pre_other[:, n].astype(F32)
        grad = mine[:, n].astype(F32) + other[:, n].astype(F32)
        grad_pre[:, n] = (grad * silu_slope(pre)).astype(BF)


def first_part(pointwise, part, *refs):
    *ins, weight, hidden, total = refs
    pointwise(*ins, hidden)
    for n in columns(weight.shape[1]):
        total[:, n] = matmul(hidden[...], weight[part, n])


def last_part(pointwise, part, count, *refs):
    *ins, weight, total, hidden = refs[:-count]
    pointwise(*ins, hidden)
    for n in columns(weight.shape[1]):
        put_rows(refs[-count:], n, total[:, n] + matmul(hidden[...], weight[part, n]))


def through(pointwise, name, parts, ins, weight, piece_like, rows):
    tokens, width = rows * piece_like.shape[0], piece_like.shape[1]
    (first, last), done = parts, []
    flops = 2 * tokens * width * (first.stop - first.start)
    like = [jax.ShapeDtypeStruct((tokens, part.stop - part.start), BF) for part in parts]
    hidden, total = run(
        functools.partial(first_part, pointwise, first),
        [like[0], jax.ShapeDtypeStruct((tokens, width), F32)],
        *ins[0], weight, flops=flops, name=name,
    )
    rest, *pieces = run(
        functools.partial(last_part, pointwise, last, rows),
        [like[1]] + [piece_like] * rows,
        *ins[1], weight, total, flops=flops, name=name,
    )
    return [hidden, rest], pieces


def both_silu(*refs):
    *ins, first, last = refs
    silu_part(*ins[:2], first)
    silu_part(*ins[2:], last)


def down_again(parts, first, last, weight, *pieces):
    for n in columns(weight.shape[1]):
        total = matmul(first[...], weight[parts[0], n]) + matmul(last[...], weight[parts[1], n])
        put_rows(pieces, n, total)


def grad_begun(row_parts, col_parts, *refs):
    *blocks, total, left, right = refs
    depth = blocks[0].shape[1]
    count = left.shape[1] // depth
    lefts, rights = blocks[: row_parts * count], blocks[row_parts * count :]
    for i, block in enumerate(lefts):
        size, part, t = block.shape[0], i // count, i % count
        left[part * size : (part + 1) * size, t * depth : (t + 1) * depth] = block[...]
    for i, block in enumerate(rights):
        size, t, part = block.shape[1], i // col_parts, i % col_parts
        right[t * depth : (t + 1) * depth, part * size : (part + 1) * size] = block[...]
    for m in columns(total.shape[0]):
        for n in columns(total.shape[1]):
            total[m, n] = matmul(left[m, :], right[:, n])


def begin_grad(lefts, rights):
    ins = [block for part in lefts for block in part] + [block for tick in rights for block in tick]
    rows = sum(part[0].shape[0] for part in lefts)
    width = sum(block.shape[1] for block in rights[0])
    depth = lefts[0][0].shape[1] * len(rights)
    return run(
        functools.partial(grad_begun, len(lefts), len(rights[0])),
        [jax.ShapeDtypeStruct((rows, width), F32)], *ins,
        flops=2 * rows * width * depth, name="grad_begun",
        scratch=[pltpu.VMEM((rows, depth), BF), pltpu.VMEM((depth, width), BF)],
    )[0]


def grads_ended(cuts, *refs):
    place, copies = 0, []
    ends = sum(left + right + 1 for left, right in cuts)
    outs, rooms = refs[ends : ends + len(cuts)], refs[ends + len(cuts) :]
    for k, (left, right) in enumerate(cuts):
        lefts, rights = refs[place : place + left], refs[place + left : place + left + right]
        total = refs[place + left + right]
        place += left + right + 1
        room, sems = rooms[2 * k : 2 * k + 2]
        row = chunk = 0
        for block in lefts:
            for m in columns(block.shape[0]):
                size, col = m.stop - m.start, 0
                here = slice(row, row + size)
                for part in rights:
                    for n in columns(part.shape[1]):
                        there = slice(col + n.start, col + n.stop)
                        room[here, there] = (total[here, there] + matmul(block[m, :], part[:, n])).astype(BF)
                    col += part.shape[1]
                copies.append(
                    pltpu.make_async_copy(room.at[pl.ds(row, size)], outs[k].at[pl.ds(row, size)], sems.at[chunk])
                )
                copies[-1].start()
                row, chunk = row + size, chunk + 1
    for copy in copies:
        copy.wait()


def end_grads(jobs):
    ins = [block for lefts, rights, total in jobs for block in (*lefts, *rights, total)]
    shapes = [total.shape for _, _, total in jobs]
    scratch = []
    for shape in shapes:
        scratch += [pltpu.VMEM(shape, BF), pltpu.SemaphoreType.DMA((len(columns(shape[0])),))]
    size = sum(rows * width for rows, width in shapes)
    return pl.pallas_call(
        functools.partial(grads_ended, tuple((len(lefts), len(rights)) for lefts, rights, _ in jobs)),
        in_specs=vmem(len(ins)),
        out_specs=[pl.BlockSpec(memory_space=pl.ANY)] * len(jobs),
        out_shape=[jax.ShapeDtypeStruct(shape, BF) for shape in shapes],
        scratch_shapes=scratch,
        compiler_params=pltpu.CompilerParams(vmem_limit_bytes=12 << 20),
        cost_estimate=pl.CostEstimate(
            flops=2 * size * jobs[0][0][0].shape[1], bytes_accessed=2 * size, transcendentals=0
        ),
        name="grads_ended",
    )(*[pltpu.with_memory_space_constraint(x, pltpu.VMEM) for x in ins])


def other_cols(partial):
    size = lax.axis_size("col")
    if size == 2:
        return turn(partial, "col", 1)
    return (lax.psum(partial.astype(F32), "col") - partial.astype(F32)).astype(BF)


def swapped(parts):
    pairs = []
    for mine in parts:
        pairs.append((mine, other_cols(after(mine, pairs[-1][1]) if pairs else mine)))
    return pairs


def silu_slope(value):
    sig = jax.nn.sigmoid(value)
    return sig * (1.0 + value * (1.0 - sig))


def matmul(a, b, dims=(((1,), (0,)), ((), ()))):
    return lax.dot_general(a, b, dims, preferred_element_type=F32)


def per_device(inputs, sample_ids, send_base, recv_base, w_up, w_down, cotangent):
    ticks = inputs.shape[1]
    rows = lax.axis_size("row")
    piece_rows, width = inputs.shape[2:]
    tokens, hidden = rows * piece_rows, w_up.shape[2]
    stack_like = jax.ShapeDtypeStruct((1, ticks, piece_rows, width), BF)
    parts = [slice(0, hidden // 2), slice(hidden // 2, hidden)]
    piece_like = jax.ShapeDtypeStruct((piece_rows, width), BF)
    part_like = jax.ShapeDtypeStruct((tokens, hidden // 2), BF)
    turned_like = jax.ShapeDtypeStruct((width, tokens), BF)
    turned_part = jax.ShapeDtypeStruct((hidden // 2, tokens), BF)

    def turn_blocks(tick, other):
        turned_ins.extend(run(turned, [turned_like], after(full_ins[tick], other)))
        for k in range(2):
            turned_acts[k].extend(run(turned, [turned_part], after(acts[tick][k], other)))

    act_in, last_cot = first_pieces(inputs, cotangent)
    cot_pieces = [last_cot] + [None] * (rows - 1)
    full_ins, acts, pres, seen_in, seen_out = [], [], [], [], []
    turned_ins, turned_acts = [], [[], []]
    for tick in range(ticks):
        waited = []
        if tick:
            act_in = run(arrive, [piece_like], bases[tick - 1], hand_over(sending, 1))[0]
            for j in beside(tick - 1):
                cot_pieces[j] = swap_rows(after(last_cot, sending), j)
                waited.append(cot_pieces[j])
        pieces = gather_rows(act_in)
        if tick == 0:
            up_kept, down_kept = hold(after([w_up[0], w_down[0]], act_in))
            pieces = after(pieces, up_kept)
        if tick == ticks - 1:
            full_cot, first_grads = products(parts, cot_pieces, down_turned)
            pieces, waited = after(pieces, first_grads), []
        full_in, partial = products(parts, pieces, up_kept, waited)
        pre = swapped(partial)
        if tick < ticks - 1:
            act, terms = through(silu_part, "down_part", parts, pre, down_kept, piece_like, rows)
            acts.append(act)
            terms_in = scatter_rows(terms)
            if tick == 0:
                (down_turned,) = run(
                    turned_weight, [jax.ShapeDtypeStruct((width, hidden), BF)], after(down_kept, terms)
                )
                stored, bases, cots = fetch(after(sample_ids, terms), inputs, send_base, recv_base, cotangent)
                terms_in[0] = after(terms_in[0], (down_turned, stored))
            if tick == 1:
                (up_turned,) = run(turned_weight, [jax.ShapeDtypeStruct((hidden, width), BF)], after(up_kept, terms))
                turn_blocks(0, terms)
                terms_in[0] = after(terms_in[0], (up_turned, turned_ins, turned_acts))
            act_out, sending = run(leave, [piece_like] * 2, act_in, *terms_in, stored[tick])
            seen_out.append(act_out)
        full_ins.append(full_in)
        pres.append(pre)
        seen_in.append(act_in)
    full_grads, pre_grads, seen_grad = [None] * ticks, [None] * ticks, [None] * ticks
    for step in range(ticks):
        tick = ticks - 1 - step
        if step == 0:
            grad_out, full_grad, partial = last_cot, full_cot, first_grads
        else:
            arrived = hand_over(sending, -1)
            if step == 1:
                acts.append(run(both_silu, [part_like] * 2, *after([*pres[-1][0], *pres[-1][1]], sending)))
                out_pieces = run(
                    functools.partial(down_again, parts), [piece_like] * rows, *acts[-1], down_kept,
                    flops=2 * tokens * width * hidden, name="down_again",
                )
                arrived = after(arrived, out_pieces)
                out_terms = list(out_pieces)
            (grad_out,) = run(arrive, [piece_like], cots[tick], arrived)
            waited = []
            for j in beside(step - 1):
                out_terms[j] = swap_rows(after(out_pieces[j], sending), j)
                waited.append(out_terms[j])
            pieces = gather_rows(grad_out)
            if step == ticks - 1:
                section_input, section_output = stacked(
                    functools.partial(finish_forward, ticks), 2, [*seen_in, *seen_out, *out_terms], stack_like,
                    "finish_forward",
                )
                begun_down = begin_grad([part[1:] for part in turned_acts], [[block] for block in after(full_grads[1:], grad_out)])
                pieces, waited = after(pieces, (section_output, begun_down)), []
            full_grad, partial = products(parts, pieces, down_turned, waited)
        full_grads[tick] = full_grad
        ins = [(*pair, *known) for pair, known in zip(swapped(partial), pres[tick])]
        grad_pre, terms = through(slope_part, "in_part", parts, ins, up_turned, piece_like, rows)
        terms_in = scatter_rows(terms)
        if step < ticks - 1:
            turn_blocks(step + 1, terms)
            terms_in[0] = after(terms_in[0], (turned_ins, turned_acts))
            if step == ticks - 2:
                begun_up = begin_grad([turned_ins[1:]], [*pre_grads[1:tick], grad_pre, *pre_grads[tick + 1 :]])
                terms_in[0] = after(terms_in[0], begun_up)
            (sending,) = run(leave_back, [piece_like], grad_out, *terms_in)
            seen_grad[tick] = sending
        pre_grads[tick] = grad_pre
    grad_up, grad_down = end_grads(
        [
            ([turned_ins[0]], grad_pre, after(begun_up, terms)),
            ([part[0] for part in turned_acts], [full_grad], begun_down),
        ]
    )
    terms_in[0] = after(terms_in[0], (grad_up, grad_down))
    (input_grad,) = stacked(finish, 1, [grad_out, *terms_in, *seen_grad[1:]], stack_like, "finish")
    return (
        section_input,
        section_output,
        input_grad,
        grad_up[None],
        grad_down[None],
    )


def solution(mesh):
    placed = (
        P("section", None, "row", "col"),
        P(),
        P("section", None, "row", "col"),
        P("section", None, "row", "col"),
        P("section", "col", "row"),
        P("section", "row", "col"),
        P("section", None, "row", "col"),
    )
    return jax.shard_map(
        per_device,
        mesh=mesh,
        in_specs=placed,
        out_specs=(
            P("section", None, "row", "col"),
            P("section", None, "row", "col"),
            P("section", None, "row", "col"),
            P("section", "col", "row"),
            P("section", "row", "col"),
        ),
        check_vma=False,
    )
```

```python
import functools

import jax
import jax.numpy as jnp
from jax import lax
from jax.experimental import pallas as pl
from jax.experimental.pallas import tpu as pltpu
from jax.sharding import PartitionSpec as P

BF = jnp.bfloat16
F32 = jnp.float32
WEIGHT_CUTS = 8


def hand_over(block, distance):
    sections = range(lax.axis_size("section"))
    return lax.ppermute(block, "section", [(i - distance, i) for i in sections if i - distance in sections])


def turn(block, axis, distance):
    size = lax.axis_size(axis)
    return lax.ppermute(block, axis, [(i, (i + distance) % size) for i in range(size)])


def partner(row, j, size):
    return row ^ ((size - j) % size) if size & (size - 1) == 0 else (j - row) % size


def swap_rows(block, j):
    size = lax.axis_size("row")
    return lax.ppermute(block, "row", [(i, partner(i, j, size)) for i in range(size)])


def gather_rows(block):
    return [swap_rows(block, j) if j else block for j in range(lax.axis_size("row"))]


def scatter_rows(pieces):
    return [swap_rows(piece, j) if j else piece for j, piece in enumerate(pieces)]


def beside(turn):
    size = lax.axis_size("row")
    return [[size - 1, size - 2], list(range(1, size - 2))][turn] if size > 2 else [[], [1]][turn]


def after(block, other):
    return lax.optimization_barrier((block, other))[0]


def vmem(count):
    return [pl.BlockSpec(memory_space=pltpu.VMEM)] * count


def run(kernel, outs, *ins, flops=0, scratch=(), name=None):
    ins = [pltpu.with_memory_space_constraint(block, pltpu.VMEM) for block in ins]
    size = sum(x.size * x.dtype.itemsize for x in [*ins, *outs])
    return pl.pallas_call(
        kernel,
        in_specs=vmem(len(ins)),
        out_specs=vmem(len(outs)),
        out_shape=[pltpu.VMEM(x.shape, x.dtype) for x in outs],
        scratch_shapes=scratch,
        compiler_params=pltpu.CompilerParams(vmem_limit_bytes=6 << 20),
        cost_estimate=pl.CostEstimate(flops=flops, bytes_accessed=size, transcendentals=0),
        name=name or kernel.__name__,
    )(*ins)


def first_kernel(inputs, cotangent, first, last, sems):
    copies = [
        pltpu.make_async_copy(inputs.at[0, 0], first, sems.at[0]),
        pltpu.make_async_copy(cotangent.at[0, cotangent.shape[1] - 1], last, sems.at[1]),
    ]
    for copy in copies:
        copy.start()
    for copy in copies:
        copy.wait()


def fetch_kernel(sample_ids, inputs, send_base, recv_base, cotangent, *refs):
    ticks = inputs.shape[1]
    count = ticks - 1
    stored, bases, cots = refs[:count], refs[count : 2 * count], refs[2 * count : 3 * count]
    fresh, sems = refs[3 * count :]
    section, sections = lax.axis_index("section"), lax.axis_size("section")
    samples = [sample_ids[tick - section + sections - 1] for tick in range(ticks)]
    copies = []
    for t in range(count):
        copies += [
            pltpu.make_async_copy(send_base.at[0, samples[t]], stored[t], sems.at[4 * t]),
            pltpu.make_async_copy(recv_base.at[0, samples[t + 1]], bases[t], sems.at[4 * t + 1]),
            pltpu.make_async_copy(inputs.at[0, t + 1], fresh.at[t], sems.at[4 * t + 2]),
            pltpu.make_async_copy(cotangent.at[0, t], cots[t], sems.at[4 * t + 3]),
        ]
    for copy in copies:
        copy.start()
    for copy in copies:
        copy.wait()
    for t in range(count):
        bases[t][...] = jnp.where(section == 0, fresh[t], bases[t][...])
        cots[t][...] = jnp.where(section == sections - 1, cots[t][...], jnp.zeros_like(cots[t]))


def fetch(sample_ids, inputs, send_base, recv_base, cotangent):
    count = inputs.shape[1] - 1
    piece = inputs.shape[2:]
    large = [pltpu.with_memory_space_constraint(x, pltpu.HBM) for x in (inputs, send_base, recv_base, cotangent)]
    outs = pl.pallas_call(
        fetch_kernel,
        in_specs=[pl.BlockSpec(memory_space=pltpu.SMEM)] + [pl.BlockSpec(memory_space=pltpu.HBM)] * len(large),
        out_specs=vmem(3 * count),
        out_shape=[pltpu.VMEM(piece, BF)] * (3 * count),
        scratch_shapes=[pltpu.VMEM((count, *piece), BF), pltpu.SemaphoreType.DMA((4 * count,))],
        compiler_params=pltpu.CompilerParams(vmem_limit_bytes=4 << 20),
        cost_estimate=pl.CostEstimate(flops=0, bytes_accessed=2 << 20, transcendentals=0),
        name="fetch",
    )(sample_ids, *large)
    return outs[:count], outs[count : 2 * count], outs[2 * count :]


def first_pieces(inputs, cotangent):
    piece = inputs.shape[2:]
    return pl.pallas_call(
        first_kernel,
        in_specs=[pl.BlockSpec(memory_space=pltpu.HBM)] * 2,
        out_specs=vmem(2),
        out_shape=[pltpu.VMEM(piece, BF)] * 2,
        scratch_shapes=[pltpu.SemaphoreType.DMA((2,))],
        compiler_params=pltpu.CompilerParams(vmem_limit_bytes=2 << 20),
        cost_estimate=pl.CostEstimate(flops=0, bytes_accessed=1 << 18, transcendentals=0),
        name="first",
    )(*[pltpu.with_memory_space_constraint(x, pltpu.HBM) for x in (inputs, cotangent)])


def added(first, terms):
    total = first[...].astype(F32)
    for term in terms:
        total = total + term[...].astype(F32)
    return total.astype(BF)


def arrive(base, arrived, out):
    out[...] = added(base, [arrived])


def leave(first, *refs):
    *terms, stored, out, delta = refs
    out[...] = added(first, terms)
    delta[...] = (out[...].astype(F32) - stored[...].astype(F32)).astype(BF)


def leave_back(first, *refs):
    *terms, out = refs
    out[...] = added(first, terms)


def finish_forward(count, *refs):
    *terms, ins, outs = refs
    entered, left, terms = terms[:count], terms[count : 2 * count - 1], terms[2 * count - 1 :]
    for t in range(count):
        ins[0, t] = entered[t][...]
    for t in range(count - 1):
        outs[0, t] = left[t][...]
    outs[0, count - 1] = added(entered[-1], terms)


def finish(first, *refs):
    *rest, grads = refs
    count = grads.shape[1] - 1
    grads[0, 0] = added(first, rest[:-count])
    for t in range(count):
        grads[0, t + 1] = rest[t - count][...]


def stacked(kernel, count, ins, like, name):
    return pl.pallas_call(
        kernel,
        in_specs=vmem(len(ins)),
        out_specs=vmem(count),
        out_shape=[like] * count,
        compiler_params=pltpu.CompilerParams(vmem_limit_bytes=6 << 20),
        cost_estimate=pl.CostEstimate(flops=0, bytes_accessed=1 << 20, transcendentals=0),
        name=name,
    )(*[pltpu.with_memory_space_constraint(x, pltpu.VMEM) for x in ins])


def turned(*refs):
    *pieces, out = refs
    out[...] = jnp.concatenate([piece[...] for piece in pieces], axis=0).T


def turned_weight(weight, out):
    for n in columns(out.shape[0]):
        out[n, :] = weight[:, n].T


def hold_kernel(*refs):
    *refs, sems = refs
    count = len(refs) // 2
    copies = []
    for k in range(count):
        step = refs[k].shape[0] // WEIGHT_CUTS
        for i in range(WEIGHT_CUTS):
            part = pl.ds(i * step, step)
            copies.append(pltpu.make_async_copy(refs[k].at[part], refs[count + k].at[part], sems.at[k, i]))
    for copy in copies:
        copy.start()
    for copy in copies:
        copy.wait()


def hold(weights):
    return pl.pallas_call(
        hold_kernel,
        in_specs=[pl.BlockSpec(memory_space=pltpu.HBM)] * len(weights),
        out_specs=vmem(len(weights)),
        out_shape=[pltpu.VMEM(weight.shape, BF) for weight in weights],
        scratch_shapes=[pltpu.SemaphoreType.DMA((len(weights), WEIGHT_CUTS))],
        compiler_params=pltpu.CompilerParams(vmem_limit_bytes=2 << 20),
        cost_estimate=pl.CostEstimate(flops=0, bytes_accessed=16 << 20, transcendentals=0),
        name="hold",
    )(*[pltpu.with_memory_space_constraint(weight, pltpu.HBM) for weight in weights])


def columns(width, step=256):
    step = min(width, step)
    return [slice(n, n + step) for n in range(0, width, step)]


def product_part(part, whole, weight, product):
    for n in columns(product.shape[1]):
        product[:, n] = matmul(whole[...], weight[:, n.start + part.start : n.stop + part.start]).astype(BF)


def stack_product(part, skip, *refs):
    *pieces, weight, whole, product = refs[skip:]
    whole[...] = jnp.concatenate([piece[...] for piece in pieces], axis=0)
    product_part(part, whole, weight, product)


def products(parts, pieces, weight, waited=()):
    tokens, width = len(pieces) * pieces[0].shape[0], weight.shape[0]
    whole_like = jax.ShapeDtypeStruct((tokens, width), BF)
    likes = [jax.ShapeDtypeStruct((tokens, part.stop - part.start), BF) for part in parts]
    flops = 2 * tokens * width * likes[0].shape[1]
    whole, first = run(
        functools.partial(stack_product, parts[0], len(waited)), [whole_like, likes[0]],
        *waited, *pieces, weight, flops=flops, name="stack_product",
    )
    rest = [
        run(functools.partial(product_part, part), [like], whole, weight, flops=flops, name="product_part")[0]
        for part, like in zip(parts[1:], likes[1:])
    ]
    return whole, [first, *rest]


def put_rows(pieces, n, product):
    rows = pieces[0].shape[0]
    for j, piece in enumerate(pieces):
        piece[:, n] = product[j * rows : (j + 1) * rows].astype(BF)


def silu_part(mine, other, act):
    for n in columns(act.shape[1]):
        pre = mine[:, n].astype(F32) + other[:, n].astype(F32)
        act[:, n] = jax.nn.silu(pre).astype(BF)


def slope_part(mine, other, pre_mine, pre_other, grad_pre):
    for n in columns(grad_pre.shape[1]):
        pre = pre_mine[:, n].astype(F32) + pre_other[:, n].astype(F32)
        grad = mine[:, n].astype(F32) + other[:, n].astype(F32)
        grad_pre[:, n] = (grad * silu_slope(pre)).astype(BF)


def first_part(pointwise, part, *refs):
    *ins, weight, hidden, total = refs
    pointwise(*ins, hidden)
    for n in columns(weight.shape[1]):
        total[:, n] = matmul(hidden[...], weight[part, n])


def last_part(pointwise, part, count, *refs):
    *ins, weight, total, hidden = refs[:-count]
    pointwise(*ins, hidden)
    for n in columns(weight.shape[1]):
        put_rows(refs[-count:], n, total[:, n] + matmul(hidden[...], weight[part, n]))


def through(pointwise, name, parts, ins, weight, piece_like, rows):
    tokens, width = rows * piece_like.shape[0], piece_like.shape[1]
    (first, last), done = parts, []
    flops = 2 * tokens * width * (first.stop - first.start)
    like = [jax.ShapeDtypeStruct((tokens, part.stop - part.start), BF) for part in parts]
    hidden, total = run(
        functools.partial(first_part, pointwise, first),
        [like[0], jax.ShapeDtypeStruct((tokens, width), F32)],
        *ins[0], weight, flops=flops, name=name,
    )
    rest, *pieces = run(
        functools.partial(last_part, pointwise, last, rows),
        [like[1]] + [piece_like] * rows,
        *ins[1], weight, total, flops=flops, name=name,
    )
    return [hidden, rest], pieces


def both_silu(*refs):
    *ins, first, last = refs
    silu_part(*ins[:2], first)
    silu_part(*ins[2:], last)


def down_again(parts, first, last, weight, *pieces):
    for n in columns(weight.shape[1]):
        total = matmul(first[...], weight[parts[0], n]) + matmul(last[...], weight[parts[1], n])
        put_rows(pieces, n, total)


def grad_begun(row_parts, col_parts, *refs):
    *blocks, total, left, right = refs
    depth = blocks[0].shape[1]
    count = left.shape[1] // depth
    lefts, rights = blocks[: row_parts * count], blocks[row_parts * count :]
    for i, block in enumerate(lefts):
        size, part, t = block.shape[0], i // count, i % count
        left[part * size : (part + 1) * size, t * depth : (t + 1) * depth] = block[...]
    for i, block in enumerate(rights):
        size, t, part = block.shape[1], i // col_parts, i % col_parts
        right[t * depth : (t + 1) * depth, part * size : (part + 1) * size] = block[...]
    for m in columns(total.shape[0]):
        for n in columns(total.shape[1]):
            total[m, n] = matmul(left[m, :], right[:, n])


def begin_grad(lefts, rights):
    ins = [block for part in lefts for block in part] + [block for tick in rights for block in tick]
    rows = sum(part[0].shape[0] for part in lefts)
    width = sum(block.shape[1] for block in rights[0])
    depth = lefts[0][0].shape[1] * len(rights)
    return run(
        functools.partial(grad_begun, len(lefts), len(rights[0])),
        [jax.ShapeDtypeStruct((rows, width), F32)], *ins,
        flops=2 * rows * width * depth, name="grad_begun",
        scratch=[pltpu.VMEM((rows, depth), BF), pltpu.VMEM((depth, width), BF)],
    )[0]


def grads_ended(cuts, *refs):
    place, copies = 0, []
    ends = sum(left + right + 1 for left, right in cuts)
    outs, rooms = refs[ends : ends + len(cuts)], refs[ends + len(cuts) :]
    for k, (left, right) in enumerate(cuts):
        lefts, rights = refs[place : place + left], refs[place + left : place + left + right]
        total = refs[place + left + right]
        place += left + right + 1
        room, sems = rooms[2 * k : 2 * k + 2]
        row = chunk = 0
        for block in lefts:
            for m in columns(block.shape[0]):
                size, col = m.stop - m.start, 0
                here = slice(row, row + size)
                for part in rights:
                    for n in columns(part.shape[1]):
                        there = slice(col + n.start, col + n.stop)
                        room[here, there] = (total[here, there] + matmul(block[m, :], part[:, n])).astype(BF)
                    col += part.shape[1]
                copies.append(
                    pltpu.make_async_copy(room.at[pl.ds(row, size)], outs[k].at[pl.ds(row, size)], sems.at[chunk])
                )
                copies[-1].start()
                row, chunk = row + size, chunk + 1
    for copy in copies:
        copy.wait()


def end_grads(jobs):
    ins = [block for lefts, rights, total in jobs for block in (*lefts, *rights, total)]
    shapes = [total.shape for _, _, total in jobs]
    scratch = []
    for shape in shapes:
        scratch += [pltpu.VMEM(shape, BF), pltpu.SemaphoreType.DMA((len(columns(shape[0])),))]
    size = sum(rows * width for rows, width in shapes)
    return pl.pallas_call(
        functools.partial(grads_ended, tuple((len(lefts), len(rights)) for lefts, rights, _ in jobs)),
        in_specs=vmem(len(ins)),
        out_specs=[pl.BlockSpec(memory_space=pl.ANY)] * len(jobs),
        out_shape=[jax.ShapeDtypeStruct(shape, BF) for shape in shapes],
        scratch_shapes=scratch,
        compiler_params=pltpu.CompilerParams(vmem_limit_bytes=12 << 20),
        cost_estimate=pl.CostEstimate(
            flops=2 * size * jobs[0][0][0].shape[1], bytes_accessed=2 * size, transcendentals=0
        ),
        name="grads_ended",
    )(*[pltpu.with_memory_space_constraint(x, pltpu.VMEM) for x in ins])


def other_cols(partial):
    size = lax.axis_size("col")
    if size == 2:
        return turn(partial, "col", 1)
    return (lax.psum(partial.astype(F32), "col") - partial.astype(F32)).astype(BF)


def silu_slope(value):
    sig = jax.nn.sigmoid(value)
    return sig * (1.0 + value * (1.0 - sig))


def matmul(a, b, dims=(((1,), (0,)), ((), ()))):
    return lax.dot_general(a, b, dims, preferred_element_type=F32)


def per_device(inputs, sample_ids, send_base, recv_base, w_up, w_down, cotangent):
    ticks = inputs.shape[1]
    rows = lax.axis_size("row")
    piece_rows, width = inputs.shape[2:]
    tokens, hidden = rows * piece_rows, w_up.shape[2]
    stack_like = jax.ShapeDtypeStruct((1, ticks, piece_rows, width), BF)
    parts = [slice(0, hidden // 2), slice(hidden // 2, hidden)]
    piece_like = jax.ShapeDtypeStruct((piece_rows, width), BF)
    part_like = jax.ShapeDtypeStruct((tokens, hidden // 2), BF)
    turned_like = jax.ShapeDtypeStruct((width, tokens), BF)
    turned_part = jax.ShapeDtypeStruct((hidden // 2, tokens), BF)

    def turn_blocks(tick, other):
        turned_ins.extend(run(turned, [turned_like], after(full_ins[tick], other)))
        for k in range(2):
            turned_acts[k].extend(run(turned, [turned_part], after(acts[tick][k], other)))

    act_in, last_cot = first_pieces(inputs, cotangent)
    cot_pieces = [last_cot] + [None] * (rows - 1)
    full_ins, acts, pres, seen_in, seen_out = [], [], [], [], []
    turned_ins, turned_acts = [], [[], []]
    for tick in range(ticks):
        waited = []
        if tick:
            act_in = run(arrive, [piece_like], bases[tick - 1], hand_over(sending, 1))[0]
            for j in beside(tick - 1):
                cot_pieces[j] = swap_rows(after(last_cot, sending), j)
                waited.append(cot_pieces[j])
        pieces = gather_rows(act_in)
        if tick == 0:
            up_kept, down_kept = hold(after([w_up[0], w_down[0]], act_in))
            pieces = after(pieces, up_kept)
        if tick == ticks - 1:
            full_cot, first_grads = products(parts, cot_pieces, down_turned)
            pieces, waited = after(pieces, first_grads), []
        full_in, partial = products(parts, pieces, up_kept, waited)
        pre = [(mine, other_cols(mine)) for mine in partial]
        if tick < ticks - 1:
            act, terms = through(silu_part, "down_part", parts, pre, down_kept, piece_like, rows)
            acts.append(act)
            terms_in = scatter_rows(terms)
            if tick == 0:
                (down_turned,) = run(
                    turned_weight, [jax.ShapeDtypeStruct((width, hidden), BF)], after(down_kept, terms)
                )
                stored, bases, cots = fetch(after(sample_ids, terms), inputs, send_base, recv_base, cotangent)
                terms_in[0] = after(terms_in[0], (down_turned, stored))
            if tick == 1:
                (up_turned,) = run(turned_weight, [jax.ShapeDtypeStruct((hidden, width), BF)], after(up_kept, terms))
                turn_blocks(0, terms)
                terms_in[0] = after(terms_in[0], (up_turned, turned_ins, turned_acts))
            act_out, sending = run(leave, [piece_like] * 2, act_in, *terms_in, stored[tick])
            seen_out.append(act_out)
        full_ins.append(full_in)
        pres.append(pre)
        seen_in.append(act_in)
    full_grads, pre_grads, seen_grad = [None] * ticks, [None] * ticks, [None] * ticks
    for step in range(ticks):
        tick = ticks - 1 - step
        if step == 0:
            grad_out, full_grad, partial = last_cot, full_cot, first_grads
        else:
            arrived = hand_over(sending, -1)
            if step == 1:
                acts.append(run(both_silu, [part_like] * 2, *after([*pres[-1][0], *pres[-1][1]], sending)))
                out_pieces = run(
                    functools.partial(down_again, parts), [piece_like] * rows, *acts[-1], down_kept,
                    flops=2 * tokens * width * hidden, name="down_again",
                )
                arrived = after(arrived, out_pieces)
                out_terms = list(out_pieces)
            (grad_out,) = run(arrive, [piece_like], cots[tick], arrived)
            waited = []
            for j in beside(step - 1):
                out_terms[j] = swap_rows(after(out_pieces[j], sending), j)
                waited.append(out_terms[j])
            pieces = gather_rows(grad_out)
            if step == ticks - 1:
                section_input, section_output = stacked(
                    functools.partial(finish_forward, ticks), 2, [*seen_in, *seen_out, *out_terms], stack_like,
                    "finish_forward",
                )
                begun_down = begin_grad([part[1:] for part in turned_acts], [[block] for block in after(full_grads[1:], grad_out)])
                pieces, waited = after(pieces, (section_output, begun_down)), []
            full_grad, partial = products(parts, pieces, down_turned, waited)
        full_grads[tick] = full_grad
        ins = [(mine, other_cols(mine), *known) for mine, known in zip(partial, pres[tick])]
        grad_pre, terms = through(slope_part, "in_part", parts, ins, up_turned, piece_like, rows)
        terms_in = scatter_rows(terms)
        if step < ticks - 1:
            turn_blocks(step + 1, terms)
            terms_in[0] = after(terms_in[0], (turned_ins, turned_acts))
            if step == ticks - 2:
                begun_up = begin_grad([turned_ins[1:]], [*pre_grads[1:tick], grad_pre, *pre_grads[tick + 1 :]])
                terms_in[0] = after(terms_in[0], begun_up)
            (sending,) = run(leave_back, [piece_like], grad_out, *terms_in)
            seen_grad[tick] = sending
        pre_grads[tick] = grad_pre
    grad_up, grad_down = end_grads(
        [
            ([turned_ins[0]], grad_pre, after(begun_up, terms)),
            ([part[0] for part in turned_acts], [full_grad], begun_down),
        ]
    )
    terms_in[0] = after(terms_in[0], (grad_up, grad_down))
    (input_grad,) = stacked(finish, 1, [grad_out, *terms_in, *seen_grad[1:]], stack_like, "finish")
    return (
        section_input,
        section_output,
        input_grad,
        grad_up[None],
        grad_down[None],
    )


def solution(mesh):
    placed = (
        P("section", None, "row", "col"),
        P(),
        P("section", None, "row", "col"),
        P("section", None, "row", "col"),
        P("section", "col", "row"),
        P("section", "row", "col"),
        P("section", None, "row", "col"),
    )
    return jax.shard_map(
        per_device,
        mesh=mesh,
        in_specs=placed,
        out_specs=(
            P("section", None, "row", "col"),
            P("section", None, "row", "col"),
            P("section", None, "row", "col"),
            P("section", "col", "row"),
            P("section", "row", "col"),
        ),
        check_vma=False,
    )
```

```python
import functools

import jax
import jax.numpy as jnp
from jax import lax
from jax.experimental import pallas as pl
from jax.experimental.pallas import tpu as pltpu
from jax.sharding import PartitionSpec as P

BF = jnp.bfloat16
F32 = jnp.float32
WEIGHT_CUTS = 8


def hand_over(block, distance):
    sections = range(lax.axis_size("section"))
    return lax.ppermute(block, "section", [(i - distance, i) for i in sections if i - distance in sections])


def turn(block, axis, distance):
    size = lax.axis_size(axis)
    return lax.ppermute(block, axis, [(i, (i + distance) % size) for i in range(size)])


def partner(row, j, size):
    return row ^ ((size - j) % size) if size & (size - 1) == 0 else (j - row) % size


def swap_rows(block, j):
    size = lax.axis_size("row")
    return lax.ppermute(block, "row", [(i, partner(i, j, size)) for i in range(size)])


def gather_rows(block):
    return [swap_rows(block, j) if j else block for j in range(lax.axis_size("row"))]


def scatter_rows(pieces):
    return [swap_rows(piece, j) if j else piece for j, piece in enumerate(pieces)]


def beside(turn):
    size = lax.axis_size("row")
    return [[size - 1, size - 2], list(range(1, size - 2))][turn] if size > 2 else [[], [1]][turn]


def after(block, other):
    return lax.optimization_barrier((block, other))[0]


def vmem(count):
    return [pl.BlockSpec(memory_space=pltpu.VMEM)] * count


def run(kernel, outs, *ins, flops=0, scratch=(), name=None):
    ins = [pltpu.with_memory_space_constraint(block, pltpu.VMEM) for block in ins]
    size = sum(x.size * x.dtype.itemsize for x in [*ins, *outs])
    return pl.pallas_call(
        kernel,
        in_specs=vmem(len(ins)),
        out_specs=vmem(len(outs)),
        out_shape=[pltpu.VMEM(x.shape, x.dtype) for x in outs],
        scratch_shapes=scratch,
        compiler_params=pltpu.CompilerParams(vmem_limit_bytes=6 << 20),
        cost_estimate=pl.CostEstimate(flops=flops, bytes_accessed=size, transcendentals=0),
        name=name or kernel.__name__,
    )(*ins)


def first_kernel(inputs, cotangent, first, last, sems):
    copies = [
        pltpu.make_async_copy(inputs.at[0, 0], first, sems.at[0]),
        pltpu.make_async_copy(cotangent.at[0, cotangent.shape[1] - 1], last, sems.at[1]),
    ]
    for copy in copies:
        copy.start()
    for copy in copies:
        copy.wait()


def fetch_kernel(sample_ids, inputs, send_base, recv_base, cotangent, *refs):
    ticks = inputs.shape[1]
    count = ticks - 1
    stored, bases, cots = refs[:count], refs[count : 2 * count], refs[2 * count : 3 * count]
    fresh, sems = refs[3 * count :]
    section, sections = lax.axis_index("section"), lax.axis_size("section")
    samples = [sample_ids[tick - section + sections - 1] for tick in range(ticks)]
    copies = []
    for t in range(count):
        copies += [
            pltpu.make_async_copy(send_base.at[0, samples[t]], stored[t], sems.at[4 * t]),
            pltpu.make_async_copy(recv_base.at[0, samples[t + 1]], bases[t], sems.at[4 * t + 1]),
            pltpu.make_async_copy(inputs.at[0, t + 1], fresh.at[t], sems.at[4 * t + 2]),
            pltpu.make_async_copy(cotangent.at[0, t], cots[t], sems.at[4 * t + 3]),
        ]
    for copy in copies:
        copy.start()
    for copy in copies:
        copy.wait()
    for t in range(count):
        bases[t][...] = jnp.where(section == 0, fresh[t], bases[t][...])
        cots[t][...] = jnp.where(section == sections - 1, cots[t][...], jnp.zeros_like(cots[t]))


def fetch(sample_ids, inputs, send_base, recv_base, cotangent):
    count = inputs.shape[1] - 1
    piece = inputs.shape[2:]
    large = [pltpu.with_memory_space_constraint(x, pltpu.HBM) for x in (inputs, send_base, recv_base, cotangent)]
    outs = pl.pallas_call(
        fetch_kernel,
        in_specs=[pl.BlockSpec(memory_space=pltpu.SMEM)] + [pl.BlockSpec(memory_space=pltpu.HBM)] * len(large),
        out_specs=vmem(3 * count),
        out_shape=[pltpu.VMEM(piece, BF)] * (3 * count),
        scratch_shapes=[pltpu.VMEM((count, *piece), BF), pltpu.SemaphoreType.DMA((4 * count,))],
        compiler_params=pltpu.CompilerParams(vmem_limit_bytes=4 << 20),
        cost_estimate=pl.CostEstimate(flops=0, bytes_accessed=2 << 20, transcendentals=0),
        name="fetch",
    )(sample_ids, *large)
    return outs[:count], outs[count : 2 * count], outs[2 * count :]


def first_pieces(inputs, cotangent):
    piece = inputs.shape[2:]
    return pl.pallas_call(
        first_kernel,
        in_specs=[pl.BlockSpec(memory_space=pltpu.HBM)] * 2,
        out_specs=vmem(2),
        out_shape=[pltpu.VMEM(piece, BF)] * 2,
        scratch_shapes=[pltpu.SemaphoreType.DMA((2,))],
        compiler_params=pltpu.CompilerParams(vmem_limit_bytes=2 << 20),
        cost_estimate=pl.CostEstimate(flops=0, bytes_accessed=1 << 18, transcendentals=0),
        name="first",
    )(*[pltpu.with_memory_space_constraint(x, pltpu.HBM) for x in (inputs, cotangent)])


def added(first, terms):
    total = first[...].astype(F32)
    for term in terms:
        total = total + term[...].astype(F32)
    return total.astype(BF)


def arrive(base, arrived, out):
    out[...] = added(base, [arrived])


def leave(first, *refs):
    *terms, stored, out, delta = refs
    out[...] = added(first, terms)
    delta[...] = (out[...].astype(F32) - stored[...].astype(F32)).astype(BF)


def leave_back(first, *refs):
    *terms, out = refs
    out[...] = added(first, terms)


def finish_forward(count, *refs):
    *terms, ins, outs = refs
    entered, left, terms = terms[:count], terms[count : 2 * count - 1], terms[2 * count - 1 :]
    for t in range(count):
        ins[0, t] = entered[t][...]
    for t in range(count - 1):
        outs[0, t] = left[t][...]
    outs[0, count - 1] = added(entered[-1], terms)


def finish(first, *refs):
    *rest, grads = refs
    count = grads.shape[1] - 1
    grads[0, 0] = added(first, rest[:-count])
    for t in range(count):
        grads[0, t + 1] = rest[t - count][...]


def stacked(kernel, count, ins, like, name):
    return pl.pallas_call(
        kernel,
        in_specs=vmem(len(ins)),
        out_specs=vmem(count),
        out_shape=[like] * count,
        compiler_params=pltpu.CompilerParams(vmem_limit_bytes=6 << 20),
        cost_estimate=pl.CostEstimate(flops=0, bytes_accessed=1 << 20, transcendentals=0),
        name=name,
    )(*[pltpu.with_memory_space_constraint(x, pltpu.VMEM) for x in ins])


def turned(*refs):
    *pieces, out = refs
    out[...] = jnp.concatenate([piece[...] for piece in pieces], axis=0).T


def turned_weight(weight, out):
    for n in columns(out.shape[0]):
        out[n, :] = weight[:, n].T


def hold_kernel(*refs):
    *refs, sems = refs
    count = len(refs) // 2
    copies = []
    for k in range(count):
        step = refs[k].shape[0] // WEIGHT_CUTS
        for i in range(WEIGHT_CUTS):
            part = pl.ds(i * step, step)
            copies.append(pltpu.make_async_copy(refs[k].at[part], refs[count + k].at[part], sems.at[k, i]))
    for copy in copies:
        copy.start()
    for copy in copies:
        copy.wait()


def hold(weights):
    return pl.pallas_call(
        hold_kernel,
        in_specs=[pl.BlockSpec(memory_space=pltpu.HBM)] * len(weights),
        out_specs=vmem(len(weights)),
        out_shape=[pltpu.VMEM(weight.shape, BF) for weight in weights],
        scratch_shapes=[pltpu.SemaphoreType.DMA((len(weights), WEIGHT_CUTS))],
        compiler_params=pltpu.CompilerParams(vmem_limit_bytes=2 << 20),
        cost_estimate=pl.CostEstimate(flops=0, bytes_accessed=16 << 20, transcendentals=0),
        name="hold",
    )(*[pltpu.with_memory_space_constraint(weight, pltpu.HBM) for weight in weights])


def columns(width, step=256):
    step = min(width, step)
    return [slice(n, n + step) for n in range(0, width, step)]


def product_part(part, whole, weight, product):
    for n in columns(product.shape[1]):
        product[:, n] = matmul(whole[...], weight[:, n.start + part.start : n.stop + part.start]).astype(BF)


def stack_product(part, skip, *refs):
    *pieces, weight, whole, product = refs[skip:]
    whole[...] = jnp.concatenate([piece[...] for piece in reversed(pieces)], axis=0)
    product_part(part, whole, weight, product)


def products(parts, pieces, weight, waited=()):
    tokens, width = len(pieces) * pieces[0].shape[0], weight.shape[0]
    whole_like = jax.ShapeDtypeStruct((tokens, width), BF)
    likes = [jax.ShapeDtypeStruct((tokens, part.stop - part.start), BF) for part in parts]
    flops = 2 * tokens * width * likes[0].shape[1]
    whole, first = run(
        functools.partial(stack_product, parts[0], len(waited)), [whole_like, likes[0]],
        *waited, *reversed(pieces), weight, flops=flops, name="stack_product",
    )
    rest = [
        run(functools.partial(product_part, part), [like], whole, weight, flops=flops, name="product_part")[0]
        for part, like in zip(parts[1:], likes[1:])
    ]
    return whole, [first, *rest]


def put_rows(pieces, n, product):
    rows = pieces[0].shape[0]
    for j, piece in enumerate(pieces):
        piece[:, n] = product[j * rows : (j + 1) * rows].astype(BF)


def silu_part(mine, other, act):
    for n in columns(act.shape[1]):
        pre = mine[:, n].astype(F32) + other[:, n].astype(F32)
        act[:, n] = jax.nn.silu(pre).astype(BF)


def slope_part(mine, other, pre_mine, pre_other, grad_pre):
    for n in columns(grad_pre.shape[1]):
        pre = pre_mine[:, n].astype(F32) + pre_other[:, n].astype(F32)
        grad = mine[:, n].astype(F32) + other[:, n].astype(F32)
        grad_pre[:, n] = (grad * silu_slope(pre)).astype(BF)


def first_part(pointwise, part, *refs):
    *ins, weight, hidden, total = refs
    pointwise(*ins, hidden)
    for n in columns(weight.shape[1]):
        total[:, n] = matmul(hidden[...], weight[part, n])


def last_part(pointwise, part, count, *refs):
    *ins, weight, total, hidden = refs[:-count]
    pointwise(*ins, hidden)
    for n in columns(weight.shape[1]):
        put_rows(refs[-count:], n, total[:, n] + matmul(hidden[...], weight[part, n]))


def through(pointwise, name, parts, ins, weight, piece_like, rows):
    tokens, width = rows * piece_like.shape[0], piece_like.shape[1]
    (first, last), done = parts, []
    flops = 2 * tokens * width * (first.stop - first.start)
    like = [jax.ShapeDtypeStruct((tokens, part.stop - part.start), BF) for part in parts]
    hidden, total = run(
        functools.partial(first_part, pointwise, first),
        [like[0], jax.ShapeDtypeStruct((tokens, width), F32)],
        *ins[0], weight, flops=flops, name=name,
    )
    rest, *pieces = run(
        functools.partial(last_part, pointwise, last, rows),
        [like[1]] + [piece_like] * rows,
        *ins[1], weight, total, flops=flops, name=name,
    )
    return [hidden, rest], pieces


def both_silu(*refs):
    *ins, first, last = refs
    silu_part(*ins[:2], first)
    silu_part(*ins[2:], last)


def down_again(parts, first, last, weight, *pieces):
    for n in columns(weight.shape[1]):
        total = matmul(first[...], weight[parts[0], n]) + matmul(last[...], weight[parts[1], n])
        put_rows(pieces, n, total)


def grad_begun(row_parts, col_parts, *refs):
    *blocks, total, left, right = refs
    depth = blocks[0].shape[1]
    count = left.shape[1] // depth
    lefts, rights = blocks[: row_parts * count], blocks[row_parts * count :]
    for i, block in enumerate(lefts):
        size, part, t = block.shape[0], i // count, i % count
        left[part * size : (part + 1) * size, t * depth : (t + 1) * depth] = block[...]
    for i, block in enumerate(rights):
        size, t, part = block.shape[1], i // col_parts, i % col_parts
        right[t * depth : (t + 1) * depth, part * size : (part + 1) * size] = block[...]
    for m in columns(total.shape[0]):
        for n in columns(total.shape[1]):
            total[m, n] = matmul(left[m, :], right[:, n])


def begin_grad(lefts, rights):
    ins = [block for part in lefts for block in part] + [block for tick in rights for block in tick]
    rows = sum(part[0].shape[0] for part in lefts)
    width = sum(block.shape[1] for block in rights[0])
    depth = lefts[0][0].shape[1] * len(rights)
    return run(
        functools.partial(grad_begun, len(lefts), len(rights[0])),
        [jax.ShapeDtypeStruct((rows, width), F32)], *ins,
        flops=2 * rows * width * depth, name="grad_begun",
        scratch=[pltpu.VMEM((rows, depth), BF), pltpu.VMEM((depth, width), BF)],
    )[0]


def grads_ended(cuts, *refs):
    place, copies = 0, []
    ends = sum(left + right + 1 for left, right in cuts)
    outs, rooms = refs[ends : ends + len(cuts)], refs[ends + len(cuts) :]
    for k, (left, right) in enumerate(cuts):
        lefts, rights = refs[place : place + left], refs[place + left : place + left + right]
        total = refs[place + left + right]
        place += left + right + 1
        room, sems = rooms[2 * k : 2 * k + 2]
        row = chunk = 0
        for block in lefts:
            for m in columns(block.shape[0]):
                size, col = m.stop - m.start, 0
                here = slice(row, row + size)
                for part in rights:
                    for n in columns(part.shape[1]):
                        there = slice(col + n.start, col + n.stop)
                        room[here, there] = (total[here, there] + matmul(block[m, :], part[:, n])).astype(BF)
                    col += part.shape[1]
                copies.append(
                    pltpu.make_async_copy(room.at[pl.ds(row, size)], outs[k].at[pl.ds(row, size)], sems.at[chunk])
                )
                copies[-1].start()
                row, chunk = row + size, chunk + 1
    for copy in copies:
        copy.wait()


def end_grads(jobs):
    ins = [block for lefts, rights, total in jobs for block in (*lefts, *rights, total)]
    shapes = [total.shape for _, _, total in jobs]
    scratch = []
    for shape in shapes:
        scratch += [pltpu.VMEM(shape, BF), pltpu.SemaphoreType.DMA((len(columns(shape[0])),))]
    size = sum(rows * width for rows, width in shapes)
    return pl.pallas_call(
        functools.partial(grads_ended, tuple((len(lefts), len(rights)) for lefts, rights, _ in jobs)),
        in_specs=vmem(len(ins)),
        out_specs=[pl.BlockSpec(memory_space=pl.ANY)] * len(jobs),
        out_shape=[jax.ShapeDtypeStruct(shape, BF) for shape in shapes],
        scratch_shapes=scratch,
        compiler_params=pltpu.CompilerParams(vmem_limit_bytes=12 << 20),
        cost_estimate=pl.CostEstimate(
            flops=2 * size * jobs[0][0][0].shape[1], bytes_accessed=2 * size, transcendentals=0
        ),
        name="grads_ended",
    )(*[pltpu.with_memory_space_constraint(x, pltpu.VMEM) for x in ins])


def other_cols(partial):
    size = lax.axis_size("col")
    if size == 2:
        return turn(partial, "col", 1)
    return (lax.psum(partial.astype(F32), "col") - partial.astype(F32)).astype(BF)


def silu_slope(value):
    sig = jax.nn.sigmoid(value)
    return sig * (1.0 + value * (1.0 - sig))


def matmul(a, b, dims=(((1,), (0,)), ((), ()))):
    return lax.dot_general(a, b, dims, preferred_element_type=F32)


def per_device(inputs, sample_ids, send_base, recv_base, w_up, w_down, cotangent):
    ticks = inputs.shape[1]
    rows = lax.axis_size("row")
    piece_rows, width = inputs.shape[2:]
    tokens, hidden = rows * piece_rows, w_up.shape[2]
    stack_like = jax.ShapeDtypeStruct((1, ticks, piece_rows, width), BF)
    parts = [slice(0, hidden // 2), slice(hidden // 2, hidden)]
    piece_like = jax.ShapeDtypeStruct((piece_rows, width), BF)
    part_like = jax.ShapeDtypeStruct((tokens, hidden // 2), BF)
    turned_like = jax.ShapeDtypeStruct((width, tokens), BF)
    turned_part = jax.ShapeDtypeStruct((hidden // 2, tokens), BF)

    def turn_blocks(tick, other):
        turned_ins.extend(run(turned, [turned_like], after(full_ins[tick], other)))
        for k in range(2):
            turned_acts[k].extend(run(turned, [turned_part], after(acts[tick][k], other)))

    act_in, last_cot = first_pieces(inputs, cotangent)
    cot_pieces = [last_cot] + [None] * (rows - 1)
    full_ins, acts, pres, seen_in, seen_out = [], [], [], [], []
    turned_ins, turned_acts = [], [[], []]
    for tick in range(ticks):
        waited = []
        if tick:
            act_in = run(arrive, [piece_like], bases[tick - 1], hand_over(sending, 1))[0]
            for j in beside(tick - 1):
                cot_pieces[j] = swap_rows(after(last_cot, sending), j)
                waited.append(cot_pieces[j])
        pieces = gather_rows(act_in)
        if tick == 0:
            up_kept, down_kept = hold(after([w_up[0], w_down[0]], act_in))
            pieces = after(pieces[::-1], up_kept)[::-1]
        if tick == ticks - 1:
            full_cot, first_grads = products(parts, cot_pieces, down_turned)
            pieces, waited = after(pieces[::-1], first_grads)[::-1], []
        full_in, partial = products(parts, pieces, up_kept, waited)
        pre = [(mine, other_cols(mine)) for mine in partial]
        if tick < ticks - 1:
            act, terms = through(silu_part, "down_part", parts, pre, down_kept, piece_like, rows)
            acts.append(act)
            terms_in = scatter_rows(terms)
            if tick == 0:
                (down_turned,) = run(
                    turned_weight, [jax.ShapeDtypeStruct((width, hidden), BF)], after(down_kept, terms)
                )
                stored, bases, cots = fetch(after(sample_ids, terms), inputs, send_base, recv_base, cotangent)
                terms_in[0] = after(terms_in[0], (down_turned, stored))
            if tick == 1:
                (up_turned,) = run(turned_weight, [jax.ShapeDtypeStruct((hidden, width), BF)], after(up_kept, terms))
                turn_blocks(0, terms)
                terms_in[0] = after(terms_in[0], (up_turned, turned_ins, turned_acts))
            act_out, sending = run(leave, [piece_like] * 2, act_in, *terms_in, stored[tick])
            seen_out.append(act_out)
        full_ins.append(full_in)
        pres.append(pre)
        seen_in.append(act_in)
    full_grads, pre_grads, seen_grad = [None] * ticks, [None] * ticks, [None] * ticks
    for step in range(ticks):
        tick = ticks - 1 - step
        if step == 0:
            grad_out, full_grad, partial = last_cot, full_cot, first_grads
        else:
            arrived = hand_over(sending, -1)
            if step == 1:
                acts.append(run(both_silu, [part_like] * 2, *after([*pres[-1][0], *pres[-1][1]], sending)))
                out_pieces = run(
                    functools.partial(down_again, parts), [piece_like] * rows, *acts[-1], down_kept,
                    flops=2 * tokens * width * hidden, name="down_again",
                )
                arrived = after(arrived, out_pieces)
                out_terms = list(out_pieces)
            (grad_out,) = run(arrive, [piece_like], cots[tick], arrived)
            waited = []
            for j in beside(step - 1):
                out_terms[j] = swap_rows(after(out_pieces[j], sending), j)
                waited.append(out_terms[j])
            pieces = gather_rows(grad_out)
            if step == ticks - 1:
                section_input, section_output = stacked(
                    functools.partial(finish_forward, ticks), 2, [*seen_in, *seen_out, *out_terms], stack_like,
                    "finish_forward",
                )
                begun_down = begin_grad([part[1:] for part in turned_acts], [[block] for block in after(full_grads[1:], grad_out)])
                pieces, waited = after(pieces[::-1], (section_output, begun_down))[::-1], []
            full_grad, partial = products(parts, pieces, down_turned, waited)
        full_grads[tick] = full_grad
        ins = [(mine, other_cols(mine), *known) for mine, known in zip(partial, pres[tick])]
        grad_pre, terms = through(slope_part, "in_part", parts, ins, up_turned, piece_like, rows)
        terms_in = scatter_rows(terms)
        if step < ticks - 1:
            turn_blocks(step + 1, terms)
            terms_in[0] = after(terms_in[0], (turned_ins, turned_acts))
            if step == ticks - 2:
                begun_up = begin_grad([turned_ins[1:]], [*pre_grads[1:tick], grad_pre, *pre_grads[tick + 1 :]])
                terms_in[0] = after(terms_in[0], begun_up)
            (sending,) = run(leave_back, [piece_like], grad_out, *terms_in)
            seen_grad[tick] = sending
        pre_grads[tick] = grad_pre
    grad_up, grad_down = end_grads(
        [
            ([turned_ins[0]], grad_pre, after(begun_up, terms)),
            ([part[0] for part in turned_acts], [full_grad], begun_down),
        ]
    )
    terms_in[0] = after(terms_in[0], (grad_up, grad_down))
    (input_grad,) = stacked(finish, 1, [grad_out, *terms_in, *seen_grad[1:]], stack_like, "finish")
    return (
        section_input,
        section_output,
        input_grad,
        grad_up[None],
        grad_down[None],
    )


def solution(mesh):
    placed = (
        P("section", None, "row", "col"),
        P(),
        P("section", None, "row", "col"),
        P("section", None, "row", "col"),
        P("section", "col", "row"),
        P("section", "row", "col"),
        P("section", None, "row", "col"),
    )
    return jax.shard_map(
        per_device,
        mesh=mesh,
        in_specs=placed,
        out_specs=(
            P("section", None, "row", "col"),
            P("section", None, "row", "col"),
            P("section", None, "row", "col"),
            P("section", "col", "row"),
            P("section", "row", "col"),
        ),
        check_vma=False,
    )
```

```python
import functools

import jax
import jax.numpy as jnp
from jax import lax
from jax.experimental import pallas as pl
from jax.experimental.pallas import tpu as pltpu
from jax.sharding import PartitionSpec as P

BF = jnp.bfloat16
F32 = jnp.float32
WEIGHT_CUTS = 8


def hand_over(block, distance):
    sections = range(lax.axis_size("section"))
    return lax.ppermute(block, "section", [(i - distance, i) for i in sections if i - distance in sections])


def turn(block, axis, distance):
    size = lax.axis_size(axis)
    return lax.ppermute(block, axis, [(i, (i + distance) % size) for i in range(size)])


def partner(row, j, size):
    away = (size - j) % size
    return row ^ away ^ (away >> 1) if size & (size - 1) == 0 else (j - row) % size


def swap_rows(block, j):
    size = lax.axis_size("row")
    return lax.ppermute(block, "row", [(i, partner(i, j, size)) for i in range(size)])


def gather_rows(block):
    return [swap_rows(block, j) if j else block for j in range(lax.axis_size("row"))]


def scatter_rows(pieces):
    return [swap_rows(piece, j) if j else piece for j, piece in enumerate(pieces)]


def beside(turn):
    size = lax.axis_size("row")
    return [[size - 1, size - 2], list(range(1, size - 2))][turn] if size > 2 else [[], [1]][turn]


def after(block, other):
    return lax.optimization_barrier((block, other))[0]


def vmem(count):
    return [pl.BlockSpec(memory_space=pltpu.VMEM)] * count


def run(kernel, outs, *ins, flops=0, scratch=(), name=None):
    ins = [pltpu.with_memory_space_constraint(block, pltpu.VMEM) for block in ins]
    size = sum(x.size * x.dtype.itemsize for x in [*ins, *outs])
    return pl.pallas_call(
        kernel,
        in_specs=vmem(len(ins)),
        out_specs=vmem(len(outs)),
        out_shape=[pltpu.VMEM(x.shape, x.dtype) for x in outs],
        scratch_shapes=scratch,
        compiler_params=pltpu.CompilerParams(vmem_limit_bytes=6 << 20),
        cost_estimate=pl.CostEstimate(flops=flops, bytes_accessed=size, transcendentals=0),
        name=name or kernel.__name__,
    )(*ins)


def first_kernel(inputs, cotangent, first, last, sems):
    copies = [
        pltpu.make_async_copy(inputs.at[0, 0], first, sems.at[0]),
        pltpu.make_async_copy(cotangent.at[0, cotangent.shape[1] - 1], last, sems.at[1]),
    ]
    for copy in copies:
        copy.start()
    for copy in copies:
        copy.wait()


def fetch_kernel(sample_ids, inputs, send_base, recv_base, cotangent, *refs):
    ticks = inputs.shape[1]
    count = ticks - 1
    stored, bases, cots = refs[:count], refs[count : 2 * count], refs[2 * count : 3 * count]
    fresh, sems = refs[3 * count :]
    section, sections = lax.axis_index("section"), lax.axis_size("section")
    samples = [sample_ids[tick - section + sections - 1] for tick in range(ticks)]
    copies = []
    for t in range(count):
        copies += [
            pltpu.make_async_copy(send_base.at[0, samples[t]], stored[t], sems.at[4 * t]),
            pltpu.make_async_copy(recv_base.at[0, samples[t + 1]], bases[t], sems.at[4 * t + 1]),
            pltpu.make_async_copy(inputs.at[0, t + 1], fresh.at[t], sems.at[4 * t + 2]),
            pltpu.make_async_copy(cotangent.at[0, t], cots[t], sems.at[4 * t + 3]),
        ]
    for copy in copies:
        copy.start()
    for copy in copies:
        copy.wait()
    for t in range(count):
        bases[t][...] = jnp.where(section == 0, fresh[t], bases[t][...])
        cots[t][...] = jnp.where(section == sections - 1, cots[t][...], jnp.zeros_like(cots[t]))


def fetch(sample_ids, inputs, send_base, recv_base, cotangent):
    count = inputs.shape[1] - 1
    piece = inputs.shape[2:]
    large = [pltpu.with_memory_space_constraint(x, pltpu.HBM) for x in (inputs, send_base, recv_base, cotangent)]
    outs = pl.pallas_call(
        fetch_kernel,
        in_specs=[pl.BlockSpec(memory_space=pltpu.SMEM)] + [pl.BlockSpec(memory_space=pltpu.HBM)] * len(large),
        out_specs=vmem(3 * count),
        out_shape=[pltpu.VMEM(piece, BF)] * (3 * count),
        scratch_shapes=[pltpu.VMEM((count, *piece), BF), pltpu.SemaphoreType.DMA((4 * count,))],
        compiler_params=pltpu.CompilerParams(vmem_limit_bytes=4 << 20),
        cost_estimate=pl.CostEstimate(flops=0, bytes_accessed=2 << 20, transcendentals=0),
        name="fetch",
    )(sample_ids, *large)
    return outs[:count], outs[count : 2 * count], outs[2 * count :]


def first_pieces(inputs, cotangent):
    piece = inputs.shape[2:]
    return pl.pallas_call(
        first_kernel,
        in_specs=[pl.BlockSpec(memory_space=pltpu.HBM)] * 2,
        out_specs=vmem(2),
        out_shape=[pltpu.VMEM(piece, BF)] * 2,
        scratch_shapes=[pltpu.SemaphoreType.DMA((2,))],
        compiler_params=pltpu.CompilerParams(vmem_limit_bytes=2 << 20),
        cost_estimate=pl.CostEstimate(flops=0, bytes_accessed=1 << 18, transcendentals=0),
        name="first",
    )(*[pltpu.with_memory_space_constraint(x, pltpu.HBM) for x in (inputs, cotangent)])


def added(first, terms):
    total = first[...].astype(F32)
    for term in terms:
        total = total + term[...].astype(F32)
    return total.astype(BF)


def arrive(base, arrived, out):
    out[...] = added(base, [arrived])


def leave(first, *refs):
    *terms, stored, out, delta = refs
    out[...] = added(first, terms)
    delta[...] = (out[...].astype(F32) - stored[...].astype(F32)).astype(BF)


def leave_back(first, *refs):
    *terms, out = refs
    out[...] = added(first, terms)


def finish_forward(count, *refs):
    *terms, ins, outs = refs
    entered, left, terms = terms[:count], terms[count : 2 * count - 1], terms[2 * count - 1 :]
    for t in range(count):
        ins[0, t] = entered[t][...]
    for t in range(count - 1):
        outs[0, t] = left[t][...]
    outs[0, count - 1] = added(entered[-1], terms)


def finish(first, *refs):
    *rest, grads = refs
    count = grads.shape[1] - 1
    grads[0, 0] = added(first, rest[:-count])
    for t in range(count):
        grads[0, t + 1] = rest[t - count][...]


def stacked(kernel, count, ins, like, name):
    return pl.pallas_call(
        kernel,
        in_specs=vmem(len(ins)),
        out_specs=vmem(count),
        out_shape=[like] * count,
        compiler_params=pltpu.CompilerParams(vmem_limit_bytes=6 << 20),
        cost_estimate=pl.CostEstimate(flops=0, bytes_accessed=1 << 20, transcendentals=0),
        name=name,
    )(*[pltpu.with_memory_space_constraint(x, pltpu.VMEM) for x in ins])


def turned(*refs):
    *pieces, out = refs
    out[...] = jnp.concatenate([piece[...] for piece in pieces], axis=0).T


def turned_weight(weight, out):
    for n in columns(out.shape[0]):
        out[n, :] = weight[:, n].T


def hold_kernel(*refs):
    *refs, sems = refs
    count = len(refs) // 2
    copies = []
    for k in range(count):
        step = refs[k].shape[0] // WEIGHT_CUTS
        for i in range(WEIGHT_CUTS):
            part = pl.ds(i * step, step)
            copies.append(pltpu.make_async_copy(refs[k].at[part], refs[count + k].at[part], sems.at[k, i]))
    for copy in copies:
        copy.start()
    for copy in copies:
        copy.wait()


def hold(weights):
    return pl.pallas_call(
        hold_kernel,
        in_specs=[pl.BlockSpec(memory_space=pltpu.HBM)] * len(weights),
        out_specs=vmem(len(weights)),
        out_shape=[pltpu.VMEM(weight.shape, BF) for weight in weights],
        scratch_shapes=[pltpu.SemaphoreType.DMA((len(weights), WEIGHT_CUTS))],
        compiler_params=pltpu.CompilerParams(vmem_limit_bytes=2 << 20),
        cost_estimate=pl.CostEstimate(flops=0, bytes_accessed=16 << 20, transcendentals=0),
        name="hold",
    )(*[pltpu.with_memory_space_constraint(weight, pltpu.HBM) for weight in weights])


def columns(width, step=256):
    step = min(width, step)
    return [slice(n, n + step) for n in range(0, width, step)]


def product_part(part, whole, weight, product):
    for n in columns(product.shape[1]):
        product[:, n] = matmul(whole[...], weight[:, n.start + part.start : n.stop + part.start]).astype(BF)


def stack_product(part, skip, *refs):
    *pieces, weight, whole, product = refs[skip:]
    whole[...] = jnp.concatenate([piece[...] for piece in reversed(pieces)], axis=0)
    product_part(part, whole, weight, product)


def products(parts, pieces, weight, waited=()):
    tokens, width = len(pieces) * pieces[0].shape[0], weight.shape[0]
    whole_like = jax.ShapeDtypeStruct((tokens, width), BF)
    likes = [jax.ShapeDtypeStruct((tokens, part.stop - part.start), BF) for part in parts]
    flops = 2 * tokens * width * likes[0].shape[1]
    whole, first = run(
        functools.partial(stack_product, parts[0], len(waited)), [whole_like, likes[0]],
        *waited, *reversed(pieces), weight, flops=flops, name="stack_product",
    )
    rest = [
        run(functools.partial(product_part, part), [like], whole, weight, flops=flops, name="product_part")[0]
        for part, like in zip(parts[1:], likes[1:])
    ]
    return whole, [first, *rest]


def put_rows(pieces, n, product):
    rows = pieces[0].shape[0]
    for j, piece in enumerate(pieces):
        piece[:, n] = product[j * rows : (j + 1) * rows].astype(BF)


def silu_part(mine, other, act):
    for n in columns(act.shape[1]):
        pre = mine[:, n].astype(F32) + other[:, n].astype(F32)
        act[:, n] = jax.nn.silu(pre).astype(BF)


def slope_part(mine, other, pre_mine, pre_other, grad_pre):
    for n in columns(grad_pre.shape[1]):
        pre = pre_mine[:, n].astype(F32) + pre_other[:, n].astype(F32)
        grad = mine[:, n].astype(F32) + other[:, n].astype(F32)
        grad_pre[:, n] = (grad * silu_slope(pre)).astype(BF)


def first_part(pointwise, part, *refs):
    *ins, weight, hidden, total = refs
    pointwise(*ins, hidden)
    for n in columns(weight.shape[1]):
        total[:, n] = matmul(hidden[...], weight[part, n])


def last_part(pointwise, part, count, *refs):
    *ins, weight, total, hidden = refs[:-count]
    pointwise(*ins, hidden)
    for n in columns(weight.shape[1]):
        put_rows(refs[-count:], n, total[:, n] + matmul(hidden[...], weight[part, n]))


def through(pointwise, name, parts, ins, weight, piece_like, rows):
    tokens, width = rows * piece_like.shape[0], piece_like.shape[1]
    (first, last), done = parts, []
    flops = 2 * tokens * width * (first.stop - first.start)
    like = [jax.ShapeDtypeStruct((tokens, part.stop - part.start), BF) for part in parts]
    hidden, total = run(
        functools.partial(first_part, pointwise, first),
        [like[0], jax.ShapeDtypeStruct((tokens, width), F32)],
        *ins[0], weight, flops=flops, name=name,
    )
    rest, *pieces = run(
        functools.partial(last_part, pointwise, last, rows),
        [like[1]] + [piece_like] * rows,
        *ins[1], weight, total, flops=flops, name=name,
    )
    return [hidden, rest], pieces


def both_silu(*refs):
    *ins, first, last = refs
    silu_part(*ins[:2], first)
    silu_part(*ins[2:], last)


def down_again(parts, first, last, weight, *pieces):
    for n in columns(weight.shape[1]):
        total = matmul(first[...], weight[parts[0], n]) + matmul(last[...], weight[parts[1], n])
        put_rows(pieces, n, total)


def grad_begun(row_parts, col_parts, *refs):
    *blocks, total, left, right = refs
    depth = blocks[0].shape[1]
    count = left.shape[1] // depth
    lefts, rights = blocks[: row_parts * count], blocks[row_parts * count :]
    for i, block in enumerate(lefts):
        size, part, t = block.shape[0], i // count, i % count
        left[part * size : (part + 1) * size, t * depth : (t + 1) * depth] = block[...]
    for i, block in enumerate(rights):
        size, t, part = block.shape[1], i // col_parts, i % col_parts
        right[t * depth : (t + 1) * depth, part * size : (part + 1) * size] = block[...]
    for m in columns(total.shape[0]):
        for n in columns(total.shape[1]):
            total[m, n] = matmul(left[m, :], right[:, n])


def begin_grad(lefts, rights):
    ins = [block for part in lefts for block in part] + [block for tick in rights for block in tick]
    rows = sum(part[0].shape[0] for part in lefts)
    width = sum(block.shape[1] for block in rights[0])
    depth = lefts[0][0].shape[1] * len(rights)
    return run(
        functools.partial(grad_begun, len(lefts), len(rights[0])),
        [jax.ShapeDtypeStruct((rows, width), F32)], *ins,
        flops=2 * rows * width * depth, name="grad_begun",
        scratch=[pltpu.VMEM((rows, depth), BF), pltpu.VMEM((depth, width), BF)],
    )[0]


def grads_ended(cuts, *refs):
    place, copies = 0, []
    ends = sum(left + right + 1 for left, right in cuts)
    outs, rooms = refs[ends : ends + len(cuts)], refs[ends + len(cuts) :]
    for k, (left, right) in enumerate(cuts):
        lefts, rights = refs[place : place + left], refs[place + left : place + left + right]
        total = refs[place + left + right]
        place += left + right + 1
        room, sems = rooms[2 * k : 2 * k + 2]
        row = chunk = 0
        for block in lefts:
            for m in columns(block.shape[0]):
                size, col = m.stop - m.start, 0
                here = slice(row, row + size)
                for part in rights:
                    for n in columns(part.shape[1]):
                        there = slice(col + n.start, col + n.stop)
                        room[here, there] = (total[here, there] + matmul(block[m, :], part[:, n])).astype(BF)
                    col += part.shape[1]
                copies.append(
                    pltpu.make_async_copy(room.at[pl.ds(row, size)], outs[k].at[pl.ds(row, size)], sems.at[chunk])
                )
                copies[-1].start()
                row, chunk = row + size, chunk + 1
    for copy in copies:
        copy.wait()


def end_grads(jobs):
    ins = [block for lefts, rights, total in jobs for block in (*lefts, *rights, total)]
    shapes = [total.shape for _, _, total in jobs]
    scratch = []
    for shape in shapes:
        scratch += [pltpu.VMEM(shape, BF), pltpu.SemaphoreType.DMA((len(columns(shape[0])),))]
    size = sum(rows * width for rows, width in shapes)
    return pl.pallas_call(
        functools.partial(grads_ended, tuple((len(lefts), len(rights)) for lefts, rights, _ in jobs)),
        in_specs=vmem(len(ins)),
        out_specs=[pl.BlockSpec(memory_space=pl.ANY)] * len(jobs),
        out_shape=[jax.ShapeDtypeStruct(shape, BF) for shape in shapes],
        scratch_shapes=scratch,
        compiler_params=pltpu.CompilerParams(vmem_limit_bytes=12 << 20),
        cost_estimate=pl.CostEstimate(
            flops=2 * size * jobs[0][0][0].shape[1], bytes_accessed=2 * size, transcendentals=0
        ),
        name="grads_ended",
    )(*[pltpu.with_memory_space_constraint(x, pltpu.VMEM) for x in ins])


def other_cols(partial):
    size = lax.axis_size("col")
    if size == 2:
        return turn(partial, "col", 1)
    return (lax.psum(partial.astype(F32), "col") - partial.astype(F32)).astype(BF)


def silu_slope(value):
    sig = jax.nn.sigmoid(value)
    return sig * (1.0 + value * (1.0 - sig))


def matmul(a, b, dims=(((1,), (0,)), ((), ()))):
    return lax.dot_general(a, b, dims, preferred_element_type=F32)


def per_device(inputs, sample_ids, send_base, recv_base, w_up, w_down, cotangent):
    ticks = inputs.shape[1]
    rows = lax.axis_size("row")
    piece_rows, width = inputs.shape[2:]
    tokens, hidden = rows * piece_rows, w_up.shape[2]
    stack_like = jax.ShapeDtypeStruct((1, ticks, piece_rows, width), BF)
    parts = [slice(0, hidden // 2), slice(hidden // 2, hidden)]
    piece_like = jax.ShapeDtypeStruct((piece_rows, width), BF)
    part_like = jax.ShapeDtypeStruct((tokens, hidden // 2), BF)
    turned_like = jax.ShapeDtypeStruct((width, tokens), BF)
    turned_part = jax.ShapeDtypeStruct((hidden // 2, tokens), BF)

    def turn_blocks(tick, other):
        turned_ins.extend(run(turned, [turned_like], after(full_ins[tick], other)))
        for k in range(2):
            turned_acts[k].extend(run(turned, [turned_part], after(acts[tick][k], other)))

    act_in, last_cot = first_pieces(inputs, cotangent)
    cot_pieces = [last_cot] + [None] * (rows - 1)
    full_ins, acts, pres, seen_in, seen_out = [], [], [], [], []
    turned_ins, turned_acts = [], [[], []]
    for tick in range(ticks):
        waited = []
        if tick:
            act_in = run(arrive, [piece_like], bases[tick - 1], hand_over(sending, 1))[0]
            for j in beside(tick - 1):
                cot_pieces[j] = swap_rows(after(last_cot, sending), j)
                waited.append(cot_pieces[j])
        pieces = gather_rows(act_in)
        if tick == 0:
            up_kept, down_kept = hold(after([w_up[0], w_down[0]], act_in))
            pieces = after(pieces[::-1], up_kept)[::-1]
        if tick == ticks - 1:
            full_cot, first_grads = products(parts, cot_pieces, down_turned)
            pieces, waited = after(pieces[::-1], first_grads)[::-1], []
        full_in, partial = products(parts, pieces, up_kept, waited)
        pre = [(mine, other_cols(mine)) for mine in partial]
        if tick < ticks - 1:
            act, terms = through(silu_part, "down_part", parts, pre, down_kept, piece_like, rows)
            acts.append(act)
            terms_in = scatter_rows(terms)
            if tick == 0:
                (down_turned,) = run(
                    turned_weight, [jax.ShapeDtypeStruct((width, hidden), BF)], after(down_kept, terms)
                )
                stored, bases, cots = fetch(after(sample_ids, terms), inputs, send_base, recv_base, cotangent)
                terms_in[0] = after(terms_in[0], (down_turned, stored))
            if tick == 1:
                (up_turned,) = run(turned_weight, [jax.ShapeDtypeStruct((hidden, width), BF)], after(up_kept, terms))
                turn_blocks(0, terms)
                terms_in[0] = after(terms_in[0], (up_turned, turned_ins, turned_acts))
            act_out, sending = run(leave, [piece_like] * 2, act_in, *terms_in, stored[tick])
            seen_out.append(act_out)
        full_ins.append(full_in)
        pres.append(pre)
        seen_in.append(act_in)
    full_grads, pre_grads, seen_grad = [None] * ticks, [None] * ticks, [None] * ticks
    for step in range(ticks):
        tick = ticks - 1 - step
        if step == 0:
            grad_out, full_grad, partial = last_cot, full_cot, first_grads
        else:
            arrived = hand_over(sending, -1)
            if step == 1:
                acts.append(run(both_silu, [part_like] * 2, *after([*pres[-1][0], *pres[-1][1]], sending)))
                out_pieces = run(
                    functools.partial(down_again, parts), [piece_like] * rows, *acts[-1], down_kept,
                    flops=2 * tokens * width * hidden, name="down_again",
                )
                arrived = after(arrived, out_pieces)
                out_terms = list(out_pieces)
            (grad_out,) = run(arrive, [piece_like], cots[tick], arrived)
            waited = []
            for j in beside(step - 1):
                out_terms[j] = swap_rows(after(out_pieces[j], sending), j)
                waited.append(out_terms[j])
            pieces = gather_rows(grad_out)
            if step == ticks - 1:
                section_input, section_output = stacked(
                    functools.partial(finish_forward, ticks), 2, [*seen_in, *seen_out, *out_terms], stack_like,
                    "finish_forward",
                )
                begun_down = begin_grad([part[1:] for part in turned_acts], [[block] for block in after(full_grads[1:], grad_out)])
                pieces, waited = after(pieces[::-1], (section_output, begun_down))[::-1], []
            full_grad, partial = products(parts, pieces, down_turned, waited)
        full_grads[tick] = full_grad
        ins = [(mine, other_cols(mine), *known) for mine, known in zip(partial, pres[tick])]
        grad_pre, terms = through(slope_part, "in_part", parts, ins, up_turned, piece_like, rows)
        terms_in = scatter_rows(terms)
        if step < ticks - 1:
            turn_blocks(step + 1, terms)
            terms_in[0] = after(terms_in[0], (turned_ins, turned_acts))
            if step == ticks - 2:
                begun_up = begin_grad([turned_ins[1:]], [*pre_grads[1:tick], grad_pre, *pre_grads[tick + 1 :]])
                terms_in[0] = after(terms_in[0], begun_up)
            (sending,) = run(leave_back, [piece_like], grad_out, *terms_in)
            seen_grad[tick] = sending
        pre_grads[tick] = grad_pre
    grad_up, grad_down = end_grads(
        [
            ([turned_ins[0]], grad_pre, after(begun_up, terms)),
            ([part[0] for part in turned_acts], [full_grad], begun_down),
        ]
    )
    terms_in[0] = after(terms_in[0], (grad_up, grad_down))
    (input_grad,) = stacked(finish, 1, [grad_out, *terms_in, *seen_grad[1:]], stack_like, "finish")
    return (
        section_input,
        section_output,
        input_grad,
        grad_up[None],
        grad_down[None],
    )


def solution(mesh):
    placed = (
        P("section", None, "row", "col"),
        P(),
        P("section", None, "row", "col"),
        P("section", None, "row", "col"),
        P("section", "col", "row"),
        P("section", "row", "col"),
        P("section", None, "row", "col"),
    )
    return jax.shard_map(
        per_device,
        mesh=mesh,
        in_specs=placed,
        out_specs=(
            P("section", None, "row", "col"),
            P("section", None, "row", "col"),
            P("section", None, "row", "col"),
            P("section", "col", "row"),
            P("section", "row", "col"),
        ),
        check_vma=False,
    )
```

```python
import functools

import jax
import jax.numpy as jnp
from jax import lax
from jax.experimental import pallas as pl
from jax.experimental.pallas import tpu as pltpu
from jax.sharding import PartitionSpec as P

BF = jnp.bfloat16
F32 = jnp.float32
WEIGHT_CUTS = 8


def hand_over(block, distance):
    sections = range(lax.axis_size("section"))
    return lax.ppermute(block, "section", [(i - distance, i) for i in sections if i - distance in sections])


def turn(block, axis, distance):
    size = lax.axis_size(axis)
    return lax.ppermute(block, axis, [(i, (i + distance) % size) for i in range(size)])


def partner(row, j, size):
    return row ^ ((size - j) % size) if size & (size - 1) == 0 else (j - row) % size


def swap_rows(block, j):
    size = lax.axis_size("row")
    return lax.ppermute(block, "row", [(i, partner(i, j, size)) for i in range(size)])


def gather_rows(block):
    return [swap_rows(block, j) if j else block for j in range(lax.axis_size("row"))]


def scatter_rows(pieces):
    return [swap_rows(piece, j) if j else piece for j, piece in enumerate(pieces)]


def beside(turn):
    size = lax.axis_size("row")
    return [list(range(2, size - 1)), [1], [size - 1]][turn] if size > 2 else [[], [1], []][turn]


def after(block, other):
    return lax.optimization_barrier((block, other))[0]


def vmem(count):
    return [pl.BlockSpec(memory_space=pltpu.VMEM)] * count


def run(kernel, outs, *ins, flops=0, scratch=(), name=None):
    ins = [pltpu.with_memory_space_constraint(block, pltpu.VMEM) for block in ins]
    size = sum(x.size * x.dtype.itemsize for x in [*ins, *outs])
    return pl.pallas_call(
        kernel,
        in_specs=vmem(len(ins)),
        out_specs=vmem(len(outs)),
        out_shape=[pltpu.VMEM(x.shape, x.dtype) for x in outs],
        scratch_shapes=scratch,
        compiler_params=pltpu.CompilerParams(vmem_limit_bytes=6 << 20),
        cost_estimate=pl.CostEstimate(flops=flops, bytes_accessed=size, transcendentals=0),
        name=name or kernel.__name__,
    )(*ins)


def first_kernel(inputs, cotangent, first, last, sems):
    copies = [
        pltpu.make_async_copy(inputs.at[0, 0], first, sems.at[0]),
        pltpu.make_async_copy(cotangent.at[0, cotangent.shape[1] - 1], last, sems.at[1]),
    ]
    for copy in copies:
        copy.start()
    for copy in copies:
        copy.wait()


def fetch_kernel(sample_ids, inputs, send_base, recv_base, cotangent, *refs):
    ticks = inputs.shape[1]
    count = ticks - 1
    stored, bases, cots = refs[:count], refs[count : 2 * count], refs[2 * count : 3 * count]
    fresh, sems = refs[3 * count :]
    section, sections = lax.axis_index("section"), lax.axis_size("section")
    samples = [sample_ids[tick - section + sections - 1] for tick in range(ticks)]
    copies = []
    for t in range(count):
        copies += [
            pltpu.make_async_copy(send_base.at[0, samples[t]], stored[t], sems.at[4 * t]),
            pltpu.make_async_copy(recv_base.at[0, samples[t + 1]], bases[t], sems.at[4 * t + 1]),
            pltpu.make_async_copy(inputs.at[0, t + 1], fresh.at[t], sems.at[4 * t + 2]),
            pltpu.make_async_copy(cotangent.at[0, t], cots[t], sems.at[4 * t + 3]),
        ]
    for copy in copies:
        copy.start()
    for copy in copies:
        copy.wait()
    for t in range(count):
        bases[t][...] = jnp.where(section == 0, fresh[t], bases[t][...])
        cots[t][...] = jnp.where(section == sections - 1, cots[t][...], jnp.zeros_like(cots[t]))


def fetch(sample_ids, inputs, send_base, recv_base, cotangent):
    count = inputs.shape[1] - 1
    piece = inputs.shape[2:]
    large = [pltpu.with_memory_space_constraint(x, pltpu.HBM) for x in (inputs, send_base, recv_base, cotangent)]
    outs = pl.pallas_call(
        fetch_kernel,
        in_specs=[pl.BlockSpec(memory_space=pltpu.SMEM)] + [pl.BlockSpec(memory_space=pltpu.HBM)] * len(large),
        out_specs=vmem(3 * count),
        out_shape=[pltpu.VMEM(piece, BF)] * (3 * count),
        scratch_shapes=[pltpu.VMEM((count, *piece), BF), pltpu.SemaphoreType.DMA((4 * count,))],
        compiler_params=pltpu.CompilerParams(vmem_limit_bytes=4 << 20),
        cost_estimate=pl.CostEstimate(flops=0, bytes_accessed=2 << 20, transcendentals=0),
        name="fetch",
    )(sample_ids, *large)
    return outs[:count], outs[count : 2 * count], outs[2 * count :]


def first_pieces(inputs, cotangent):
    piece = inputs.shape[2:]
    return pl.pallas_call(
        first_kernel,
        in_specs=[pl.BlockSpec(memory_space=pltpu.HBM)] * 2,
        out_specs=vmem(2),
        out_shape=[pltpu.VMEM(piece, BF)] * 2,
        scratch_shapes=[pltpu.SemaphoreType.DMA((2,))],
        compiler_params=pltpu.CompilerParams(vmem_limit_bytes=2 << 20),
        cost_estimate=pl.CostEstimate(flops=0, bytes_accessed=1 << 18, transcendentals=0),
        name="first",
    )(*[pltpu.with_memory_space_constraint(x, pltpu.HBM) for x in (inputs, cotangent)])


def added(first, terms):
    total = first[...].astype(F32)
    for term in terms:
        total = total + term[...].astype(F32)
    return total.astype(BF)


def arrive(base, arrived, out):
    out[...] = added(base, [arrived])


def leave(first, *refs):
    *terms, stored, out, delta = refs
    out[...] = added(first, terms)
    delta[...] = (out[...].astype(F32) - stored[...].astype(F32)).astype(BF)


def leave_back(first, *refs):
    *terms, out = refs
    out[...] = added(first, terms)


def finish_forward(count, *refs):
    *terms, ins, outs = refs
    entered, left, terms = terms[:count], terms[count : 2 * count - 1], terms[2 * count - 1 :]
    for t in range(count):
        ins[0, t] = entered[t][...]
    for t in range(count - 1):
        outs[0, t] = left[t][...]
    outs[0, count - 1] = added(entered[-1], terms)


def finish(first, *refs):
    *rest, grads = refs
    count = grads.shape[1] - 1
    grads[0, 0] = added(first, rest[:-count])
    for t in range(count):
        grads[0, t + 1] = rest[t - count][...]


def stacked(kernel, count, ins, like, name):
    return pl.pallas_call(
        kernel,
        in_specs=vmem(len(ins)),
        out_specs=vmem(count),
        out_shape=[like] * count,
        compiler_params=pltpu.CompilerParams(vmem_limit_bytes=6 << 20),
        cost_estimate=pl.CostEstimate(flops=0, bytes_accessed=1 << 20, transcendentals=0),
        name=name,
    )(*[pltpu.with_memory_space_constraint(x, pltpu.VMEM) for x in ins])


def turned(*refs):
    *pieces, out = refs
    out[...] = jnp.concatenate([piece[...] for piece in pieces], axis=0).T


def turned_weight(weight, out):
    for n in columns(out.shape[0]):
        out[n, :] = weight[:, n].T


def hold_kernel(*refs):
    *refs, sems = refs
    count = len(refs) // 2
    copies = []
    for k in range(count):
        step = refs[k].shape[0] // WEIGHT_CUTS
        for i in range(WEIGHT_CUTS):
            part = pl.ds(i * step, step)
            copies.append(pltpu.make_async_copy(refs[k].at[part], refs[count + k].at[part], sems.at[k, i]))
    for copy in copies:
        copy.start()
    for copy in copies:
        copy.wait()


def hold(weights):
    return pl.pallas_call(
        hold_kernel,
        in_specs=[pl.BlockSpec(memory_space=pltpu.HBM)] * len(weights),
        out_specs=vmem(len(weights)),
        out_shape=[pltpu.VMEM(weight.shape, BF) for weight in weights],
        scratch_shapes=[pltpu.SemaphoreType.DMA((len(weights), WEIGHT_CUTS))],
        compiler_params=pltpu.CompilerParams(vmem_limit_bytes=2 << 20),
        cost_estimate=pl.CostEstimate(flops=0, bytes_accessed=16 << 20, transcendentals=0),
        name="hold",
    )(*[pltpu.with_memory_space_constraint(weight, pltpu.HBM) for weight in weights])


def columns(width, step=256):
    step = min(width, step)
    return [slice(n, n + step) for n in range(0, width, step)]


def product_part(part, whole, weight, product):
    for n in columns(product.shape[1]):
        product[:, n] = matmul(whole[...], weight[:, n.start + part.start : n.stop + part.start]).astype(BF)


def stack_product(part, skip, *refs):
    *pieces, weight, whole, product = refs[skip:]
    whole[...] = jnp.concatenate([piece[...] for piece in reversed(pieces)], axis=0)
    product_part(part, whole, weight, product)


def products(parts, pieces, weight, waited=()):
    tokens, width = len(pieces) * pieces[0].shape[0], weight.shape[0]
    whole_like = jax.ShapeDtypeStruct((tokens, width), BF)
    likes = [jax.ShapeDtypeStruct((tokens, part.stop - part.start), BF) for part in parts]
    flops = 2 * tokens * width * likes[0].shape[1]
    whole, first = run(
        functools.partial(stack_product, parts[0], len(waited)), [whole_like, likes[0]],
        *waited, *reversed(pieces), weight, flops=flops, name="stack_product",
    )
    rest = [
        run(functools.partial(product_part, part), [like], whole, weight, flops=flops, name="product_part")[0]
        for part, like in zip(parts[1:], likes[1:])
    ]
    return whole, [first, *rest]


def put_rows(pieces, n, product):
    rows = pieces[0].shape[0]
    for j, piece in enumerate(pieces):
        piece[:, n] = product[j * rows : (j + 1) * rows].astype(BF)


def silu_part(mine, other, act):
    for n in columns(act.shape[1]):
        pre = mine[:, n].astype(F32) + other[:, n].astype(F32)
        act[:, n] = jax.nn.silu(pre).astype(BF)


def slope_part(mine, other, pre_mine, pre_other, grad_pre):
    for n in columns(grad_pre.shape[1]):
        pre = pre_mine[:, n].astype(F32) + pre_other[:, n].astype(F32)
        grad = mine[:, n].astype(F32) + other[:, n].astype(F32)
        grad_pre[:, n] = (grad * silu_slope(pre)).astype(BF)


def first_part(pointwise, part, *refs):
    *ins, weight, hidden, total = refs
    pointwise(*ins, hidden)
    for n in columns(weight.shape[1]):
        total[:, n] = matmul(hidden[...], weight[part, n])


def last_part(pointwise, part, count, *refs):
    *ins, weight, total, hidden = refs[:-count]
    pointwise(*ins, hidden)
    for n in columns(weight.shape[1]):
        put_rows(refs[-count:], n, total[:, n] + matmul(hidden[...], weight[part, n]))


def through(pointwise, name, parts, ins, weight, piece_like, rows):
    tokens, width = rows * piece_like.shape[0], piece_like.shape[1]
    (first, last), done = parts, []
    flops = 2 * tokens * width * (first.stop - first.start)
    like = [jax.ShapeDtypeStruct((tokens, part.stop - part.start), BF) for part in parts]
    hidden, total = run(
        functools.partial(first_part, pointwise, first),
        [like[0], jax.ShapeDtypeStruct((tokens, width), F32)],
        *ins[0], weight, flops=flops, name=name,
    )
    rest, *pieces = run(
        functools.partial(last_part, pointwise, last, rows),
        [like[1]] + [piece_like] * rows,
        *ins[1], weight, total, flops=flops, name=name,
    )
    return [hidden, rest], pieces


def both_silu(*refs):
    *ins, first, last = refs
    silu_part(*ins[:2], first)
    silu_part(*ins[2:], last)


def down_again(parts, first, last, weight, *pieces):
    for n in columns(weight.shape[1]):
        total = matmul(first[...], weight[parts[0], n]) + matmul(last[...], weight[parts[1], n])
        put_rows(pieces, n, total)


def grad_begun(row_parts, col_parts, *refs):
    *blocks, total, left, right = refs
    depth = blocks[0].shape[1]
    count = left.shape[1] // depth
    lefts, rights = blocks[: row_parts * count], blocks[row_parts * count :]
    for i, block in enumerate(lefts):
        size, part, t = block.shape[0], i // count, i % count
        left[part * size : (part + 1) * size, t * depth : (t + 1) * depth] = block[...]
    for i, block in enumerate(rights):
        size, t, part = block.shape[1], i // col_parts, i % col_parts
        right[t * depth : (t + 1) * depth, part * size : (part + 1) * size] = block[...]
    for m in columns(total.shape[0]):
        for n in columns(total.shape[1]):
            total[m, n] = matmul(left[m, :], right[:, n])


def begin_grad(lefts, rights):
    ins = [block for part in lefts for block in part] + [block for tick in rights for block in tick]
    rows = sum(part[0].shape[0] for part in lefts)
    width = sum(block.shape[1] for block in rights[0])
    depth = lefts[0][0].shape[1] * len(rights)
    return run(
        functools.partial(grad_begun, len(lefts), len(rights[0])),
        [jax.ShapeDtypeStruct((rows, width), F32)], *ins,
        flops=2 * rows * width * depth, name="grad_begun",
        scratch=[pltpu.VMEM((rows, depth), BF), pltpu.VMEM((depth, width), BF)],
    )[0]


def grads_ended(cuts, *refs):
    place, copies = 0, []
    ends = sum(left + right + 1 for left, right in cuts)
    outs, rooms = refs[ends : ends + len(cuts)], refs[ends + len(cuts) :]
    for k, (left, right) in enumerate(cuts):
        lefts, rights = refs[place : place + left], refs[place + left : place + left + right]
        total = refs[place + left + right]
        place += left + right + 1
        room, sems = rooms[2 * k : 2 * k + 2]
        row = chunk = 0
        for block in lefts:
            for m in columns(block.shape[0]):
                size, col = m.stop - m.start, 0
                here = slice(row, row + size)
                for part in rights:
                    for n in columns(part.shape[1]):
                        there = slice(col + n.start, col + n.stop)
                        room[here, there] = (total[here, there] + matmul(block[m, :], part[:, n])).astype(BF)
                    col += part.shape[1]
                copies.append(
                    pltpu.make_async_copy(room.at[pl.ds(row, size)], outs[k].at[pl.ds(row, size)], sems.at[chunk])
                )
                copies[-1].start()
                row, chunk = row + size, chunk + 1
    for copy in copies:
        copy.wait()


def end_grads(jobs):
    ins = [block for lefts, rights, total in jobs for block in (*lefts, *rights, total)]
    shapes = [total.shape for _, _, total in jobs]
    scratch = []
    for shape in shapes:
        scratch += [pltpu.VMEM(shape, BF), pltpu.SemaphoreType.DMA((len(columns(shape[0])),))]
    size = sum(rows * width for rows, width in shapes)
    return pl.pallas_call(
        functools.partial(grads_ended, tuple((len(lefts), len(rights)) for lefts, rights, _ in jobs)),
        in_specs=vmem(len(ins)),
        out_specs=[pl.BlockSpec(memory_space=pl.ANY)] * len(jobs),
        out_shape=[jax.ShapeDtypeStruct(shape, BF) for shape in shapes],
        scratch_shapes=scratch,
        compiler_params=pltpu.CompilerParams(vmem_limit_bytes=12 << 20),
        cost_estimate=pl.CostEstimate(
            flops=2 * size * jobs[0][0][0].shape[1], bytes_accessed=2 * size, transcendentals=0
        ),
        name="grads_ended",
    )(*[pltpu.with_memory_space_constraint(x, pltpu.VMEM) for x in ins])


def other_cols(partial):
    size = lax.axis_size("col")
    if size == 2:
        return turn(partial, "col", 1)
    return (lax.psum(partial.astype(F32), "col") - partial.astype(F32)).astype(BF)


def silu_slope(value):
    sig = jax.nn.sigmoid(value)
    return sig * (1.0 + value * (1.0 - sig))


def matmul(a, b, dims=(((1,), (0,)), ((), ()))):
    return lax.dot_general(a, b, dims, preferred_element_type=F32)


def per_device(inputs, sample_ids, send_base, recv_base, w_up, w_down, cotangent):
    ticks = inputs.shape[1]
    rows = lax.axis_size("row")
    piece_rows, width = inputs.shape[2:]
    tokens, hidden = rows * piece_rows, w_up.shape[2]
    stack_like = jax.ShapeDtypeStruct((1, ticks, piece_rows, width), BF)
    parts = [slice(0, hidden // 2), slice(hidden // 2, hidden)]
    piece_like = jax.ShapeDtypeStruct((piece_rows, width), BF)
    part_like = jax.ShapeDtypeStruct((tokens, hidden // 2), BF)
    turned_like = jax.ShapeDtypeStruct((width, tokens), BF)
    turned_part = jax.ShapeDtypeStruct((hidden // 2, tokens), BF)

    def turn_blocks(tick, other):
        turned_ins.extend(run(turned, [turned_like], after(full_ins[tick], other)))
        for k in range(2):
            turned_acts[k].extend(run(turned, [turned_part], after(acts[tick][k], other)))

    act_in, last_cot = first_pieces(inputs, cotangent)
    cot_pieces = [last_cot] + [None] * (rows - 1)
    full_ins, acts, pres, seen_in, seen_out = [], [], [], [], []
    turned_ins, turned_acts = [], [[], []]
    for tick in range(ticks):
        waited = []
        if tick:
            act_in = run(arrive, [piece_like], bases[tick - 1], hand_over(sending, 1))[0]
            for j in beside(tick - 1):
                cot_pieces[j] = swap_rows(after(last_cot, sending), j)
                waited.append(cot_pieces[j])
        pieces = gather_rows(act_in)
        if tick == 0:
            up_kept, down_kept = hold(after([w_up[0], w_down[0]], act_in))
            pieces = after(pieces[::-1], up_kept)[::-1]
        if tick == ticks - 1:
            full_cot, first_grads = products(parts, cot_pieces, down_turned)
            pieces, waited = after(pieces[::-1], first_grads)[::-1], []
        full_in, partial = products(parts, pieces, up_kept, waited)
        pre = [(mine, other_cols(mine)) for mine in partial]
        if tick < ticks - 1:
            act, terms = through(silu_part, "down_part", parts, pre, down_kept, piece_like, rows)
            acts.append(act)
            terms_in = scatter_rows(terms)
            if tick == 0:
                (down_turned,) = run(
                    turned_weight, [jax.ShapeDtypeStruct((width, hidden), BF)], after(down_kept, terms)
                )
                stored, bases, cots = fetch(after(sample_ids, terms), inputs, send_base, recv_base, cotangent)
                for j in beside(2):
                    cot_pieces[j] = swap_rows(after(last_cot, down_turned), j)
                terms_in[0] = after(terms_in[0], (down_turned, stored, [cot_pieces[j] for j in beside(2)]))
            if tick == 1:
                (up_turned,) = run(turned_weight, [jax.ShapeDtypeStruct((hidden, width), BF)], after(up_kept, terms))
                turn_blocks(0, terms)
                terms_in[0] = after(terms_in[0], (up_turned, turned_ins, turned_acts))
            act_out, sending = run(leave, [piece_like] * 2, act_in, *terms_in, stored[tick])
            seen_out.append(act_out)
        full_ins.append(full_in)
        pres.append(pre)
        seen_in.append(act_in)
    full_grads, pre_grads, seen_grad = [None] * ticks, [None] * ticks, [None] * ticks
    for step in range(ticks):
        tick = ticks - 1 - step
        if step == 0:
            grad_out, full_grad, partial = last_cot, full_cot, first_grads
        else:
            arrived = hand_over(sending, -1)
            if step == 1:
                acts.append(run(both_silu, [part_like] * 2, *after([*pres[-1][0], *pres[-1][1]], sending)))
                out_pieces = run(
                    functools.partial(down_again, parts), [piece_like] * rows, *acts[-1], down_kept,
                    flops=2 * tokens * width * hidden, name="down_again",
                )
                arrived = after(arrived, out_pieces)
                out_terms = list(out_pieces)
            (grad_out,) = run(arrive, [piece_like], cots[tick], arrived)
            waited = []
            for j in beside(step - 1):
                out_terms[j] = swap_rows(after(out_pieces[j], sending), j)
                waited.append(out_terms[j])
            pieces = gather_rows(grad_out)
            if step == ticks - 1:
                section_input, section_output = stacked(
                    functools.partial(finish_forward, ticks), 2, [*seen_in, *seen_out, *out_terms], stack_like,
                    "finish_forward",
                )
                begun_down = begin_grad([part[1:] for part in turned_acts], [[block] for block in after(full_grads[1:], grad_out)])
                pieces, waited = after(pieces[::-1], (section_output, begun_down))[::-1], []
            full_grad, partial = products(parts, pieces, down_turned, waited)
        full_grads[tick] = full_grad
        ins = [(mine, other_cols(mine), *known) for mine, known in zip(partial, pres[tick])]
        grad_pre, terms = through(slope_part, "in_part", parts, ins, up_turned, piece_like, rows)
        terms_in = scatter_rows(terms)
        if step < ticks - 1:
            turn_blocks(step + 1, terms)
            terms_in[0] = after(terms_in[0], (turned_ins, turned_acts))
            if step == ticks - 2:
                begun_up = begin_grad([turned_ins[1:]], [*pre_grads[1:tick], grad_pre, *pre_grads[tick + 1 :]])
                for j in beside(2):
                    out_terms[j] = swap_rows(after(out_pieces[j], begun_up), j)
                terms_in[0] = after(terms_in[0], (begun_up, [out_terms[j] for j in beside(2)]))
            (sending,) = run(leave_back, [piece_like], grad_out, *terms_in)
            seen_grad[tick] = sending
        pre_grads[tick] = grad_pre
    grad_up, grad_down = end_grads(
        [
            ([turned_ins[0]], grad_pre, after(begun_up, terms)),
            ([part[0] for part in turned_acts], [full_grad], begun_down),
        ]
    )
    terms_in[0] = after(terms_in[0], (grad_up, grad_down))
    (input_grad,) = stacked(finish, 1, [grad_out, *terms_in, *seen_grad[1:]], stack_like, "finish")
    return (
        section_input,
        section_output,
        input_grad,
        grad_up[None],
        grad_down[None],
    )


def solution(mesh):
    placed = (
        P("section", None, "row", "col"),
        P(),
        P("section", None, "row", "col"),
        P("section", None, "row", "col"),
        P("section", "col", "row"),
        P("section", "row", "col"),
        P("section", None, "row", "col"),
    )
    return jax.shard_map(
        per_device,
        mesh=mesh,
        in_specs=placed,
        out_specs=(
            P("section", None, "row", "col"),
            P("section", None, "row", "col"),
            P("section", None, "row", "col"),
            P("section", "col", "row"),
            P("section", "row", "col"),
        ),
        check_vma=False,
    )
```
